32 devices in a mesh: wide: 8 (over z, y), narrow: 4 (over x, core).
Axes of the slice: x: 2, y: 2, z: 4, core: 2. Of those that a mesh axis runs over, the one named last changes fastest.
Arguments:
- residual_input: bfloat16 [65536, 768], P(('wide', 'narrow')), may hold values from -12 to 12
- extents_per_device: int32 [32, 4], P(('wide', 'narrow')), may hold values from 1 to 1024, 2048 in all within a row
- attention_lookup_lerp: bfloat16 [768], P(('wide', 'narrow')), may hold values from 0 to 1
- attention_payload_lerp: bfloat16 [768], P(('wide', 'narrow')), may hold values from 0 to 1
- attention_receptance_lerp: bfloat16 [768], P(('wide', 'narrow')), may hold values from 0 to 1
- logarithmic_fading_speed: bfloat16 [768], P(('wide', 'narrow')), may hold values from -9 to -3
- present_reward: bfloat16 [768], P(('wide', 'narrow')), may hold values from -1 to 1
- attention_lookup_proj: bfloat16 [768, 768], P(('wide', 'narrow')), may hold values from -0.21875 to 0.21875
- attention_payload_proj: bfloat16 [768, 768], P(('wide', 'narrow')), may hold values from -0.21875 to 0.21875
- attention_receptance_proj: bfloat16 [768, 768], P(('wide', 'narrow')), may hold values from -0.21875 to 0.21875
- attention_result_proj: bfloat16 [768, 768], P(('wide', 'narrow')), may hold values from -0.875 to 0.875
- feedforward_lookup_lerp: bfloat16 [768], P(('wide', 'narrow')), may hold values from 0 to 1
- feedforward_receptance_lerp: bfloat16 [768], P(('wide', 'narrow')), may hold values from 0 to 1
- feedforward_lookup_proj: bfloat16 [768, 3072], P(('wide', 'narrow')), may hold values from -0.21875 to 0.21875
- feedforward_payload_proj: bfloat16 [3072, 768], P(('wide', 'narrow')), may hold values from -0.109375 to 0.109375
- feedforward_receptance_proj: bfloat16 [768, 768], P(('wide', 'narrow')), may hold values from -0.21875 to 0.21875
- first_normalizer_scaling: bfloat16 [768], P(('wide', 'narrow')), may hold values from 0.5 to 1.5
- first_normalizer_offset: bfloat16 [768], P(('wide', 'narrow')), may hold values from -1 to 1
- second_normalizer_scaling: bfloat16 [768], P(('wide', 'narrow')), may hold values from 0.5 to 1.5
- second_normalizer_offset: bfloat16 [768], P(('wide', 'narrow')), may hold values from -1 to 1
- upstream_adjoint: bfloat16 [65536, 768], P(('wide', 'narrow')), may hold values from -6 to 6
Outputs:
- output: bfloat16 [65536, 768], P(('wide', 'narrow'))
- stream_gradient: bfloat16 [65536, 768], P(('wide', 'narrow'))
- shift_key_gradient: float32 [768], P(('wide', 'narrow'))
- shift_value_gradient: float32 [768], P(('wide', 'narrow'))
- shift_gate_gradient: float32 [768], P(('wide', 'narrow'))
- decay_log_gradient: float32 [768], P(('wide', 'narrow'))
- first_bonus_gradient: float32 [768], P(('wide', 'narrow'))
- mixer_key_gradient: float32 [768, 768], P(('wide', 'narrow'))
- mixer_value_gradient: float32 [768, 768], P(('wide', 'narrow'))
- mixer_gate_gradient: float32 [768, 768], P(('wide', 'narrow'))
- mixer_output_gradient: float32 [768, 768], P(('wide', 'narrow'))
- hidden_shift_gradient: float32 [768], P(('wide', 'narrow'))
- gating_shift_gradient: float32 [768], P(('wide', 'narrow'))
- hidden_key_gradient: float32 [768, 3072], P(('wide', 'narrow'))
- hidden_value_gradient: float32 [3072, 768], P(('wide', 'narrow'))
- hidden_gate_gradient: float32 [768, 768], P(('wide', 'narrow'))
- first_gain_gradient: float32 [768], P(('wide', 'narrow'))
- first_bias_gradient: float32 [768], P(('wide', 'narrow'))
- second_gain_gradient: float32 [768], P(('wide', 'narrow'))
- second_bias_gradient: float32 [768], P(('wide', 'narrow'))
- rms_values: float32 [3], replicated
The draws below stay inside these ranges and needn't reach their ends.
Inputs may be any that keep to these rules, and one draw needn't show every extreme that they name: `extents_per_device`: row i lists, in order, the lengths of the sequences held by device i of wide+narrow; each row sums to 2048 and its largest entry is 1024.
All inputs are finite; a program needn't handle non-finite values.
Results may differ from the reference program's by a relative error of at most 0.011.
Values may be sent and summed in bfloat16 or wider, within the bound.
A program may use at most 320 MiB of HBM per device.

```python
import math
import jax
import jax.numpy as jnp
import numpy as np
from jax import lax

EMBED_SIZE = 768
FF = 3072
TOK_DEV = 2048
SEQS = 4
MAX_LEN = 1024
TOKENS = 65536
N_WIDE = 8
N_NARROW = 4


def draw_residual_input(key, part):
    key = jax.random.fold_in(key, 11)
    places = jnp.arange(TOKENS, dtype=jnp.float32) / max(TOKENS - 1, 1)
    entries = jnp.clip(jax.random.normal(key, (TOKENS, EMBED_SIZE), jnp.float32), -6.0, 6.0)
    scales = 0.5 + 1.5 * places
    return (entries * scales[:, None]).astype(jnp.bfloat16)


def levels(rng, extent, shards, least, top_value):
    factor_of = 1.0
    for dim, shards_of in shards:
        draws = jax.random.uniform(jax.random.fold_in(jax.random.fold_in(rng, 6), dim), (shards_of,), jnp.float32, least / len(shards), top_value / len(shards))
        factor_of = factor_of * jnp.repeat(jnp.exp(draws), extent[dim] // shards_of).reshape((-1,) + (1,) * (len(extent) - 1 - dim))
    return factor_of


def split_up(amount, total, most, slope):
    portions = [(1 << 20) // math.isqrt(standing ** slope) + 1 for standing in range(2, amount + 1)]
    spare, holding = total - most - (amount - 1), [1] * (amount - 1)
    while spare > 0:
        candidates = [i for i in range(amount - 1) if holding[i] < most]
        whole, remaining = sum([portions[i] for i in candidates]), spare
        for i in candidates:
            extra = min(most - holding[i], max(1, remaining * portions[i] // whole), spare)
            holding[i] = holding[i] + extra
            spare = spare - extra
    return np.array([most] + holding)


def uneven(stream_key, number_of, total, reach, slope):
    if number_of == 2:
        one = jax.random.randint(stream_key, (), max(1, total - reach), min(reach, total - 1) + 1)
        return jnp.stack([one, total - one])
    tallies = jnp.asarray(split_up(number_of, total, reach, slope), jnp.int32)
    twos = (number_of - 1) // 2
    donor, receiver = tallies[1:1 + 2 * twos:2], tallies[2:2 + 2 * twos:2]
    slack = jnp.minimum(donor - 1, reach - receiver)
    passed = jax.random.randint(jax.random.fold_in(stream_key, 1), (twos,), 0, 1 << 20) % (slack + 1)
    tallies = tallies.at[1:1 + 2 * twos:2].set(donor - passed).at[2:2 + 2 * twos:2].set(receiver + passed)
    return tallies[jax.random.permutation(jax.random.fold_in(stream_key, 2), number_of)]


def gaussian(own_key, shape, scale, bound, cuts=(), kind=jnp.bfloat16):
    loudness = levels(own_key, shape, cuts, -0.22, 0.18) if cuts else 1.0
    values = jax.random.normal(own_key, shape, jnp.float32) * scale * loudness
    return jnp.minimum(jnp.maximum(values, -bound), bound).astype(kind)


def setup_inputs(seed: int = 0) -> dict:
    streams_of = jax.random.split(jax.random.key(seed), 22)
    return {
        "residual_input": draw_residual_input(jax.random.fold_in(streams_of[21], 71), 0),
        "extents_per_device": jax.vmap(lambda own: uneven(own, SEQS, TOK_DEV, MAX_LEN, 1))(jax.random.split(streams_of[1], (N_WIDE * N_NARROW))).reshape((N_WIDE * N_NARROW, SEQS)).astype(jnp.int32),
        "attention_lookup_lerp": jnp.clip(1.0 * jax.random.uniform(streams_of[2], (EMBED_SIZE,), jnp.float32) ** levels(streams_of[2], (EMBED_SIZE,), ((0, 32),), -0.2, 0.2), 0.0, 1.0).astype(jnp.bfloat16),
        "attention_payload_lerp": jnp.clip(1.0 * jax.random.uniform(streams_of[3], (EMBED_SIZE,), jnp.float32) ** levels(streams_of[3], (EMBED_SIZE,), ((0, 32),), -0.2, 0.2), 0.0, 1.0).astype(jnp.bfloat16),
        "attention_receptance_lerp": jnp.clip(1.0 * jax.random.uniform(streams_of[4], (EMBED_SIZE,), jnp.float32) ** levels(streams_of[4], (EMBED_SIZE,), ((0, 32),), -0.2, 0.2), 0.0, 1.0).astype(jnp.bfloat16),
        "logarithmic_fading_speed": jnp.clip(-9.0 + 6.0 * jax.random.uniform(streams_of[5], (EMBED_SIZE,), jnp.float32) ** levels(streams_of[5], (EMBED_SIZE,), ((0, 32),), -0.2, 0.2), -9.0, -3.0).astype(jnp.bfloat16),
        "present_reward": jnp.clip(jax.random.uniform(streams_of[6], (EMBED_SIZE,), jnp.float32, -1.0, 1.0) * levels(streams_of[6], (EMBED_SIZE,), ((0, 32),), -0.4, 0.0), -1.0, 1.0).astype(jnp.bfloat16),
        "attention_lookup_proj": gaussian(streams_of[7], (EMBED_SIZE, EMBED_SIZE), EMBED_SIZE ** -0.5, 0.21875, ((0, 32),)),
        "attention_payload_proj": gaussian(streams_of[8], (EMBED_SIZE, EMBED_SIZE), EMBED_SIZE ** -0.5, 0.21875, ((0, 32),)),
        "attention_receptance_proj": gaussian(streams_of[9], (EMBED_SIZE, EMBED_SIZE), EMBED_SIZE ** -0.5, 0.21875, ((0, 32),)),
        "attention_result_proj": gaussian(streams_of[10], (EMBED_SIZE, EMBED_SIZE), (EMBED_SIZE // 16) ** -0.5, 0.875, ((0, 32),)),
        "feedforward_lookup_lerp": jnp.clip(1.0 * jax.random.uniform(streams_of[11], (EMBED_SIZE,), jnp.float32) ** levels(streams_of[11], (EMBED_SIZE,), ((0, 32),), -0.2, 0.2), 0.0, 1.0).astype(jnp.bfloat16),
        "feedforward_receptance_lerp": jnp.clip(1.0 * jax.random.uniform(streams_of[12], (EMBED_SIZE,), jnp.float32) ** levels(streams_of[12], (EMBED_SIZE,), ((0, 32),), -0.2, 0.2), 0.0, 1.0).astype(jnp.bfloat16),
        "feedforward_lookup_proj": gaussian(streams_of[13], (EMBED_SIZE, FF), EMBED_SIZE ** -0.5, 0.21875, ((0, 32),)),
        "feedforward_payload_proj": gaussian(streams_of[14], (FF, EMBED_SIZE), FF ** -0.5, 0.109375, ((0, 32),)),
        "feedforward_receptance_proj": gaussian(streams_of[15], (EMBED_SIZE, EMBED_SIZE), EMBED_SIZE ** -0.5, 0.21875, ((0, 32),)),
        "first_normalizer_scaling": jnp.clip(1.0 + 0.1 * jax.random.normal(streams_of[16], (EMBED_SIZE,), jnp.float32), 0.5, 1.5).astype(jnp.bfloat16),
        "first_normalizer_offset": gaussian(streams_of[17], (EMBED_SIZE,), 0.2, 1.0, ((0, 32),)),
        "second_normalizer_scaling": jnp.clip(1.0 + 0.1 * jax.random.normal(streams_of[18], (EMBED_SIZE,), jnp.float32), 0.5, 1.5).astype(jnp.bfloat16),
        "second_normalizer_offset": gaussian(streams_of[19], (EMBED_SIZE,), 0.2, 1.0, ((0, 32),)),
        "upstream_adjoint": gaussian(streams_of[20], (TOKENS, EMBED_SIZE), 1.0, 6.0, ((0, 32),)),
    }


HIGHEST = lax.Precision.HIGHEST

@jax.custom_vjp
def narrow_numeric_format(v):
    return lax.optimization_barrier(v.astype(jnp.bfloat16)).astype(jnp.float32)

@jax.custom_vjp
def low_back(v):
    return v

def low_keep(v):
    return (narrow_numeric_format(v), None)

def low_pass(kept, grad):
    return (grad,)

def back_keep(v):
    return (v, None)

def back_low(kept, grad):
    return (narrow_numeric_format(grad),)
narrow_numeric_format.defvjp(low_keep, low_pass)
low_back.defvjp(back_keep, back_low)

def product(left, right):
    return jnp.dot(left, right, precision=HIGHEST, preferred_element_type=jnp.float32)

def token_starts(row_lengths, total_rows):
    offsets = jnp.cumsum(row_lengths) - row_lengths
    places = jnp.arange(total_rows, dtype=jnp.int32)
    chosen = jnp.where(offsets[None, :] <= places[:, None], offsets[None, :], 0)
    return lax.optimization_barrier(jnp.max(chosen, axis=1)).astype(jnp.int32)

def norm_rows(inputs, gain_vec, bias_vec):
    centered = inputs - lax.optimization_barrier(jnp.mean(inputs, axis=1, keepdims=True))
    variance = lax.optimization_barrier(jnp.mean(centered * centered, axis=1, keepdims=True))
    return centered * lax.rsqrt(variance + 1e-05) * gain_vec + bias_vec

def earlier_rows(inputs, segment_beginnings):
    places = jnp.arange(inputs.shape[0], dtype=jnp.int32)
    moved = jnp.concatenate([jnp.zeros((1, inputs.shape[1]), inputs.dtype), inputs[:-1]], axis=0)
    return moved * (places != segment_beginnings).astype(inputs.dtype)[:, None]

def time_inputs(inputs, gain_vec, bias_vec, mix_key, mix_value, mix_gate, segment_beginnings):
    normed = norm_rows(inputs, gain_vec, bias_vec)
    before = earlier_rows(normed, segment_beginnings)
    return (normed * mix_key + before * (1.0 - mix_key), normed * mix_value + before * (1.0 - mix_value), normed * mix_gate + before * (1.0 - mix_gate))

def channel_inputs(inputs, gain_vec, bias_vec, mix_key, mix_gate, segment_beginnings):
    normed = norm_rows(inputs, gain_vec, bias_vec)
    before = earlier_rows(normed, segment_beginnings)
    return (normed * mix_key + before * (1.0 - mix_key), normed * mix_gate + before * (1.0 - mix_gate))

def faded_lookup_lines(lookup_lines, payload_lines, segment_beginnings, logarithmic_fading_speed, reward_array):
    total_rows = lookup_lines.shape[0]
    width = lookup_lines.shape[1]
    block_rows = min(128, total_rows)
    blocks = total_rows // block_rows
    rates = jnp.exp(logarithmic_fading_speed)
    local = jnp.arange(block_rows, dtype=jnp.int32)
    local_real = local.astype(jnp.float32)
    growth = jnp.exp((local_real + 1.0)[:, None] * rates)
    shrink = jnp.exp(-local_real[:, None] * rates)
    fading = jnp.exp(-(block_rows - 1.0 - local_real)[:, None] * rates)
    whole_fade = jnp.exp(-block_rows * rates)

    def advance(carried, pieces):
        top_state, bottom_state = carried
        lookup_segment_lines, value_block, start_block, first_row = pieces
        positions = first_row + local
        paired = ((local[None, :] < local[:, None]) & (positions[None, :] >= start_block[:, None])).astype(lookup_segment_lines.dtype)
        inherit = (start_block < first_row).astype(lookup_segment_lines.dtype)[:, None]
        key_weight = jnp.exp(lookup_segment_lines)
        key_value = key_weight * value_block
        owned_coefficient_slice = jnp.exp(reward_array + lookup_segment_lines)
        upper = shrink * product(paired, growth * key_value) + owned_coefficient_slice * value_block + inherit * shrink * top_state
        lower = shrink * product(paired, growth * key_weight) + owned_coefficient_slice + inherit * shrink * bottom_state
        tail_mask = (positions >= start_block[block_rows - 1]).astype(lookup_segment_lines.dtype)[:, None]
        carry_last = inherit[block_rows - 1]
        new_top = lax.optimization_barrier(jnp.sum(tail_mask * fading * key_value, axis=0)) + carry_last * whole_fade * top_state
        new_bottom = lax.optimization_barrier(jnp.sum(tail_mask * fading * key_weight, axis=0)) + carry_last * whole_fade * bottom_state
        return ((new_top, new_bottom), upper / lower)
    pieces = (lookup_lines.reshape(blocks, block_rows, width), payload_lines.reshape(blocks, block_rows, width), segment_beginnings.reshape(blocks, block_rows), jnp.arange(blocks, dtype=jnp.int32) * block_rows)
    empty_state = jnp.zeros_like(rates)
    unused, outcome = lax.scan(jax.checkpoint(advance), (empty_state, empty_state), pieces)
    return outcome.reshape(total_rows, width)

def layer(inputs, coefficient_bundle, segment_beginnings):
    attention_lookup_lerp, attention_payload_lerp, attention_receptance_lerp, logarithmic_fading_speed, present_reward, attention_lookup_proj, attention_payload_proj, attention_receptance_proj, attention_result_proj, feedforward_lookup_lerp, feedforward_receptance_lerp, feedforward_lookup_proj, feedforward_payload_proj, feedforward_receptance_proj, first_normalizer_scaling, first_normalizer_offset, second_normalizer_scaling, second_normalizer_offset = coefficient_bundle
    mixed_key, mixed_value, mixed_gate = time_inputs(inputs, first_normalizer_scaling, first_normalizer_offset, attention_lookup_lerp, attention_payload_lerp, attention_receptance_lerp, segment_beginnings)
    lookup_lines = low_back(product(narrow_numeric_format(mixed_key), attention_lookup_proj))
    payload_lines = low_back(product(narrow_numeric_format(mixed_value), attention_payload_proj))
    receptance_lines = low_back(product(narrow_numeric_format(mixed_gate), attention_receptance_proj))
    combined_lerp = narrow_numeric_format(jax.nn.sigmoid(receptance_lines) * faded_lookup_lines(lookup_lines, payload_lines, segment_beginnings, logarithmic_fading_speed, present_reward))
    attended = low_back(product(combined_lerp, attention_result_proj))
    middle = inputs + attended
    feed_key, feed_gate = channel_inputs(middle, second_normalizer_scaling, second_normalizer_offset, feedforward_lookup_lerp, feedforward_receptance_lerp, segment_beginnings)
    lifted = low_back(product(narrow_numeric_format(feed_key), feedforward_lookup_proj))
    squared = narrow_numeric_format(jnp.square(jax.nn.relu(lifted)))
    lowered = low_back(product(squared, feedforward_payload_proj))
    gate_in = low_back(product(narrow_numeric_format(feed_gate), feedforward_receptance_proj))
    feed_out = jax.nn.sigmoid(gate_in) * lowered
    result = middle + feed_out
    square_sums = jnp.stack([jnp.sum(result * result), jnp.sum(attended * attended), jnp.sum(feed_out * feed_out)])
    return (result, square_sums)

def reference(residual_input, extents_per_device, attention_lookup_lerp, attention_payload_lerp, attention_receptance_lerp, logarithmic_fading_speed, present_reward, attention_lookup_proj, attention_payload_proj, attention_receptance_proj, attention_result_proj, feedforward_lookup_lerp, feedforward_receptance_lerp, feedforward_lookup_proj, feedforward_payload_proj, feedforward_receptance_proj, first_normalizer_scaling, first_normalizer_offset, second_normalizer_scaling, second_normalizer_offset, upstream_adjoint):
    coefficient_bundle = tuple((coefficient_table.astype(jnp.float32) for coefficient_table in (attention_lookup_lerp, attention_payload_lerp, attention_receptance_lerp, logarithmic_fading_speed, present_reward, attention_lookup_proj, attention_payload_proj, attention_receptance_proj, attention_result_proj, feedforward_lookup_lerp, feedforward_receptance_lerp, feedforward_lookup_proj, feedforward_payload_proj, feedforward_receptance_proj, first_normalizer_scaling, first_normalizer_offset, second_normalizer_scaling, second_normalizer_offset)))
    groups = extents_per_device.shape[0]
    total_rows = residual_input.shape[0] // groups
    width = residual_input.shape[1]
    stream_blocks = residual_input.reshape(groups, total_rows, width)
    cot_blocks = upstream_adjoint.reshape(groups, total_rows, width)

    def step(carried, pieces):
        grads, sums = carried
        block, row_lengths, block_cot = pieces
        segment_beginnings = token_starts(row_lengths, total_rows)

        def forward(source, weights):
            return layer(source, weights, segment_beginnings)
        result, pullback, square_sums = jax.vjp(forward, block.astype(jnp.float32), coefficient_bundle, has_aux=True)
        grad_in, grad_weights = pullback(block_cot.astype(jnp.float32))
        grads = jax.tree.map(lambda first, second: first + second, grads, grad_weights)
        return ((grads, sums + square_sums), (result.astype(jnp.bfloat16), grad_in.astype(jnp.bfloat16)))
    empty_grads = tuple((jnp.zeros_like(coefficient_table) for coefficient_table in coefficient_bundle))
    (grads, sums), (outcome, grad_rows) = lax.scan(step, (empty_grads, jnp.zeros((3,), jnp.float32)), (stream_blocks, extents_per_device, cot_blocks))
    rms_values = jnp.sqrt(sums / (residual_input.shape[0] * width))
    return (outcome.reshape(residual_input.shape[0], width), grad_rows.reshape(residual_input.shape[0], width), grads[0], grads[1], grads[2], grads[3], grads[4], grads[5], grads[6], grads[7], grads[8], grads[9], grads[10], grads[11], grads[12], grads[13], grads[14], grads[15], grads[16], grads[17], rms_values)
```

```python
import functools

import jax
import jax.numpy as jnp
from jax import lax
from jax.experimental import pallas as pl
from jax.experimental.pallas import tpu as pltpu
from jax.sharding import PartitionSpec as P

F32 = jnp.float32
LOW = jnp.bfloat16
AXES = ("wide", "narrow")
BLOCK = 128
EDGE = 8
MIB = 2**20

(KEY_MIX, VALUE_MIX, GATE_MIX, FADING, REWARD, FEED_MIX, GATING_MIX, GAIN_ONE, BIAS_ONE, GAIN_TWO, BIAS_TWO) = range(11)
VECTORS = 16


def dot(left, right):
    return jnp.dot(left, right, preferred_element_type=F32)


def dot_nt(left, right):
    return lax.dot_general(left, right, (((1,), (1,)), ((), ())), preferred_element_type=F32)


def dot_tn(left, right):
    return lax.dot_general(left, right, (((0,), (0,)), ((), ())), preferred_element_type=F32)


def offsets_of(extents):
    offsets, total = [], 0
    for j in range(extents.shape[1] - 1):
        total = total + extents[0, j]
        offsets.append(total)
    return offsets


def start_of(places, offsets):
    begun = jnp.zeros_like(places)
    for offset in offsets:
        begun = jnp.where(places >= offset, offset, begun)
    return begun


def normed(x):
    centered = x - jnp.mean(x, axis=1, keepdims=True)
    scale = lax.rsqrt(jnp.mean(centered * centered, axis=1, keepdims=True) + 1e-05)
    return centered * scale, scale


def fold(x):
    return jnp.sum(x.reshape(x.shape[0] // 8, 8, x.shape[1]), axis=0)


def rows_of(shape, axis=0):
    return lax.broadcasted_iota(jnp.int32, shape, axis)


def shift_down(x, first, keep):
    return jnp.where(rows_of((x.shape[0], 1)) == 0, first, pltpu.roll(x, 1, 0)) * keep


def shift_up(x, last):
    rows = x.shape[0]
    return jnp.where(rows_of((rows, 1)) == rows - 1, last, pltpu.roll(x, rows - 1, 0))


def split(top, bottom):
    both = jnp.concatenate([top, bottom], axis=1)
    high = both.astype(LOW)
    low = (both - high.astype(F32)).astype(LOW)
    return jnp.concatenate([high, low], axis=0)


def norm_grad(back_normed, hat, scale, gain):
    back_hat = back_normed * gain
    return scale * (
        back_hat
        - jnp.mean(back_hat, axis=1, keepdims=True)
        - hat * jnp.mean(back_hat * hat, axis=1, keepdims=True)
    )


def vec(vectors, row):
    return vectors[row : row + 1, :]


def front_kernel(
    extents, vectors, x_ref, wk, wv, wr, wo,
    k_out, v_out, s_out, y_out, d_out, blend_out, mid_out, state_out, square_out,
    grow, shrink, last, state,
):
    tile = pl.program_id(0)
    rows, width = x_ref.shape
    half = BLOCK // 2
    offsets = offsets_of(extents)
    rate = jnp.exp(vec(vectors, FADING))

    @pl.when(tile == 0)
    def _():
        local = rows_of((BLOCK + EDGE, 1)).astype(F32)
        shrink[...] = jnp.exp((half - local) * rate)
        grow[...] = jnp.exp((local[:BLOCK] + (1 - half)) * rate)
        last[...] = jnp.zeros_like(last)
        state[...] = jnp.zeros_like(state)
        square_out[...] = jnp.zeros_like(square_out)

    x = x_ref[...].astype(F32)
    hat, _ = normed(x)
    norm = hat * vec(vectors, GAIN_ONE) + vec(vectors, BIAS_ONE)
    places = tile * rows + rows_of((rows, 1))
    keep = (places != start_of(places, offsets)).astype(F32)
    before = shift_down(norm, last[0:1, :], keep)
    last[0:1, :] = norm[rows - 1 : rows, :]

    def mixed(row):
        mix = vec(vectors, row)
        return (norm * mix + before * (1.0 - mix)).astype(LOW)

    keys = dot(mixed(KEY_MIX), wk[...])
    values = dot(mixed(VALUE_MIX), wv[...])
    sig = jax.nn.sigmoid(dot(mixed(GATE_MIX), wr[...]))
    k_out[...] = keys
    v_out[...] = values
    s_out[...] = sig
    fade_half = jnp.exp(-half * rate)
    reward = vec(vectors, REWARD)
    for block in range(rows // BLOCK):
        here = slice(block * BLOCK, (block + 1) * BLOCK)
        key, value = keys[here], values[here]
        weight = grow[...] * jnp.exp(key)
        first = tile * rows + block * BLOCK
        after = first + rows_of((BLOCK + EDGE, 1))
        column = rows_of((1, 2 * BLOCK), 1)
        source = first + jnp.where(column >= BLOCK, column - BLOCK, column)
        begun = start_of(after, offsets)
        paired = ((source < after) & (source >= begun)).astype(LOW)
        sums = dot(paired, split(weight * value, weight))
        inherit = (begun < first).astype(F32)
        top = shrink[...] * (sums[:, :width] + inherit * (fade_half * state[0:1, :]))
        bottom = shrink[...] * (sums[:, width:] + inherit * (fade_half * state[1:2, :]))
        state[0:1, :] = top[BLOCK : BLOCK + 1]
        state[1:2, :] = bottom[BLOCK : BLOCK + 1]
        state_out[block, :, :] = state[...]
        own = jnp.exp(reward + key)
        inverse = 1.0 / (bottom[:BLOCK] + own)
        wkv = (top[:BLOCK] + own * value) * inverse
        y_out[here, :] = wkv
        d_out[here, :] = inverse
        blend_out[here, :] = (sig[here] * wkv).astype(LOW)
    attended = dot(blend_out[...], wo[...])
    mid_out[...] = x + attended
    square_out[...] += fold(attended * attended)


def feed_kernel(
    extents, vectors, mid_ref, edge_ref, up_ref, w1, w2, wg,
    out_out, back_out, fk_out, fg_out, sq_out, bl_out, bg_out, lift_out, sums_out,
    lift, carry,
):
    step = pl.program_id(0)
    tile = pl.num_programs(0) - 1 - step
    rows, width = mid_ref.shape
    hidden = w1.shape[1]
    offsets = offsets_of(extents)

    @pl.when(step == 0)
    def _():
        carry[...] = jnp.zeros_like(carry)
        sums_out[...] = jnp.zeros_like(sums_out)

    gain, bias = vec(vectors, GAIN_TWO), vec(vectors, BIAS_TWO)
    mid = mid_ref[...]
    hat, scale = normed(mid)
    norm = hat * gain + bias
    edge_hat, _ = normed(edge_ref[...])
    edge = (edge_hat * gain + bias)[EDGE - 1 : EDGE]
    places = tile * rows + rows_of((rows, 1))
    keep = (places != start_of(places, offsets)).astype(F32)
    before = shift_down(norm, edge, keep)
    mix_k, mix_g = vec(vectors, FEED_MIX), vec(vectors, GATING_MIX)
    feed_key = (norm * mix_k + before * (1.0 - mix_k)).astype(LOW)
    feed_gate = (norm * mix_g + before * (1.0 - mix_g)).astype(LOW)
    fk_out[...] = feed_key
    fg_out[...] = feed_gate
    lowered = None
    for j in range(hidden // width):
        chunk = slice(j * width, (j + 1) * width)
        lifted = jnp.maximum(dot(feed_key, w1[:, chunk]), 0.0)
        lift[:, chunk] = lifted
        squared = (lifted * lifted).astype(LOW)
        sq_out[:, chunk] = squared
        part = dot(squared, w2[chunk, :])
        lowered = part if lowered is None else lowered + part
    sig = jax.nn.sigmoid(dot(feed_gate, wg[...]))
    feed_out = sig * lowered
    result = mid + feed_out
    out_out[...] = result.astype(LOW)
    upstream = up_ref[...].astype(F32)
    back_lowered = (upstream * sig).astype(LOW)
    back_gate = (upstream * lowered * sig * (1.0 - sig)).astype(LOW)
    bl_out[...] = back_lowered
    bg_out[...] = back_gate
    back_key = None
    for j in range(hidden // width):
        chunk = slice(j * width, (j + 1) * width)
        back_lifted = (2.0 * lift[:, chunk] * dot_nt(back_lowered, w2[chunk, :])).astype(LOW)
        lift_out[:, chunk] = back_lifted
        part = dot_nt(back_lifted, w1[:, chunk])
        back_key = part if back_key is None else back_key + part
    back_gating = dot_nt(back_gate, wg[...])
    late = norm - before
    back_before = keep * (back_key * (1.0 - mix_k) + back_gating * (1.0 - mix_g))
    back_norm = back_key * mix_k + back_gating * mix_g + shift_up(back_before, carry[0:1, :])
    carry[0:1, :] = back_before[0:1]
    back_out[...] = upstream + norm_grad(back_norm, hat, scale, gain)
    for row, piece in enumerate(
        (back_key * late, back_gating * late, back_norm * hat, back_norm, result * result, feed_out * feed_out)
    ):
        sums_out[8 * row : 8 * row + 8, :] += fold(piece)


def back_kernel(
    extents, vectors, x_ref, edge_ref, k_ref, v_ref, s_ref, y_ref, d_ref, state_ref, mid_ref, wk, wv, wr, wo,
    stream_out, ba_out, bk_out, bv_out, bg_out, mk_out, mv_out, mg_out, sums_out,
    grow, shrink, carry, state,
):
    step = pl.program_id(0)
    tile = pl.num_programs(0) - 1 - step
    rows, width = x_ref.shape
    half = BLOCK // 2
    offsets = offsets_of(extents)
    rate = jnp.exp(vec(vectors, FADING))

    @pl.when(step == 0)
    def _():
        local = rows_of((BLOCK + EDGE, 1)).astype(F32)
        shrink[...] = jnp.exp((half - local[:BLOCK]) * rate)
        grow[...] = jnp.exp((local + (1 - EDGE - half)) * rate)
        carry[...] = jnp.zeros_like(carry)
        state[...] = jnp.zeros_like(state)
        sums_out[...] = jnp.zeros_like(sums_out)

    back_mid = mid_ref[...]
    back_attended = back_mid.astype(LOW)
    ba_out[...] = back_attended
    back_blend = dot_nt(back_attended, wo[...])
    sig = s_ref[...]
    wkv = y_ref[...]
    bg_out[...] = (back_blend * wkv * sig * (1.0 - sig)).astype(LOW)
    back_top = back_blend * sig * d_ref[...]
    fade_half = jnp.exp(-half * rate)
    reward = vec(vectors, REWARD)
    for block in reversed(range(rows // BLOCK)):
        here = slice(block * BLOCK, (block + 1) * BLOCK)
        key, value = k_ref[here, :], v_ref[here, :]
        first = tile * rows + block * BLOCK
        source = first - EDGE + rows_of((BLOCK + EDGE, 1))
        column = rows_of((1, 2 * BLOCK), 1)
        after = first + jnp.where(column >= BLOCK, column - BLOCK, column)
        paired = ((source < after) & (source >= start_of(after, offsets))).astype(LOW)
        bt = back_top[here]
        weighted = shrink[...] * bt
        sums = dot(paired, split(weighted, -weighted * wkv[here]))
        following = start_of(first + BLOCK + jnp.zeros((1, 1), jnp.int32), offsets)
        tail = (source >= following).astype(F32)
        top = grow[...] * (sums[:, :width] + tail * (fade_half * state[0:1, :]))
        bottom = grow[...] * (sums[:, width:] + tail * (fade_half * state[1:2, :]))
        crossing = state_ref[block, :, :] * state[...]
        sums_out[32:40, :] += jnp.where(rows_of((8, 1)) < 2, crossing * (-1.0 * BLOCK), 0.0)
        state[0:1, :] = top[EDGE - 1 : EDGE]
        state[1:2, :] = bottom[EDGE - 1 : EDGE]
        weight = jnp.exp(key)
        own = jnp.exp(reward + key) * bt
        passed = weight * (value * top[EDGE:] + bottom[EDGE:])
        bonus = own * (value - wkv[here])
        back_key = passed + bonus
        bk_out[here, :] = back_key.astype(LOW)
        bv_out[here, :] = (weight * top[EDGE:] + own).astype(LOW)
        local = rows_of((BLOCK, 1)).astype(F32)
        sums_out[24:32, :] += fold(bonus)
        sums_out[32:40, :] += fold(local * back_key + passed)

    gain, bias = vec(vectors, GAIN_ONE), vec(vectors, BIAS_ONE)
    hat, scale = normed(x_ref[...].astype(F32))
    norm = hat * gain + bias
    edge_hat, _ = normed(edge_ref[...].astype(F32))
    edge = (edge_hat * gain + bias)[edge_ref.shape[0] - 1 : edge_ref.shape[0]]
    places = tile * rows + rows_of((rows, 1))
    keep = (places != start_of(places, offsets)).astype(F32)
    before = shift_down(norm, edge, keep)
    late = norm - before
    back_norm, back_before = None, None
    for number, (mix_row, back_ref, weights, mixed_ref) in enumerate(
        ((KEY_MIX, bk_out, wk, mk_out), (VALUE_MIX, bv_out, wv, mv_out), (GATE_MIX, bg_out, wr, mg_out))
    ):
        mix = vec(vectors, mix_row)
        mixed_ref[...] = (norm * mix + before * (1.0 - mix)).astype(LOW)
        back_mixed = dot_nt(back_ref[...], weights[...])
        sums_out[8 * number : 8 * number + 8, :] += fold(back_mixed * late)
        one, two = back_mixed * mix, back_mixed * (1.0 - mix)
        back_norm = one if back_norm is None else back_norm + one
        back_before = two if back_before is None else back_before + two
    back_before = back_before * keep
    back_norm = back_norm + shift_up(back_before, carry[0:1, :])
    carry[0:1, :] = back_before[0:1]
    sums_out[40:48, :] += fold(back_norm * hat)
    sums_out[48:56, :] += fold(back_norm)
    stream_out[...] = (back_mid + norm_grad(back_norm, hat, scale, gain)).astype(LOW)


def whole(shape):
    return pl.BlockSpec(shape, lambda i: (0,) * len(shape), pipeline_mode=pl.Buffered(1))


def kept(shape):
    return pl.BlockSpec(shape, lambda i: (0,) * len(shape))


def smem():
    return pl.BlockSpec(memory_space=pltpu.SMEM)


def front(extents, vectors, x, wk, wv, wr, wo, rows):
    tokens, width = x.shape
    tiles, blocks = tokens // rows, rows // BLOCK
    tile = pl.BlockSpec((rows, width), lambda i: (i, 0))
    wide = jax.ShapeDtypeStruct((tokens, width), F32)
    low = jax.ShapeDtypeStruct((tokens, width), LOW)
    return pl.pallas_call(
        front_kernel,
        name="front",
        grid=(tiles,),
        in_specs=[smem(), whole(vectors.shape), tile] + [whole((width, width))] * 4,
        out_specs=[tile] * 7 + [pl.BlockSpec((blocks, 8, width), lambda i: (i, 0, 0)), kept((8, width))],
        out_shape=[wide] * 5
        + [
            low,
            wide,
            jax.ShapeDtypeStruct((tokens // BLOCK, 8, width), F32),
            jax.ShapeDtypeStruct((8, width), F32),
        ],
        scratch_shapes=[
            pltpu.VMEM((BLOCK, width), F32),
            pltpu.VMEM((BLOCK + EDGE, width), F32),
            pltpu.VMEM((8, width), F32),
            pltpu.VMEM((8, width), F32),
        ],
        compiler_params=pltpu.CompilerParams(vmem_limit_bytes=56 * MIB),
    )(extents, vectors, x, wk, wv, wr, wo)


def feed(extents, vectors, mid, upstream, w1, w2, wg, rows):
    tokens, width = mid.shape
    hidden = w1.shape[1]
    tiles = tokens // rows
    tile = pl.BlockSpec((rows, width), lambda i: (tiles - 1 - i, 0))
    deep = pl.BlockSpec((rows, hidden), lambda i: (tiles - 1 - i, 0))
    edge = pl.BlockSpec((EDGE, width), lambda i: (jnp.maximum((tiles - 1 - i) * (rows // EDGE) - 1, 0), 0))
    wide = jax.ShapeDtypeStruct((tokens, width), F32)
    low = jax.ShapeDtypeStruct((tokens, width), LOW)
    low_deep = jax.ShapeDtypeStruct((tokens, hidden), LOW)
    return pl.pallas_call(
        feed_kernel,
        name="feed",
        grid=(tiles,),
        in_specs=[smem(), whole(vectors.shape), tile, edge, tile, whole(w1.shape), whole(w2.shape), whole(wg.shape)],
        out_specs=[tile, tile, tile, tile, deep, tile, tile, deep, kept((48, width))],
        out_shape=[low, wide, low, low, low_deep, low, low, low_deep, jax.ShapeDtypeStruct((48, width), F32)],
        scratch_shapes=[pltpu.VMEM((rows, hidden), F32), pltpu.VMEM((8, width), F32)],
        compiler_params=pltpu.CompilerParams(vmem_limit_bytes=60 * MIB),
    )(extents, vectors, mid, mid, upstream, w1, w2, wg)


def back(extents, vectors, x, saved, states, back_mid, wk, wv, wr, wo, rows):
    tokens, width = x.shape
    tiles, blocks = tokens // rows, rows // BLOCK
    tile = pl.BlockSpec((rows, width), lambda i: (tiles - 1 - i, 0))
    edge = pl.BlockSpec((16, width), lambda i: (jnp.maximum((tiles - 1 - i) * (rows // 16) - 1, 0), 0))
    low = jax.ShapeDtypeStruct((tokens, width), LOW)
    return pl.pallas_call(
        back_kernel,
        name="back",
        grid=(tiles,),
        in_specs=[smem(), whole(vectors.shape), tile, edge]
        + [tile] * 5
        + [pl.BlockSpec((blocks, 8, width), lambda i: (tiles - 1 - i, 0, 0)), tile]
        + [whole((width, width))] * 4,
        out_specs=[tile] * 8 + [kept((56, width))],
        out_shape=[low] * 8 + [jax.ShapeDtypeStruct((56, width), F32)],
        scratch_shapes=[
            pltpu.VMEM((BLOCK + EDGE, width), F32),
            pltpu.VMEM((BLOCK, width), F32),
            pltpu.VMEM((8, width), F32),
            pltpu.VMEM((8, width), F32),
        ],
        compiler_params=pltpu.CompilerParams(vmem_limit_bytes=56 * MIB),
    )(extents, vectors, x, x, *saved, states, back_mid, wk, wv, wr, wo)


def layer(extents, vectors, x, upstream, wk, wv, wr, wo, w1, w2, wg):
    tokens, width = x.shape
    rows = min(256, tokens)
    *saved, blend, mid, states, attended_square = front(extents, vectors, x, wk, wv, wr, wo, rows)
    outcome, back_mid, fk, fg, sq, bl, bgate, lift, sums_two = feed(extents, vectors, mid, upstream, w1, w2, wg, rows)
    stream, ba, bk, bv, bg, mk, mv, mg, sums_one = back(
        extents, vectors, x, saved, states, back_mid, wk, wv, wr, wo, rows
    )
    grads = [dot_tn(mk, bk), dot_tn(mv, bv), dot_tn(mg, bg), dot_tn(blend, ba)]
    grads += [dot_tn(fk, lift), dot_tn(sq, bl), dot_tn(fg, bgate)]
    one = jnp.sum(sums_one.reshape(7, 8, width), axis=1)
    two = jnp.sum(sums_two.reshape(6, 8, width), axis=1)
    decay = one[4] * jnp.exp(vectors[FADING])
    small = jnp.stack(
        [one[0], one[1], one[2], decay, one[3], two[0], two[1], one[5], one[6], two[2], two[3]]
    )
    squares = jnp.stack([jnp.sum(two[4]), jnp.sum(attended_square), jnp.sum(two[5])])
    return outcome, stream, grads, small, squares


def body(residual_input, extents, *rest):
    parameters, upstream = rest[:18], rest[18]
    small_names = (0, 1, 2, 3, 4, 9, 10, 14, 15, 16, 17)
    large_names = (5, 6, 7, 8, 11, 12, 13)
    held = jnp.stack([parameters[i] for i in small_names])
    width = held.shape[1] * lax.axis_size(AXES)
    vectors = lax.all_gather(held, AXES, axis=1, tiled=True).astype(F32)
    vectors = jnp.pad(vectors, ((0, VECTORS - len(small_names)), (0, 0)))
    weights = [lax.all_gather(parameters[i], AXES, axis=0, tiled=True) for i in large_names]
    outcome, stream, grads, small, squares = layer(extents, vectors, residual_input, upstream, *weights)
    totals = lax.psum(squares, AXES)
    entries = residual_input.shape[0] * width * lax.axis_size(AXES)
    rms_values = jnp.sqrt(totals / entries)
    small = lax.psum_scatter(small, AXES, scatter_dimension=1, tiled=True)
    shards = [None] * 18
    for row, i in enumerate(small_names):
        shards[i] = small[row]
    for grad, i in zip(grads, large_names):
        shards[i] = lax.psum_scatter(grad, AXES, scatter_dimension=0, tiled=True)
    return (outcome, stream, *shards, rms_values)


def solution(mesh):
    rows, vector = P(AXES, None), P(AXES)
    kinds = [vector] * 5 + [rows] * 4 + [vector] * 2 + [rows] * 3 + [vector] * 4
    return jax.shard_map(
        body,
        mesh=mesh,
        in_specs=(rows, rows, *kinds, rows),
        out_specs=(rows, rows, *kinds, P()),
        check_vma=False,
    )
```

```python
import functools

import jax
import jax.numpy as jnp
from jax import lax
from jax.experimental import pallas as pl
from jax.experimental.pallas import tpu as pltpu
from jax.sharding import PartitionSpec as P

F32 = jnp.float32
LOW = jnp.bfloat16
AXES = ("wide", "narrow")
BLOCK = 128
EDGE = 8
MIB = 2**20

(KEY_MIX, VALUE_MIX, GATE_MIX, FADING, REWARD, FEED_MIX, GATING_MIX, GAIN_ONE, BIAS_ONE, GAIN_TWO, BIAS_TWO) = range(11)
VECTORS = 16


def dot(left, right):
    return jnp.dot(left, right, preferred_element_type=F32)


def dot_nt(left, right):
    return lax.dot_general(left, right, (((1,), (1,)), ((), ())), preferred_element_type=F32)


def dot_tn(left, right):
    return lax.dot_general(left, right, (((0,), (0,)), ((), ())), preferred_element_type=F32)


def offsets_of(extents):
    offsets, total = [], 0
    for j in range(extents.shape[1] - 1):
        total = total + extents[0, j]
        offsets.append(total)
    return offsets


def start_of(places, offsets):
    begun = jnp.zeros_like(places)
    for offset in offsets:
        begun = jnp.where(places >= offset, offset, begun)
    return begun


def normed(x):
    centered = x - jnp.mean(x, axis=1, keepdims=True)
    scale = lax.rsqrt(jnp.mean(centered * centered, axis=1, keepdims=True) + 1e-05)
    return centered * scale, scale


def fold(x):
    return jnp.sum(x.reshape(x.shape[0] // 8, 8, x.shape[1]), axis=0)


def rows_of(shape, axis=0):
    return lax.broadcasted_iota(jnp.int32, shape, axis)


def shift_down(x, first, keep):
    return jnp.where(rows_of((x.shape[0], 1)) == 0, first, pltpu.roll(x, 1, 0)) * keep


def shift_up(x, last):
    rows = x.shape[0]
    return jnp.where(rows_of((rows, 1)) == rows - 1, last, pltpu.roll(x, rows - 1, 0))


def split(top, bottom):
    both = jnp.concatenate([top, bottom], axis=1)
    high = both.astype(LOW)
    low = (both - high.astype(F32)).astype(LOW)
    return jnp.concatenate([high, low], axis=0)


def norm_grad(back_normed, hat, scale, gain):
    back_hat = back_normed * gain
    return scale * (
        back_hat
        - jnp.mean(back_hat, axis=1, keepdims=True)
        - hat * jnp.mean(back_hat * hat, axis=1, keepdims=True)
    )


def vec(vectors, row):
    return vectors[row : row + 1, :]


def matrix(ref):
    return ref[...].reshape(-1, ref.shape[-1])


def front_tile(
    tile, extents, vectors, x_ref, wk, wv, wr, wo,
    k_out, v_out, s_out, y_out, d_out, blend_out, mid_out, state_out, square_out,
    grow, shrink, last, state,
):
    rows, width = x_ref.shape
    half = BLOCK // 2
    offsets = offsets_of(extents)
    rate = jnp.exp(vec(vectors, FADING))

    @pl.when(tile == 0)
    def _():
        local = rows_of((BLOCK + EDGE, 1)).astype(F32)
        shrink[...] = jnp.exp((half - local) * rate)
        grow[...] = jnp.exp((local[:BLOCK] + (1 - half)) * rate)
        last[...] = jnp.zeros_like(last)
        state[...] = jnp.zeros_like(state)
        square_out[...] = jnp.zeros_like(square_out)

    x = x_ref[...].astype(F32)
    hat, _ = normed(x)
    norm = hat * vec(vectors, GAIN_ONE) + vec(vectors, BIAS_ONE)
    places = tile * rows + rows_of((rows, 1))
    keep = (places != start_of(places, offsets)).astype(F32)
    before = shift_down(norm, last[0:1, :], keep)
    last[0:1, :] = norm[rows - 1 : rows, :]

    def mixed(row):
        mix = vec(vectors, row)
        return (norm * mix + before * (1.0 - mix)).astype(LOW)

    keys = dot(mixed(KEY_MIX), matrix(wk))
    values = dot(mixed(VALUE_MIX), matrix(wv))
    sig = jax.nn.sigmoid(dot(mixed(GATE_MIX), matrix(wr)))
    k_out[...] = keys
    v_out[...] = values
    s_out[...] = sig
    fade_half = jnp.exp(-half * rate)
    reward = vec(vectors, REWARD)
    for block in range(rows // BLOCK):
        here = slice(block * BLOCK, (block + 1) * BLOCK)
        key, value = keys[here], values[here]
        weight = grow[...] * jnp.exp(key)
        first = tile * rows + block * BLOCK
        after = first + rows_of((BLOCK + EDGE, 1))
        column = rows_of((1, 2 * BLOCK), 1)
        source = first + jnp.where(column >= BLOCK, column - BLOCK, column)
        begun = start_of(after, offsets)
        paired = ((source < after) & (source >= begun)).astype(LOW)
        sums = dot(paired, split(weight * value, weight))
        inherit = (begun < first).astype(F32)
        top = shrink[...] * (sums[:, :width] + inherit * (fade_half * state[0:1, :]))
        bottom = shrink[...] * (sums[:, width:] + inherit * (fade_half * state[1:2, :]))
        state[0:1, :] = top[BLOCK : BLOCK + 1]
        state[1:2, :] = bottom[BLOCK : BLOCK + 1]
        state_out[block, :, :] = state[...]
        own = jnp.exp(reward + key)
        inverse = 1.0 / (bottom[:BLOCK] + own)
        wkv = (top[:BLOCK] + own * value) * inverse
        y_out[here, :] = wkv
        d_out[here, :] = inverse
        blend_out[here, :] = (sig[here] * wkv).astype(LOW)
    attended = dot(blend_out[...], matrix(wo))
    mid_out[...] = x + attended
    square_out[...] += fold(attended * attended)


def front_kernel(extents, vectors, x_ref, weights, *rest):
    front_tile(pl.program_id(0), extents, vectors, x_ref, *[weights.at[u] for u in range(4)], *rest)


def feed_kernel(
    extents, vectors, mid_ref, edge_ref, up_ref, blend_ref, packed,
    out_out, back_out, acts, sums_out,
    lift, carry, wg, w1, w2, load,
):
    step = pl.program_id(0)
    tile = pl.num_programs(0) - 1 - step
    rows, width = mid_ref.shape
    hidden = lift.shape[1]
    offsets = offsets_of(extents)

    @pl.when(step == 0)
    def _():
        copies = [(packed.at[4], wg), (packed.at[5:9], w1)]
        copies += [(packed.at[9 + j], w2.at[:, :, :, :, j]) for j in range(4)]
        copies = [pltpu.make_async_copy(a, b, load.at[i]) for i, (a, b) in enumerate(copies)]
        for copy in copies:
            copy.start()
        for copy in copies:
            copy.wait()
        carry[...] = jnp.zeros_like(carry)
        sums_out[...] = jnp.zeros_like(sums_out)

    gain, bias = vec(vectors, GAIN_TWO), vec(vectors, BIAS_TWO)
    mid = mid_ref[...]
    hat, scale = normed(mid)
    norm = hat * gain + bias
    edge_hat, _ = normed(edge_ref[...])
    edge = (edge_hat * gain + bias)[EDGE - 1 : EDGE]
    places = tile * rows + rows_of((rows, 1))
    keep = (places != start_of(places, offsets)).astype(F32)
    before = shift_down(norm, edge, keep)
    mix_k, mix_g = vec(vectors, FEED_MIX), vec(vectors, GATING_MIX)
    feed_key = (norm * mix_k + before * (1.0 - mix_k)).astype(LOW)
    feed_gate = (norm * mix_g + before * (1.0 - mix_g)).astype(LOW)
    acts[0] = feed_key
    acts[5] = feed_gate
    acts[6] = blend_ref[...]
    lowered = None
    for j in range(hidden // width):
        chunk = slice(j * width, (j + 1) * width)
        lifted = jnp.maximum(dot(feed_key, matrix(w1.at[j])), 0.0)
        lift[:, chunk] = lifted
        squared = (lifted * lifted).astype(LOW)
        acts[1 + j] = squared
        part = dot(squared, matrix(w2.at[j]))
        lowered = part if lowered is None else lowered + part
    sig = jax.nn.sigmoid(dot(feed_gate, matrix(wg)))
    feed_out = sig * lowered
    result = mid + feed_out
    out_out[...] = result.astype(LOW)
    upstream = up_ref[...].astype(F32)
    back_lowered = (upstream * sig).astype(LOW)
    back_gate = (upstream * lowered * sig * (1.0 - sig)).astype(LOW)
    acts[11] = back_lowered
    acts[12] = back_gate
    back_key = None
    for j in range(hidden // width):
        chunk = slice(j * width, (j + 1) * width)
        back_lifted = (2.0 * lift[:, chunk] * dot_nt(back_lowered, matrix(w2.at[j]))).astype(LOW)
        acts[7 + j] = back_lifted
        part = dot_nt(back_lifted, matrix(w1.at[j]))
        back_key = part if back_key is None else back_key + part
    back_gating = dot_nt(back_gate, matrix(wg))
    late = norm - before
    back_before = keep * (back_key * (1.0 - mix_k) + back_gating * (1.0 - mix_g))
    back_norm = back_key * mix_k + back_gating * mix_g + shift_up(back_before, carry[0:1, :])
    carry[0:1, :] = back_before[0:1]
    back_mid = upstream + norm_grad(back_norm, hat, scale, gain)
    back_out[...] = back_mid
    acts[13] = back_mid.astype(LOW)
    for row, piece in enumerate(
        (back_key * late, back_gating * late, back_norm * hat, back_norm, result * result, feed_out * feed_out)
    ):
        sums_out[8 * row : 8 * row + 8, :] += fold(piece)


def back_tile(
    tile, begins, extents, vectors, x_ref, edge_ref, k_ref, v_ref, s_ref, y_ref, d_ref, state_ref, mid_ref, weights,
    stream_out, acts, sums_out,
    grow, shrink, carry, state,
):
    rows, width = x_ref.shape
    half = BLOCK // 2
    offsets = offsets_of(extents)
    rate = jnp.exp(vec(vectors, FADING))

    @pl.when(begins)
    def _():
        local = rows_of((BLOCK + EDGE, 1)).astype(F32)
        shrink[...] = jnp.exp((half - local[:BLOCK]) * rate)
        grow[...] = jnp.exp((local + (1 - EDGE - half)) * rate)
        carry[...] = jnp.zeros_like(carry)
        state[...] = jnp.zeros_like(state)
        sums_out[...] = jnp.zeros_like(sums_out)

    back_mid = mid_ref[...]
    back_attended = back_mid.astype(LOW)
    back_blend = dot_nt(back_attended, matrix(weights.at[3]))
    sig = s_ref[...]
    wkv = y_ref[...]
    acts[5] = (back_blend * wkv * sig * (1.0 - sig)).astype(LOW)
    back_top = back_blend * sig * d_ref[...]
    fade_half = jnp.exp(-half * rate)
    reward = vec(vectors, REWARD)
    for block in reversed(range(rows // BLOCK)):
        here = slice(block * BLOCK, (block + 1) * BLOCK)
        key, value = k_ref[here, :], v_ref[here, :]
        first = tile * rows + block * BLOCK
        source = first - EDGE + rows_of((BLOCK + EDGE, 1))
        column = rows_of((1, 2 * BLOCK), 1)
        after = first + jnp.where(column >= BLOCK, column - BLOCK, column)
        paired = ((source < after) & (source >= start_of(after, offsets))).astype(LOW)
        bt = back_top[here]
        weighted = shrink[...] * bt
        sums = dot(paired, split(weighted, -weighted * wkv[here]))
        following = start_of(first + BLOCK + jnp.zeros((1, 1), jnp.int32), offsets)
        tail = (source >= following).astype(F32)
        top = grow[...] * (sums[:, :width] + tail * (fade_half * state[0:1, :]))
        bottom = grow[...] * (sums[:, width:] + tail * (fade_half * state[1:2, :]))
        crossing = state_ref[block, :, :] * state[...]
        sums_out[32:40, :] += jnp.where(rows_of((8, 1)) < 2, crossing * (-1.0 * BLOCK), 0.0)
        state[0:1, :] = top[EDGE - 1 : EDGE]
        state[1:2, :] = bottom[EDGE - 1 : EDGE]
        weight = jnp.exp(key)
        own = jnp.exp(reward + key) * bt
        passed = weight * (value * top[EDGE:] + bottom[EDGE:])
        bonus = own * (value - wkv[here])
        back_key = passed + bonus
        acts[3, here, :] = back_key.astype(LOW)
        acts[4, here, :] = (weight * top[EDGE:] + own).astype(LOW)
        local = rows_of((BLOCK, 1)).astype(F32)
        sums_out[24:32, :] += fold(bonus)
        sums_out[32:40, :] += fold(local * back_key + passed)

    gain, bias = vec(vectors, GAIN_ONE), vec(vectors, BIAS_ONE)
    hat, scale = normed(x_ref[...].astype(F32))
    norm = hat * gain + bias
    edge_hat, _ = normed(edge_ref[...].astype(F32))
    edge = (edge_hat * gain + bias)[edge_ref.shape[0] - 1 : edge_ref.shape[0]]
    places = tile * rows + rows_of((rows, 1))
    keep = (places != start_of(places, offsets)).astype(F32)
    before = shift_down(norm, edge, keep)
    late = norm - before
    back_norm, back_before = None, None
    for number, mix_row in enumerate((KEY_MIX, VALUE_MIX, GATE_MIX)):
        mix = vec(vectors, mix_row)
        acts[number] = (norm * mix + before * (1.0 - mix)).astype(LOW)
        back_mixed = dot_nt(acts[3 + number], matrix(weights.at[number]))
        sums_out[8 * number : 8 * number + 8, :] += fold(back_mixed * late)
        one, two = back_mixed * mix, back_mixed * (1.0 - mix)
        back_norm = one if back_norm is None else back_norm + one
        back_before = two if back_before is None else back_before + two
    back_before = back_before * keep
    back_norm = back_norm + shift_up(back_before, carry[0:1, :])
    carry[0:1, :] = back_before[0:1]
    sums_out[40:48, :] += fold(back_norm * hat)
    sums_out[48:56, :] += fold(back_norm)
    stream_out[...] = (back_mid + norm_grad(back_norm, hat, scale, gain)).astype(LOW)


def back_kernel(*refs):
    step = pl.program_id(0)
    back_tile(pl.num_programs(0) - 1 - step, step == 0, *refs)


MESH = pl.DeviceIdType.MESH
GRID = (4, 2, 2, 2)
SMALL_ROWS = 16
HOPS = 11


def place():
    wide, narrow = lax.axis_index("wide"), lax.axis_index("narrow")
    return wide // 2, wide % 2, narrow // 2, narrow % 2


def device(z, y, x, c):
    return (z * 2 + y, x * 2 + c)


def greet():
    z, y, x, c = place()
    others = [(z, y, x, 1 - c), (z, y, 1 - x, c), (z, 1 - y, x, c)]
    others += [(lax.rem(z + k, GRID[0]), y, x, c) for k in range(1, GRID[0])]
    barrier = pltpu.get_barrier_semaphore()
    for other in others:
        pl.semaphore_signal(barrier, inc=1, device_id=device(*other), device_id_type=MESH)
    pl.semaphore_wait(barrier, len(others))


class Gather:
    def __init__(self, own, held, send, receive):
        self.own, self.held, self.send, self.receive = own, held, send, receive
        self.z, self.y, self.x, self.c = place()

    def column(self, y, x, c, half=None):
        if half is None:
            return self.held.at[:, y, x, c]
        part = GRID[0] // 2
        return self.held.at[pl.ds(half * part, part), y, x, c]

    def copy(self, number, source, target, to):
        return pltpu.make_async_remote_copy(
            src_ref=source,
            dst_ref=target,
            send_sem=self.send.at[number],
            recv_sem=self.receive.at[number],
            device_id=device(*to),
            device_id_type=MESH,
        )

    def along(self, k, mine):
        z = self.z if mine else lax.rem(self.z + GRID[0] - k, GRID[0])
        view = self.held.at[z, self.y, self.x, self.c]
        return self.copy(k - 1, self.own, view, (lax.rem(self.z + k, GRID[0]), self.y, self.x, self.c))

    def hop(self, number, mine):
        z, y, x, c = self.z, self.y, self.x, self.c
        if number < 3:
            return self.along(number + 1, mine)
        sent = (
            ((y, x, c), None, (z, y, 1 - x, c)),
            ((y, x, c), None, (z, 1 - y, x, c)),
            ((y, 1 - x, c), 0, (z, 1 - y, x, c)),
            ((1 - y, x, c), 1, (z, y, 1 - x, c)),
            ((y, x, c), None, (z, y, x, 1 - c)),
            ((y, 1 - x, c), None, (z, y, x, 1 - c)),
            ((1 - y, x, c), None, (z, y, x, 1 - c)),
            ((1 - y, 1 - x, c), None, (z, y, x, 1 - c)),
        )
        landing = (
            (y, 1 - x, c),
            (1 - y, x, c),
            (1 - y, 1 - x, c),
            (1 - y, 1 - x, c),
            (y, x, 1 - c),
            (y, 1 - x, 1 - c),
            (1 - y, x, 1 - c),
            (1 - y, 1 - x, 1 - c),
        )
        source, half, to = sent[number - 3]
        view = self.column(*(source if mine else landing[number - 3]), half)
        return self.copy(number, view, view, to)

    def start(self, *numbers):
        for number in numbers:
            self.hop(number, True).start()

    def arrived(self, *numbers):
        for number in numbers:
            self.hop(number, False).wait_recv()

    def sent(self):
        for number in range(HOPS):
            self.hop(number, True).wait_send()


def gather_kernel(
    tiles, extents, small, wk, wv, wr, wo, wg, w1, w2, x_ref,
    held, vectors, k_out, v_out, s_out, y_out, d_out, blend_out, mid_out, state_out, square_out,
    small_held, own, weights, grow, shrink, last, state, own_sem, load_sem, send, receive, small_send, small_receive,
):
    tick = pl.program_id(0)
    z, y, x, c = place()
    units = held.shape[0]
    width = x_ref.shape[1]
    first_tile = 7

    def unit(u):
        return Gather(own.at[u], held.at[u], send.at[lax.rem(u, 4)], receive.at[u])

    def small_unit():
        return Gather(small, small_held, small_send, small_receive)

    def keep(u):
        return pltpu.make_async_copy(own.at[u], held.at[u, z, y, x, c], own_sem.at[u])

    def load(u):
        return pltpu.make_async_copy(held.at[u], weights.at[u], load_sem.at[u])

    @pl.when(tick == 0)
    def _():
        for u, ref in enumerate((wk, wv, wr, wo, wg)):
            own[u] = ref[...]
        for j in range(4):
            own[5 + j] = w1[:, j * width : (j + 1) * width]
            own[9 + j] = w2[j]
        small_held[z, y, x, c] = small[...]
        for u in range(units):
            keep(u).start()
        greet()
        small_unit().start(0, 1, 2)
        unit(0).start(0, 1, 2)
        unit(1).start(0, 1, 2)

    @pl.when(tick < units)
    def _():
        keep(tick).wait()
        unit(tick).arrived(0, 1, 2)
        unit(tick).start(3, 4, 7)

    @pl.when(tick + 2 < units)
    def _():
        unit(tick + 2).start(0, 1, 2)

    @pl.when(tick == 0)
    def _():
        small_unit().arrived(0, 1, 2)
        small_unit().start(3, 4, 7)

    @pl.when(jnp.logical_and(tick >= 1, tick < units + 1))
    def _():
        unit(tick - 1).arrived(3, 4)
        unit(tick - 1).start(5, 6, 8, 9)

    @pl.when(tick == 1)
    def _():
        small_unit().arrived(3, 4)
        small_unit().start(5, 6, 8, 9)

    @pl.when(jnp.logical_and(tick >= 2, tick < units + 2))
    def _():
        unit(tick - 2).arrived(5, 6)
        unit(tick - 2).start(10)

    @pl.when(tick == 2)
    def _():
        small_unit().arrived(5, 6)
        small_unit().start(10)

    @pl.when(tick >= 3)
    def _():
        unit(tick - 3).arrived(7, 8, 9, 10)
        unit(tick - 3).sent()

    @pl.when(jnp.logical_and(tick >= 3, tick < 7))
    def _():
        load(tick - 3).start()

    @pl.when(tick == first_tile)
    def _():
        for u in range(4):
            load(u).wait()

    @pl.when(tick == 3)
    def _():
        small_unit().arrived(7, 8, 9, 10)
        small_unit().sent()
        share = width // (GRID[0] * 8)
        total = jnp.zeros((SMALL_ROWS, width), F32)
        empty = jnp.zeros((SMALL_ROWS, width - 128), F32)
        for number in range(GRID[0] * 8):
            block = small_held[number // 8, number // 4 % 2, number // 2 % 2, number % 2].astype(F32)
            total += pltpu.roll(jnp.concatenate([block, empty], axis=1), number * share, 1)
        vectors[...] = total

    @pl.when(jnp.logical_and(tick >= first_tile, tick < first_tile + tiles))
    def _():
        front_tile(
            tick - first_tile, extents, vectors, x_ref, *[weights.at[u] for u in range(4)],
            k_out, v_out, s_out, y_out, d_out, blend_out, mid_out, state_out, square_out,
            grow, shrink, last, state,
        )


class Order:
    def __init__(self, units, tiles, lead):
        self.units, self.tiles, self.lead = units, tiles, lead
        self.turns = 2 * (units - lead)
        last = lead - 1 if self.turns == 0 else lead + self.turns - 2
        self.ticks = max(units + tiles, last + 5)

    def units_before(self, tick):
        return jnp.minimum(jnp.minimum(tick, self.lead + jnp.maximum(tick - self.lead + 1, 0) // 2), self.units - 1)

    def tiles_before(self, tick):
        after = jnp.maximum(tick - self.lead, 0) // 2
        return jnp.clip(jnp.maximum(after, tick - self.units), 0, self.tiles - 1)

    def makes(self, tick):
        turn = jnp.logical_and(lax.rem(jnp.maximum(tick - self.lead, 0), 2) == 0, tick < self.lead + self.turns)
        return jnp.logical_and(tick >= 0, jnp.logical_or(tick < self.lead, turn))

    def tile_now(self, tick):
        return jnp.logical_and(jnp.logical_not(self.makes(tick)), tick < self.units + self.tiles)


class Reduce:
    def __init__(self, order, turned, out, mine, pairs, sides_x, sides_y, blocks_x, blocks_y, kept_sum, going, coming,
                 send, receive, turned_in=None, turned_receive=None):
        self.order, self.turned, self.out = order, turned, out
        self.mine, self.pairs, self.sides_x, self.sides_y = mine, pairs, sides_x, sides_y
        self.blocks_x, self.blocks_y, self.kept_sum, self.going, self.coming = blocks_x, blocks_y, kept_sum, going, coming
        self.send, self.receive, self.turned_in, self.turned_receive = send, receive, turned_in, turned_receive
        z, y, x, c = place()
        self.z, self.y, self.x, self.c = z, y, x, c
        self.core, self.over_x, self.over_y = (z, y, x, 1 - c), (z, y, 1 - x, c), (z, 1 - y, x, c)
        part = GRID[0] // 2
        self.low, self.high = pl.ds(0, part), pl.ds(part, part)

    def slot(self, u):
        return lax.rem(u, SLOTS)

    def remote(self, u, number, source, target, to, receive=None):
        return pltpu.make_async_remote_copy(
            src_ref=source,
            dst_ref=target,
            send_sem=self.send.at[self.slot(u), number],
            recv_sem=self.receive.at[u, number] if receive is None else receive,
            device_id=device(*to),
            device_id_type=MESH,
        )

    def pair(self, u):
        return self.remote(u, 0, self.mine.at[self.slot(u), 1 - self.c], self.pairs.at[u], self.core)

    def sides(self, u):
        held = self.mine.at[self.slot(u), self.c]
        y, x = 1 - self.y, 1 - self.x
        return (
            self.remote(u, 1, held.at[self.low, y, x], self.sides_x.at[u], self.over_x),
            self.remote(u, 2, held.at[self.high, y, x], self.sides_y.at[u], self.over_y),
        )

    def blocks(self, u):
        held = self.mine.at[self.slot(u), self.c]
        return (
            self.remote(u, 3, held.at[:, self.y, 1 - self.x], self.blocks_x.at[u], self.over_x),
            self.remote(u, 4, held.at[:, 1 - self.y, self.x], self.blocks_y.at[u], self.over_y),
        )

    def ends(self, u):
        found = []
        for k in range(1, GRID[0]):
            to = lax.rem(self.z + k, GRID[0])
            going = self.going.at[self.slot(u), to]
            found.append(self.remote(u, 4 + k, going, self.coming.at[u, k - 1], (to, self.y, self.x, self.c)))
        return found

    def turned_end(self, u, k):
        to = u - self.turned[0]
        return self.remote(
            u, 5, self.going.at[self.slot(u)], self.turned_in.at[k - 1], (to, self.y, self.x, self.c),
            self.turned_receive.at[k - 1],
        )

    def is_turned(self, u):
        return jnp.logical_and(u >= self.turned[0], u < self.turned[1])

    def make(self, tick, left, right):
        u = self.order.units_before(tick)

        @pl.when(self.order.makes(tick))
        def _():
            slot = self.slot(u)
            grad = dot_tn(left[0], right[0]).astype(LOW)
            depth, width = self.out.shape[-2:]
            z, y, x, c = GRID

            def even():
                blocks = grad.reshape(z, y, x, c, depth, width)
                for core in range(c):
                    self.mine[slot, core] = blocks[:, :, :, core]

            def turned():
                blocks = grad.reshape(y, x, c, z, depth, width)
                for core in range(c):
                    for j in range(y):
                        for i in range(x):
                            self.mine[slot, core, :, j, i] = blocks[j, i, core]

            if self.turned is None:
                even()
            else:
                pl.when(self.is_turned(u))(turned)
                pl.when(jnp.logical_not(self.is_turned(u)))(even)
            self.pair(u).start()

    def stage(self, tick, lag, work):
        u = self.order.units_before(tick - lag)
        pl.when(self.order.makes(tick - lag))(functools.partial(work, u))

    def add_pair(self, u):
        slot, c = self.slot(u), self.c
        self.pair(u).wait()
        self.mine[slot, c] = (self.mine[slot, c].astype(F32) + self.pairs[u].astype(F32)).astype(LOW)
        for copy in self.sides(u):
            copy.start()

    def add_sides(self, u):
        for copy in self.sides(u):
            copy.wait()
        held = self.mine.at[self.slot(u), self.c]
        low, high, y, x = self.low, self.high, self.y, self.x
        held[low, 1 - y, x] = (held[low, 1 - y, x].astype(F32) + self.sides_x[u].astype(F32)).astype(LOW)
        held[high, y, 1 - x] = (held[high, y, 1 - x].astype(F32) + self.sides_y[u].astype(F32)).astype(LOW)
        for copy in self.blocks(u):
            copy.start()

    def add_blocks(self, u):
        slot = self.slot(u)
        for copy in self.blocks(u):
            copy.wait()
        total = self.mine[slot, self.c, :, self.y, self.x].astype(F32)
        total = total + self.blocks_x[u].astype(F32) + self.blocks_y[u].astype(F32)
        self.kept_sum[slot] = total
        self.going[slot] = total.astype(LOW)

        def even():
            for copy in self.ends(u):
                copy.start()

        if self.turned is None:
            even()
        else:
            pl.when(jnp.logical_not(self.is_turned(u)))(even)
            for k in range(1, GRID[0]):
                away = lax.rem(self.z + GRID[0] - (u - self.turned[0]), GRID[0]) == k
                pl.when(jnp.logical_and(self.is_turned(u), away))(lambda k=k: self.turned_end(u, k).start())

    def add_ends(self, u):
        slot = self.slot(u)

        def even():
            for copy in self.ends(u):
                copy.wait()
            total = self.kept_sum[slot, self.z]
            for k in range(GRID[0] - 1):
                total += self.coming[u, k].astype(F32)
            self.out[u] = total

        def turned_here():
            total = self.kept_sum[slot]
            for k in range(1, GRID[0]):
                self.turned_end(u, k).wait_recv()
                total += self.turned_in[k - 1].astype(F32)
            self.out[self.turned[0] : self.turned[1]] = total

        if self.turned is None:
            even()
        else:
            pl.when(jnp.logical_not(self.is_turned(u)))(even)
            ahead = lax.rem(self.z + GRID[0] - (u - self.turned[0]), GRID[0])
            pl.when(jnp.logical_and(self.is_turned(u), ahead == 0))(turned_here)
            for k in range(1, GRID[0]):
                pl.when(jnp.logical_and(self.is_turned(u), ahead == k))(lambda k=k: self.turned_end(u, k).wait_send())

    def run(self, tick, left, right):
        self.make(tick, left, right)
        self.stage(tick, 1, self.add_pair)
        self.stage(tick, 2, self.add_sides)
        self.stage(tick, 3, self.add_blocks)
        self.stage(tick, 4, self.add_ends)


def back_reduce_kernel(order, *refs):
    inputs, refs = refs[:12], refs[12:]
    left, right, *refs = refs
    outputs, out, refs = refs[:3], refs[3], refs[4:]
    scratch, refs = refs[:4], refs[4:]
    tick = pl.program_id(0)
    pl.when(tick == 0)(greet)
    Reduce(order, (4, 8), out, *refs).run(tick, left, right)

    @pl.when(order.tile_now(tick))
    def _():
        number = order.tiles_before(tick)
        back_tile(order.tiles - 1 - number, number == 0, *inputs, *outputs, *scratch)


def last_reduce_kernel(order, vectors, sums_one, sums_two, square, left, right, out, small_out, *refs):
    *refs, sums, small_in, small_send, small_receive = refs
    tick = pl.program_id(0)
    z, y, x, c = place()
    partners = (
        (z, y, x, 1 - c),
        (z, y, 1 - x, c),
        (z, 1 - y, x, c),
        (z + 1 - 2 * lax.rem(z, 2), y, x, c),
        (lax.rem(z + 2, GRID[0]), y, x, c),
    )

    def exchange(step):
        return pltpu.make_async_remote_copy(
            src_ref=sums.at[step],
            dst_ref=small_in.at[step],
            send_sem=small_send.at[step],
            recv_sem=small_receive.at[step],
            device_id=device(*partners[step]),
            device_id_type=MESH,
        )

    @pl.when(tick == 0)
    def _():
        sums[0] = small_grads(vectors, sums_one, sums_two, square)
        greet()
        exchange(0).start()

    Reduce(order, None, out, *refs).run(tick, left, right)

    for step in range(1, 6):

        @pl.when(tick == step)
        def _():
            exchange(step - 1).wait()
            total = sums[step - 1] + small_in[step - 1]
            if step == 5:
                small_out[...] = total
            else:
                sums[step] = total
                exchange(step).start()


def whole(shape):
    return pl.BlockSpec(shape, lambda i: (0,) * len(shape), pipeline_mode=pl.Buffered(1))


def kept(shape):
    return pl.BlockSpec(shape, lambda i: (0,) * len(shape))


def smem():
    return pl.BlockSpec(memory_space=pltpu.SMEM)


ROWS = 256
UNITS = 13
SLOTS = 5
FEED_ACTS = 14


def four(packed):
    return pl.BlockSpec((4, *packed.shape[1:]), lambda i: (0,) * len(packed.shape), pipeline_mode=pl.Buffered(1))


def front_shapes(tokens, width):
    wide = jax.ShapeDtypeStruct((tokens, width), F32)
    low = jax.ShapeDtypeStruct((tokens, width), LOW)
    states = jax.ShapeDtypeStruct((tokens // BLOCK, 8, width), F32)
    return [wide] * 5 + [low, wide, states, jax.ShapeDtypeStruct((8, width), F32)]


def front_specs(width, index):
    tile = pl.BlockSpec((ROWS, width), lambda i: (index(i), 0))
    states = pl.BlockSpec((ROWS // BLOCK, 8, width), lambda i: (index(i), 0, 0))
    return [tile] * 7 + [states, kept((8, width))]


def front_scratch(width):
    return [
        pltpu.VMEM((BLOCK, width), F32),
        pltpu.VMEM((BLOCK + EDGE, width), F32),
        pltpu.VMEM((8, width), F32),
        pltpu.VMEM((8, width), F32),
    ]


def front(extents, vectors, x, packed):
    tokens, width = x.shape
    return pl.pallas_call(
        front_kernel,
        name="front",
        grid=(tokens // ROWS,),
        in_specs=[smem(), whole(vectors.shape), pl.BlockSpec((ROWS, width), lambda i: (i, 0)), four(packed)],
        out_specs=front_specs(width, lambda i: i),
        out_shape=front_shapes(tokens, width),
        scratch_shapes=front_scratch(width),
        compiler_params=pltpu.CompilerParams(vmem_limit_bytes=56 * MIB),
    )(extents, vectors, x, packed)


def gather_front(extents, small, shards, x):
    tokens, width = x.shape
    tiles = tokens // ROWS
    depth = shards[0].shape[0]
    anywhere = pl.BlockSpec(memory_space=pl.ANY)

    def index(i):
        return jnp.clip(i - 7, 0, tiles - 1)

    dma = pltpu.SemaphoreType.DMA
    return pl.pallas_call(
        functools.partial(gather_kernel, tiles),
        name="gather_front",
        grid=(max(UNITS + 3, tiles + 7),),
        in_specs=[smem()]
        + [whole(part.shape) for part in (small, *shards)]
        + [pl.BlockSpec((ROWS, width), lambda i: (index(i), 0))],
        out_specs=[anywhere, kept((SMALL_ROWS, width))] + front_specs(width, index),
        out_shape=[
            jax.ShapeDtypeStruct((UNITS, *GRID, depth, width), LOW),
            jax.ShapeDtypeStruct((SMALL_ROWS, width), F32),
        ]
        + front_shapes(tokens, width),
        scratch_shapes=[
            pltpu.VMEM((*GRID, *small.shape), LOW),
            pltpu.VMEM((UNITS, depth, width), LOW),
            pltpu.VMEM((4, *GRID, depth, width), LOW),
        ]
        + front_scratch(width)
        + [dma((UNITS,)), dma((4,)), dma((4, HOPS)), dma((UNITS, HOPS)), dma((HOPS,)), dma((HOPS,))],
        compiler_params=pltpu.CompilerParams(vmem_limit_bytes=56 * MIB, collective_id=0, has_side_effects=True),
    )(extents, small, *shards, x)


def feed(extents, vectors, mid, upstream, blend, packed):
    tokens, width = mid.shape
    hidden = 4 * width
    rows, tiles = ROWS, tokens // ROWS
    tile = pl.BlockSpec((rows, width), lambda i: (tiles - 1 - i, 0))
    edge = pl.BlockSpec((EDGE, width), lambda i: (jnp.maximum((tiles - 1 - i) * (rows // EDGE) - 1, 0), 0))
    block = packed.shape[1:]
    return pl.pallas_call(
        feed_kernel,
        name="feed",
        grid=(tiles,),
        in_specs=[smem(), whole(vectors.shape), tile, edge, tile, tile, pl.BlockSpec(memory_space=pl.ANY)],
        out_specs=[
            tile,
            tile,
            pl.BlockSpec((FEED_ACTS, rows, width), lambda i: (0, tiles - 1 - i, 0)),
            kept((48, width)),
        ],
        out_shape=[
            jax.ShapeDtypeStruct((tokens, width), LOW),
            jax.ShapeDtypeStruct((tokens, width), F32),
            jax.ShapeDtypeStruct((FEED_ACTS, tokens, width), LOW),
            jax.ShapeDtypeStruct((48, width), F32),
        ],
        scratch_shapes=[
            pltpu.VMEM((rows, hidden), F32),
            pltpu.VMEM((8, width), F32),
            pltpu.VMEM(block, LOW),
            pltpu.VMEM((4, *block), LOW),
            pltpu.VMEM((*block[:4], 4, *block[4:]), LOW),
            pltpu.SemaphoreType.DMA((6,)),
        ],
        compiler_params=pltpu.CompilerParams(vmem_limit_bytes=60 * MIB),
    )(extents, vectors, mid, mid, upstream, blend, packed)


def back_specs(tokens, width, packed, index):
    blocks = ROWS // BLOCK
    tile = pl.BlockSpec((ROWS, width), lambda i: (index(i), 0))
    edge = pl.BlockSpec((16, width), lambda i: (jnp.maximum(index(i) * (ROWS // 16) - 1, 0), 0))
    states = pl.BlockSpec((blocks, 8, width), lambda i: (index(i), 0, 0))
    inputs = [smem(), whole((SMALL_ROWS, width)), tile, edge] + [tile] * 5 + [states, tile, four(packed)]
    outputs = [tile, pl.BlockSpec((6, ROWS, width), lambda i: (0, index(i), 0)), kept((56, width))]
    shapes = [
        jax.ShapeDtypeStruct((tokens, width), LOW),
        jax.ShapeDtypeStruct((6, tokens, width), LOW),
        jax.ShapeDtypeStruct((56, width), F32),
    ]
    scratch = [
        pltpu.VMEM((BLOCK + EDGE, width), F32),
        pltpu.VMEM((BLOCK, width), F32),
        pltpu.VMEM((8, width), F32),
        pltpu.VMEM((8, width), F32),
    ]
    return inputs, outputs, shapes, scratch


def back(extents, vectors, x, saved, states, back_mid, packed):
    tokens, width = x.shape
    tiles = tokens // ROWS
    inputs, outputs, shapes, scratch = back_specs(tokens, width, packed, lambda i: tiles - 1 - i)
    return pl.pallas_call(
        back_kernel,
        name="back",
        grid=(tiles,),
        in_specs=inputs,
        out_specs=outputs,
        out_shape=shapes,
        scratch_shapes=scratch,
        compiler_params=pltpu.CompilerParams(vmem_limit_bytes=56 * MIB),
    )(extents, vectors, x, x, *saved, states, back_mid, packed)


def reduce_scratch(units, depth, width):
    z, y, x, c = GRID
    dma = pltpu.SemaphoreType.DMA
    return [
        pltpu.VMEM((SLOTS, c, z, y, x, depth, width), LOW),
        pltpu.VMEM((units, z, y, x, depth, width), LOW),
        pltpu.VMEM((units, z // 2, depth, width), LOW),
        pltpu.VMEM((units, z // 2, depth, width), LOW),
        pltpu.VMEM((units, z, depth, width), LOW),
        pltpu.VMEM((units, z, depth, width), LOW),
        pltpu.VMEM((SLOTS, z, depth, width), F32),
        pltpu.VMEM((SLOTS, z, depth, width), LOW),
        pltpu.VMEM((units, z - 1, depth, width), LOW),
        dma((SLOTS, 8)),
        dma((units, 8)),
    ]


def back_reduce(extents, vectors, x, saved, states, back_mid, packed, acts):
    tokens, width = x.shape
    tiles, depth, units, lead = tokens // ROWS, packed.shape[-2], 10, 4
    order = Order(units, tiles, lead)
    inputs, outputs, shapes, scratch = back_specs(tokens, width, packed, lambda i: tiles - 1 - order.tiles_before(i))
    left = pl.BlockSpec((1, tokens, width), lambda i: (jnp.maximum(order.units_before(i) - 3, 0), 0, 0))
    right = pl.BlockSpec(
        (1, tokens, width),
        lambda i: (7 + jnp.minimum(order.units_before(i), 4) + jnp.maximum(order.units_before(i) - 7, 0), 0, 0),
    )
    z, _, _, _ = GRID
    dma = pltpu.SemaphoreType.DMA
    return pl.pallas_call(
        functools.partial(back_reduce_kernel, order),
        name="back_reduce",
        grid=(order.ticks,),
        in_specs=inputs + [left, right],
        out_specs=outputs + [kept((units, depth, width))],
        out_shape=shapes + [jax.ShapeDtypeStruct((units, depth, width), F32)],
        scratch_shapes=scratch
        + reduce_scratch(units, depth, width)
        + [pltpu.VMEM((z - 1, z, depth, width), LOW), dma((z - 1,))],
        compiler_params=pltpu.CompilerParams(vmem_limit_bytes=63 * MIB, collective_id=1, has_side_effects=True),
    )(extents, vectors, x, x, *saved, states, back_mid, packed, acts, acts)


def last_reduce(vectors, acts, sums_one, sums_two, square, depth):
    tokens, width = acts.shape[1:]
    units = 3
    order = Order(units, 0, units)
    left = pl.BlockSpec((1, tokens, width), lambda i: (jnp.minimum(i, units - 1), 0, 0))
    right = pl.BlockSpec((1, tokens, width), lambda i: (units + jnp.minimum(i, units - 1), 0, 0))
    dma = pltpu.SemaphoreType.DMA
    small = (SMALL_ROWS, width)
    return pl.pallas_call(
        functools.partial(last_reduce_kernel, order),
        name="last_reduce",
        grid=(order.ticks,),
        in_specs=[whole(a.shape) for a in (vectors, sums_one, sums_two, square)] + [left, right],
        out_specs=[kept((units, depth, width)), kept(small)],
        out_shape=[jax.ShapeDtypeStruct((units, depth, width), F32), jax.ShapeDtypeStruct(small, F32)],
        scratch_shapes=reduce_scratch(units, depth, width)
        + [pltpu.VMEM((5, *small), F32), pltpu.VMEM((5, *small), F32), dma((5,)), dma((5,))],
        compiler_params=pltpu.CompilerParams(vmem_limit_bytes=56 * MIB, collective_id=2, has_side_effects=True),
    )(vectors, sums_one, sums_two, square, acts, acts)


def small_grads(vectors, sums_one, sums_two, square):
    width = vectors.shape[1]
    one = [jnp.sum(sums_one[8 * i : 8 * i + 8, :], axis=0, keepdims=True) for i in range(7)]
    two = [jnp.sum(sums_two[8 * i : 8 * i + 8, :], axis=0, keepdims=True) for i in range(6)]
    decay = one[4] * jnp.exp(vec(vectors, FADING))
    lane = rows_of((1, width), 1)
    squares = jnp.zeros((1, width), F32)
    for place_of, total in enumerate((two[4], jnp.sum(square[...], axis=0, keepdims=True), two[5])):
        squares = jnp.where(lane == place_of, jnp.sum(total, axis=1, keepdims=True), squares)
    rows = [one[0], one[1], one[2], decay, one[3], two[0], two[1], one[5], one[6], two[2], two[3], squares]
    return jnp.concatenate(rows + [jnp.zeros((SMALL_ROWS - len(rows), width), F32)], axis=0)


def pack(weights):
    *square, w1, w2 = weights
    depth, width = square[0].shape[-2:]
    parts = list(square)
    parts += [w1[..., j * width : (j + 1) * width] for j in range(4)]
    parts += [w2[..., j * depth : (j + 1) * depth, :] for j in range(4)]
    return jnp.stack(parts)


SMALL = (0, 1, 2, 3, 4, 9, 10, 14, 15, 16, 17)
LARGE = (5, 6, 7, 8, 13, 11, 12)


def finish(outcome, stream, large, small, squares, entries):
    shards = [None] * 18
    for row, i in enumerate(SMALL):
        shards[i] = small[row]
    for grad, i in zip(large, LARGE):
        shards[i] = grad
    return (outcome, stream, *shards, jnp.sqrt(squares / entries))


def body_any(residual_input, extents, *rest):
    parameters, upstream = rest[:18], rest[18]
    devices = lax.axis_size(AXES)
    held = jnp.stack([parameters[i] for i in SMALL])
    width = held.shape[1] * devices
    vectors = lax.all_gather(held, AXES, axis=1, tiled=True).astype(F32)
    vectors = jnp.pad(vectors, ((0, SMALL_ROWS - len(SMALL)), (0, 0)))
    blocks = 1
    for size in GRID:
        blocks *= size
    weights = [lax.all_gather(parameters[i], AXES, axis=0, tiled=True) for i in LARGE]
    packed = pack([w.reshape(blocks, -1, w.shape[1]) for w in weights])
    packed = packed.reshape(UNITS, *GRID, *packed.shape[2:])
    *saved, blend, mid, states, square = front(extents, vectors, residual_input, packed)
    outcome, back_mid, acts, sums_two = feed(extents, vectors, mid, upstream, blend, packed)
    stream, mixed, sums_one = back(extents, vectors, residual_input, saved, states, back_mid, packed)
    small = small_grads(vectors, sums_one, sums_two, square)
    grads = [dot_tn(mixed[i], mixed[3 + i]) for i in range(3)] + [dot_tn(acts[6], acts[13]), dot_tn(acts[5], acts[12])]
    grads.append(jnp.concatenate([dot_tn(acts[0], acts[7 + j]) for j in range(4)], axis=1))
    grads.append(jnp.concatenate([dot_tn(acts[1 + j], acts[11]) for j in range(4)], axis=0))
    squares = lax.psum(small[len(SMALL), :3], AXES)
    small = lax.psum_scatter(small[: len(SMALL)], AXES, scatter_dimension=1, tiled=True)
    large = [lax.psum_scatter(grad, AXES, scatter_dimension=0, tiled=True) for grad in grads]
    return finish(outcome, stream, large, small, squares, residual_input.shape[0] * width * devices)


def body(residual_input, extents, *rest):
    parameters, upstream = rest[:18], rest[18]
    devices = lax.axis_size(AXES)
    width = residual_input.shape[1]
    share = width // devices
    small = jnp.stack([parameters[i] for i in SMALL])
    small = jnp.pad(small, ((0, SMALL_ROWS - len(SMALL)), (0, 128 - share)))
    shards = [parameters[i] for i in LARGE]
    shards[6] = shards[6].reshape(4, share, width)
    packed, vectors, *saved, blend, mid, states, square = gather_front(extents, small, shards, residual_input)
    outcome, back_mid, acts, sums_two = feed(extents, vectors, mid, upstream, blend, packed)
    stream, mixed, sums_one, most = back_reduce(
        extents, vectors, residual_input, saved, states, back_mid, packed, acts
    )
    rest, small = last_reduce(vectors, mixed, sums_one, sums_two, square, share)
    mine = lax.axis_index(AXES)
    squares = small[len(SMALL), :3]
    small = lax.dynamic_slice(small, (0, mine * share), (len(SMALL), share))
    large = [rest[0], rest[1], rest[2], most[9], most[8]]
    large.append(jnp.concatenate([most[j] for j in range(4)], axis=1))
    large.append(most[4:8].reshape(4 * share, width))
    return finish(outcome, stream, large, small, squares, residual_input.shape[0] * width * devices)


def solution(mesh):
    rows, vector = P(AXES, None), P(AXES)
    kinds = [vector] * 5 + [rows] * 4 + [vector] * 2 + [rows] * 3 + [vector] * 4
    sizes = (mesh.shape["wide"], mesh.shape["narrow"])
    return jax.shard_map(
        body if sizes == (GRID[0] * GRID[1], GRID[2] * GRID[3]) else body_any,
        mesh=mesh,
        in_specs=(rows, rows, *kinds, rows),
        out_specs=(rows, rows, *kinds, P()),
        check_vma=False,
    )
```

```python
import functools

import jax
import jax.numpy as jnp
from jax import lax
from jax.experimental import pallas as pl
from jax.experimental.pallas import tpu as pltpu
from jax.sharding import PartitionSpec as P

F32 = jnp.float32
LOW = jnp.bfloat16
AXES = ("wide", "narrow")
BLOCK = 128
EDGE = 8
MIB = 2**20

(KEY_MIX, VALUE_MIX, GATE_MIX, FADING, REWARD, FEED_MIX, GATING_MIX, GAIN_ONE, BIAS_ONE, GAIN_TWO, BIAS_TWO) = range(11)
VECTORS = 16


def dot(left, right):
    return jnp.dot(left, right, preferred_element_type=F32)


def dot_nt(left, right):
    return lax.dot_general(left, right, (((1,), (1,)), ((), ())), preferred_element_type=F32)


def dot_tn(left, right):
    return lax.dot_general(left, right, (((0,), (0,)), ((), ())), preferred_element_type=F32)


def offsets_of(extents):
    offsets, total = [], 0
    for j in range(extents.shape[1] - 1):
        total = total + extents[0, j]
        offsets.append(total)
    return offsets


def start_of(places, offsets):
    begun = jnp.zeros_like(places)
    for offset in offsets:
        begun = jnp.where(places >= offset, offset, begun)
    return begun


def normed(x):
    centered = x - jnp.mean(x, axis=1, keepdims=True)
    scale = lax.rsqrt(jnp.mean(centered * centered, axis=1, keepdims=True) + 1e-05)
    return centered * scale, scale


def fold(x):
    return jnp.sum(x.reshape(x.shape[0] // 8, 8, x.shape[1]), axis=0)


def rows_of(shape, axis=0):
    return lax.broadcasted_iota(jnp.int32, shape, axis)


def shift_down(x, first, keep):
    return jnp.where(rows_of((x.shape[0], 1)) == 0, first, pltpu.roll(x, 1, 0)) * keep


def shift_up(x, last):
    rows = x.shape[0]
    return jnp.where(rows_of((rows, 1)) == rows - 1, last, pltpu.roll(x, rows - 1, 0))


def split(top, bottom):
    both = jnp.concatenate([top, bottom], axis=1)
    high = both.astype(LOW)
    low = (both - high.astype(F32)).astype(LOW)
    return jnp.concatenate([high, low], axis=0)


def norm_grad(back_normed, hat, scale, gain):
    back_hat = back_normed * gain
    return scale * (
        back_hat
        - jnp.mean(back_hat, axis=1, keepdims=True)
        - hat * jnp.mean(back_hat * hat, axis=1, keepdims=True)
    )


def vec(vectors, row):
    return vectors[row : row + 1, :]


def matrix(ref):
    return ref[...].reshape(-1, ref.shape[-1])


def front_tile(
    tile, extents, vectors, x_ref, wk, wv, wr, wo,
    k_out, v_out, s_out, y_out, d_out, blend_out, mid_out, state_out, square_out,
    grow, shrink, last, state,
):
    rows, width = x_ref.shape
    half = BLOCK // 2
    offsets = offsets_of(extents)
    rate = jnp.exp(vec(vectors, FADING))

    @pl.when(tile == 0)
    def _():
        local = rows_of((BLOCK + EDGE, 1)).astype(F32)
        shrink[...] = jnp.exp((half - local) * rate)
        grow[...] = jnp.exp((local[:BLOCK] + (1 - half)) * rate)
        last[...] = jnp.zeros_like(last)
        state[...] = jnp.zeros_like(state)
        square_out[...] = jnp.zeros_like(square_out)

    x = x_ref[...].astype(F32)
    hat, _ = normed(x)
    norm = hat * vec(vectors, GAIN_ONE) + vec(vectors, BIAS_ONE)
    places = tile * rows + rows_of((rows, 1))
    keep = (places != start_of(places, offsets)).astype(F32)
    before = shift_down(norm, last[0:1, :], keep)
    last[0:1, :] = norm[rows - 1 : rows, :]

    def mixed(row):
        mix = vec(vectors, row)
        return (norm * mix + before * (1.0 - mix)).astype(LOW)

    keys = dot(mixed(KEY_MIX), matrix(wk))
    values = dot(mixed(VALUE_MIX), matrix(wv))
    sig = jax.nn.sigmoid(dot(mixed(GATE_MIX), matrix(wr)))
    k_out[...] = keys
    v_out[...] = values
    s_out[...] = sig
    fade_half = jnp.exp(-half * rate)
    reward = vec(vectors, REWARD)
    for block in range(rows // BLOCK):
        here = slice(block * BLOCK, (block + 1) * BLOCK)
        key, value = keys[here], values[here]
        weight = grow[...] * jnp.exp(key)
        first = tile * rows + block * BLOCK
        after = first + rows_of((BLOCK + EDGE, 1))
        column = rows_of((1, 2 * BLOCK), 1)
        source = first + jnp.where(column >= BLOCK, column - BLOCK, column)
        begun = start_of(after, offsets)
        paired = ((source < after) & (source >= begun)).astype(LOW)
        sums = dot(paired, split(weight * value, weight))
        inherit = (begun < first).astype(F32)
        top = shrink[...] * (sums[:, :width] + inherit * (fade_half * state[0:1, :]))
        bottom = shrink[...] * (sums[:, width:] + inherit * (fade_half * state[1:2, :]))
        state[0:1, :] = top[BLOCK : BLOCK + 1]
        state[1:2, :] = bottom[BLOCK : BLOCK + 1]
        state_out[block, :, :] = state[...]
        own = jnp.exp(reward + key)
        inverse = 1.0 / (bottom[:BLOCK] + own)
        wkv = (top[:BLOCK] + own * value) * inverse
        y_out[here, :] = wkv
        d_out[here, :] = inverse
        blend_out[here, :] = (sig[here] * wkv).astype(LOW)
    attended = dot(blend_out[...], matrix(wo))
    mid_out[...] = x + attended
    square_out[...] += fold(attended * attended)


def front_kernel(extents, vectors, x_ref, weights, *rest):
    front_tile(pl.program_id(0), extents, vectors, x_ref, *[weights.at[u] for u in range(4)], *rest)


def feed_kernel(
    extents, vectors, mid_ref, edge_ref, up_ref, blend_ref, packed,
    out_out, back_out, acts, sums_out,
    lift, carry, wg, w1, w2, load,
):
    step = pl.program_id(0)
    tile = pl.num_programs(0) - 1 - step
    rows, width = mid_ref.shape
    hidden = lift.shape[1]
    offsets = offsets_of(extents)

    @pl.when(step == 0)
    def _():
        copies = [(packed.at[4], wg), (packed.at[5:9], w1)]
        copies += [(packed.at[9 + j], w2.at[:, :, :, :, j]) for j in range(4)]
        copies = [pltpu.make_async_copy(a, b, load.at[i]) for i, (a, b) in enumerate(copies)]
        for copy in copies:
            copy.start()
        for copy in copies:
            copy.wait()
        carry[...] = jnp.zeros_like(carry)
        sums_out[...] = jnp.zeros_like(sums_out)

    gain, bias = vec(vectors, GAIN_TWO), vec(vectors, BIAS_TWO)
    mid = mid_ref[...]
    hat, scale = normed(mid)
    norm = hat * gain + bias
    edge_hat, _ = normed(edge_ref[...])
    edge = (edge_hat * gain + bias)[EDGE - 1 : EDGE]
    places = tile * rows + rows_of((rows, 1))
    keep = (places != start_of(places, offsets)).astype(F32)
    before = shift_down(norm, edge, keep)
    mix_k, mix_g = vec(vectors, FEED_MIX), vec(vectors, GATING_MIX)
    feed_key = (norm * mix_k + before * (1.0 - mix_k)).astype(LOW)
    feed_gate = (norm * mix_g + before * (1.0 - mix_g)).astype(LOW)
    acts[0] = feed_key
    acts[5] = feed_gate
    acts[6] = blend_ref[...]
    lowered = None
    for j in range(hidden // width):
        chunk = slice(j * width, (j + 1) * width)
        lifted = jnp.maximum(dot(feed_key, matrix(w1.at[j])), 0.0)
        lift[:, chunk] = lifted
        squared = (lifted * lifted).astype(LOW)
        acts[1 + j] = squared
        part = dot(squared, matrix(w2.at[j]))
        lowered = part if lowered is None else lowered + part
    sig = jax.nn.sigmoid(dot(feed_gate, matrix(wg)))
    feed_out = sig * lowered
    result = mid + feed_out
    out_out[...] = result.astype(LOW)
    upstream = up_ref[...].astype(F32)
    back_lowered = (upstream * sig).astype(LOW)
    back_gate = (upstream * lowered * sig * (1.0 - sig)).astype(LOW)
    acts[11] = back_lowered
    acts[12] = back_gate
    back_key = None
    for j in range(hidden // width):
        chunk = slice(j * width, (j + 1) * width)
        back_lifted = (2.0 * lift[:, chunk] * dot_nt(back_lowered, matrix(w2.at[j]))).astype(LOW)
        acts[7 + j] = back_lifted
        part = dot_nt(back_lifted, matrix(w1.at[j]))
        back_key = part if back_key is None else back_key + part
    back_gating = dot_nt(back_gate, matrix(wg))
    late = norm - before
    back_before = keep * (back_key * (1.0 - mix_k) + back_gating * (1.0 - mix_g))
    back_norm = back_key * mix_k + back_gating * mix_g + shift_up(back_before, carry[0:1, :])
    carry[0:1, :] = back_before[0:1]
    back_mid = upstream + norm_grad(back_norm, hat, scale, gain)
    back_out[...] = back_mid
    acts[13] = back_mid.astype(LOW)
    for row, piece in enumerate(
        (back_key * late, back_gating * late, back_norm * hat, back_norm, result * result, feed_out * feed_out)
    ):
        sums_out[8 * row : 8 * row + 8, :] += fold(piece)


def back_tile(
    tile, begins, extents, vectors, x_ref, edge_ref, k_ref, v_ref, s_ref, y_ref, d_ref, state_ref, mid_ref, weights,
    stream_out, acts, sums_out,
    grow, shrink, carry, state, between=(),
):
    rows, width = x_ref.shape
    half = BLOCK // 2
    offsets = offsets_of(extents)
    rate = jnp.exp(vec(vectors, FADING))

    @pl.when(begins)
    def _():
        local = rows_of((BLOCK + EDGE, 1)).astype(F32)
        shrink[...] = jnp.exp((half - local[:BLOCK]) * rate)
        grow[...] = jnp.exp((local + (1 - EDGE - half)) * rate)
        carry[...] = jnp.zeros_like(carry)
        state[...] = jnp.zeros_like(state)
        sums_out[...] = jnp.zeros_like(sums_out)

    between = iter(between)
    back_mid = mid_ref[...]
    back_attended = back_mid.astype(LOW)
    back_blend = dot_nt(back_attended, matrix(weights.at[3]))
    sig = s_ref[...]
    wkv = y_ref[...]
    acts[5] = (back_blend * wkv * sig * (1.0 - sig)).astype(LOW)
    back_top = back_blend * sig * d_ref[...]
    fade_half = jnp.exp(-half * rate)
    reward = vec(vectors, REWARD)
    for block in reversed(range(rows // BLOCK)):
        next(between, int)()
        here = slice(block * BLOCK, (block + 1) * BLOCK)
        key, value = k_ref[here, :], v_ref[here, :]
        first = tile * rows + block * BLOCK
        source = first - EDGE + rows_of((BLOCK + EDGE, 1))
        column = rows_of((1, 2 * BLOCK), 1)
        after = first + jnp.where(column >= BLOCK, column - BLOCK, column)
        paired = ((source < after) & (source >= start_of(after, offsets))).astype(LOW)
        bt = back_top[here]
        weighted = shrink[...] * bt
        sums = dot(paired, split(weighted, -weighted * wkv[here]))
        following = start_of(first + BLOCK + jnp.zeros((1, 1), jnp.int32), offsets)
        tail = (source >= following).astype(F32)
        top = grow[...] * (sums[:, :width] + tail * (fade_half * state[0:1, :]))
        bottom = grow[...] * (sums[:, width:] + tail * (fade_half * state[1:2, :]))
        next(between, int)()
        crossing = state_ref[block, :, :] * state[...]
        sums_out[32:40, :] += jnp.where(rows_of((8, 1)) < 2, crossing * (-1.0 * BLOCK), 0.0)
        state[0:1, :] = top[EDGE - 1 : EDGE]
        state[1:2, :] = bottom[EDGE - 1 : EDGE]
        weight = jnp.exp(key)
        own = jnp.exp(reward + key) * bt
        passed = weight * (value * top[EDGE:] + bottom[EDGE:])
        bonus = own * (value - wkv[here])
        back_key = passed + bonus
        acts[3, here, :] = back_key.astype(LOW)
        acts[4, here, :] = (weight * top[EDGE:] + own).astype(LOW)
        local = rows_of((BLOCK, 1)).astype(F32)
        sums_out[24:32, :] += fold(bonus)
        sums_out[32:40, :] += fold(local * back_key + passed)

    gain, bias = vec(vectors, GAIN_ONE), vec(vectors, BIAS_ONE)
    hat, scale = normed(x_ref[...].astype(F32))
    norm = hat * gain + bias
    edge_hat, _ = normed(edge_ref[...].astype(F32))
    edge = (edge_hat * gain + bias)[edge_ref.shape[0] - 1 : edge_ref.shape[0]]
    places = tile * rows + rows_of((rows, 1))
    keep = (places != start_of(places, offsets)).astype(F32)
    before = shift_down(norm, edge, keep)
    late = norm - before
    back_norm, back_before = None, None
    for number, mix_row in enumerate((KEY_MIX, VALUE_MIX, GATE_MIX)):
        next(between, int)()
        mix = vec(vectors, mix_row)
        acts[number] = (norm * mix + before * (1.0 - mix)).astype(LOW)
        back_mixed = dot_nt(acts[3 + number], matrix(weights.at[number]))
        sums_out[8 * number : 8 * number + 8, :] += fold(back_mixed * late)
        one, two = back_mixed * mix, back_mixed * (1.0 - mix)
        back_norm = one if back_norm is None else back_norm + one
        back_before = two if back_before is None else back_before + two
    back_before = back_before * keep
    back_norm = back_norm + shift_up(back_before, carry[0:1, :])
    carry[0:1, :] = back_before[0:1]
    sums_out[40:48, :] += fold(back_norm * hat)
    sums_out[48:56, :] += fold(back_norm)
    stream_out[...] = (back_mid + norm_grad(back_norm, hat, scale, gain)).astype(LOW)


def back_kernel(*refs):
    step = pl.program_id(0)
    back_tile(pl.num_programs(0) - 1 - step, step == 0, *refs)


MESH = pl.DeviceIdType.MESH
GRID = (4, 2, 2, 2)
SMALL_ROWS = 16
HOPS = 11


def place():
    wide, narrow = lax.axis_index("wide"), lax.axis_index("narrow")
    return wide // 2, wide % 2, narrow // 2, narrow % 2


def device(z, y, x, c):
    return (z * 2 + y, x * 2 + c)


def greet():
    z, y, x, c = place()
    others = [(z, y, x, 1 - c), (z, y, 1 - x, c), (z, 1 - y, x, c)]
    others += [(lax.rem(z + k, GRID[0]), y, x, c) for k in range(1, GRID[0])]
    barrier = pltpu.get_barrier_semaphore()
    for other in others:
        pl.semaphore_signal(barrier, inc=1, device_id=device(*other), device_id_type=MESH)
    pl.semaphore_wait(barrier, len(others))


class Gather:
    def __init__(self, own, held, send, receive):
        self.own, self.held, self.send, self.receive = own, held, send, receive
        self.z, self.y, self.x, self.c = place()

    def column(self, y, x, c, half=None):
        if half is None:
            return self.held.at[:, y, x, c]
        part = GRID[0] // 2
        return self.held.at[pl.ds(half * part, part), y, x, c]

    def copy(self, number, source, target, to):
        return pltpu.make_async_remote_copy(
            src_ref=source,
            dst_ref=target,
            send_sem=self.send.at[number],
            recv_sem=self.receive.at[number],
            device_id=device(*to),
            device_id_type=MESH,
        )

    def along(self, k, mine):
        z = self.z if mine else lax.rem(self.z + GRID[0] - k, GRID[0])
        view = self.held.at[z, self.y, self.x, self.c]
        return self.copy(k - 1, self.own, view, (lax.rem(self.z + k, GRID[0]), self.y, self.x, self.c))

    def hop(self, number, mine):
        z, y, x, c = self.z, self.y, self.x, self.c
        if number < 3:
            return self.along(number + 1, mine)
        sent = (
            ((y, x, c), None, (z, y, 1 - x, c)),
            ((y, x, c), None, (z, 1 - y, x, c)),
            ((y, 1 - x, c), 0, (z, 1 - y, x, c)),
            ((1 - y, x, c), 1, (z, y, 1 - x, c)),
            ((y, x, c), None, (z, y, x, 1 - c)),
            ((y, 1 - x, c), None, (z, y, x, 1 - c)),
            ((1 - y, x, c), None, (z, y, x, 1 - c)),
            ((1 - y, 1 - x, c), None, (z, y, x, 1 - c)),
        )
        landing = (
            (y, 1 - x, c),
            (1 - y, x, c),
            (1 - y, 1 - x, c),
            (1 - y, 1 - x, c),
            (y, x, 1 - c),
            (y, 1 - x, 1 - c),
            (1 - y, x, 1 - c),
            (1 - y, 1 - x, 1 - c),
        )
        source, half, to = sent[number - 3]
        view = self.column(*(source if mine else landing[number - 3]), half)
        return self.copy(number, view, view, to)

    def start(self, *numbers):
        for number in numbers:
            self.hop(number, True).start()

    def arrived(self, *numbers):
        for number in numbers:
            self.hop(number, False).wait_recv()

    def sent(self):
        for number in range(HOPS):
            self.hop(number, True).wait_send()


def gather_kernel(
    tiles, extents, small, wk, wv, wr, wo, wg, w1, w2, x_ref,
    held, vectors, k_out, v_out, s_out, y_out, d_out, blend_out, mid_out, state_out, square_out,
    small_held, own, weights, grow, shrink, last, state, own_sem, load_sem, send, receive, small_send, small_receive,
):
    tick = pl.program_id(0)
    z, y, x, c = place()
    units = held.shape[0]
    width = x_ref.shape[1]
    first_tile = 7

    def unit(u):
        return Gather(own.at[u], held.at[u], send.at[lax.rem(u, 6)], receive.at[u])

    def small_unit():
        return Gather(small, small_held, small_send, small_receive)

    def keep(u):
        return pltpu.make_async_copy(own.at[u], held.at[u, z, y, x, c], own_sem.at[u])

    def load(u):
        return pltpu.make_async_copy(held.at[u], weights.at[u], load_sem.at[u])

    @pl.when(tick == 0)
    def _():
        for u, ref in enumerate((wk, wv, wr, wo, wg)):
            own[u] = ref[...]
        for j in range(4):
            own[5 + j] = w1[:, j * width : (j + 1) * width]
            own[9 + j] = w2[j]
        small_held[z, y, x, c] = small[...]
        for u in range(units):
            keep(u).start()
        greet()
        small_unit().start(0, 1, 2)
        unit(0).start(0, 1, 2)
        unit(1).start(0, 1, 2)

    @pl.when(tick < units)
    def _():
        keep(tick).wait()
        unit(tick).arrived(0, 1, 2)
        unit(tick).start(3, 4, 7)

    @pl.when(tick + 2 < units)
    def _():
        unit(tick + 2).start(0, 1, 2)

    @pl.when(tick == 0)
    def _():
        small_unit().arrived(0, 1, 2)
        small_unit().start(3, 4, 7)

    @pl.when(jnp.logical_and(tick >= 1, tick < units + 1))
    def _():
        unit(tick - 1).arrived(3, 4)
        unit(tick - 1).start(5, 6, 8, 9)

    @pl.when(tick == 1)
    def _():
        small_unit().arrived(3, 4)
        small_unit().start(5, 6, 8, 9)

    def diagonal(u):
        unit(u).arrived(5, 6)
        unit(u).start(10)

    def complete(u):
        unit(u).arrived(7, 8, 9, 10)
        unit(u).sent()

    def within(u, first, end):
        return jnp.logical_and(u >= first, u < end)

    pl.when(within(tick - 2, 0, 4))(lambda: diagonal(tick - 2))
    pl.when(within(tick - 3, 4, units))(lambda: diagonal(tick - 3))

    @pl.when(tick == 2)
    def _():
        small_unit().arrived(5, 6)
        small_unit().start(10)

    pl.when(within(tick - 3, 0, 4))(lambda: complete(tick - 3))
    pl.when(within(tick - 5, 4, units))(lambda: complete(tick - 5))

    @pl.when(jnp.logical_and(tick >= 3, tick < 7))
    def _():
        load(tick - 3).start()

    @pl.when(tick == first_tile)
    def _():
        for u in range(4):
            load(u).wait()

    @pl.when(tick == 3)
    def _():
        small_unit().arrived(7, 8, 9, 10)
        small_unit().sent()
        share = width // (GRID[0] * 8)
        total = jnp.zeros((SMALL_ROWS, width), F32)
        empty = jnp.zeros((SMALL_ROWS, width - 128), F32)
        for number in range(GRID[0] * 8):
            block = small_held[number // 8, number // 4 % 2, number // 2 % 2, number % 2].astype(F32)
            total += pltpu.roll(jnp.concatenate([block, empty], axis=1), number * share, 1)
        vectors[...] = total

    @pl.when(jnp.logical_and(tick >= first_tile, tick < first_tile + tiles))
    def _():
        front_tile(
            tick - first_tile, extents, vectors, x_ref, *[weights.at[u] for u in range(4)],
            k_out, v_out, s_out, y_out, d_out, blend_out, mid_out, state_out, square_out,
            grow, shrink, last, state,
        )


class Reduce:
    def __init__(self, out, mine, pairs, sides_x, sides_y, blocks_x, blocks_y, kept_sum, going, coming,
                 turned_in, send, receive, turned_receive):
        self.out = out
        self.mine, self.pairs, self.sides_x, self.sides_y = mine, pairs, sides_x, sides_y
        self.blocks_x, self.blocks_y, self.kept_sum, self.going, self.coming = blocks_x, blocks_y, kept_sum, going, coming
        self.send, self.receive, self.turned_in, self.turned_receive = send, receive, turned_in, turned_receive
        z, y, x, c = place()
        self.z, self.y, self.x, self.c = z, y, x, c
        self.core, self.over_x, self.over_y = (z, y, x, 1 - c), (z, y, 1 - x, c), (z, 1 - y, x, c)
        part = GRID[0] // 2
        self.low, self.high = pl.ds(0, part), pl.ds(part, part)

    def slot(self, u):
        return lax.rem(u, SLOTS)

    def remote(self, u, number, source, target, to, receive=None):
        return pltpu.make_async_remote_copy(
            src_ref=source,
            dst_ref=target,
            send_sem=self.send.at[self.slot(u), number],
            recv_sem=self.receive.at[u, number] if receive is None else receive,
            device_id=device(*to),
            device_id_type=MESH,
        )

    def pair(self, u):
        return self.remote(u, 0, self.mine.at[self.slot(u), 1 - self.c], self.pairs.at[self.slot(u)], self.core)

    def sides(self, u):
        held = self.mine.at[self.slot(u), self.c]
        y, x = 1 - self.y, 1 - self.x
        return (
            self.remote(u, 1, held.at[self.low, y, x], self.sides_x.at[u], self.over_x),
            self.remote(u, 2, held.at[self.high, y, x], self.sides_y.at[u], self.over_y),
        )

    def blocks(self, u):
        held = self.mine.at[self.slot(u), self.c]
        return (
            self.remote(u, 3, held.at[:, self.y, 1 - self.x], self.blocks_x.at[u], self.over_x),
            self.remote(u, 4, held.at[:, 1 - self.y, self.x], self.blocks_y.at[u], self.over_y),
        )

    def ends(self, u):
        found = []
        for k in range(1, GRID[0]):
            to = lax.rem(self.z + k, GRID[0])
            going = self.going.at[self.slot(u), to]
            found.append(self.remote(u, 4 + k, going, self.coming.at[u, k - 1], (to, self.y, self.x, self.c)))
        return found

    def turned_end(self, u, k):
        to = u - TURNED[0]
        return self.remote(
            u, 5, self.going.at[self.slot(u)], self.turned_in.at[k - 1], (to, self.y, self.x, self.c),
            self.turned_receive.at[k - 1],
        )

    def is_turned(self, u):
        return jnp.logical_and(u >= TURNED[0], u < TURNED[1])

    def pieces(self, u, left, right):
        slot, depth = self.slot(u), self.out.shape[-2]
        z, y, x, c = GRID
        turned = jnp.logical_and(u >= TURNED[0], u < TURNED[1]).astype(jnp.int32)

        def piece(part, columns):
            many = left.shape[-1] // PIECES[0]
            wide = right.shape[-1] // PIECES[1]
            lanes = slice(columns * wide, (columns + 1) * wide)
            grad = dot_tn(left[:, part * many : (part + 1) * many], right[:, lanes]).astype(LOW)
            blocks = grad.reshape(many // depth, depth, grad.shape[1])
            for number in range(many // depth):
                b = part * (many // depth) + number
                even = (b % c, b // (x * y * c), b // (x * c) % y, b // c % x)
                other = (b // z % c, b % z, b // (z * c * x), b // (z * c) % x)
                where = [i + turned * (j - i) for i, j in zip(even, other)]
                self.mine[slot, where[0], where[1], where[2], where[3], :, lanes] = blocks[number]

        return [functools.partial(piece, i, j) for i in range(PIECES[0]) for j in range(PIECES[1])]

    def stage(self, tick, lag, work):
        pl.when(jnp.logical_and(tick >= lag, tick < lag + UNITS))(functools.partial(work, tick - lag))

    def add_pair(self, u):
        slot, c = self.slot(u), self.c
        self.pair(u).wait()
        self.mine[slot, c] = (self.mine[slot, c].astype(F32) + self.pairs[slot].astype(F32)).astype(LOW)
        for copy in self.sides(u):
            copy.start()

    def add_sides(self, u):
        for copy in self.sides(u):
            copy.wait()
        held = self.mine.at[self.slot(u), self.c]
        low, high, y, x = self.low, self.high, self.y, self.x
        held[low, 1 - y, x] = (held[low, 1 - y, x].astype(F32) + self.sides_x[u].astype(F32)).astype(LOW)
        held[high, y, 1 - x] = (held[high, y, 1 - x].astype(F32) + self.sides_y[u].astype(F32)).astype(LOW)
        for copy in self.blocks(u):
            copy.start()

    def add_blocks(self, u):
        slot = self.slot(u)
        for copy in self.blocks(u):
            copy.wait()
        total = self.mine[slot, self.c, :, self.y, self.x].astype(F32)
        total = total + self.blocks_x[u].astype(F32) + self.blocks_y[u].astype(F32)
        self.kept_sum[slot] = total
        self.going[slot] = total.astype(LOW)

        def even():
            for copy in self.ends(u):
                copy.start()

        pl.when(jnp.logical_not(self.is_turned(u)))(even)
        for k in range(1, GRID[0]):
            away = lax.rem(self.z + 2 * GRID[0] - jnp.minimum(u, 2 * GRID[0]), GRID[0]) == k
            pl.when(jnp.logical_and(self.is_turned(u), away))(lambda k=k: self.turned_end(u, k).start())

    def add_ends(self, u):
        slot = self.slot(u)

        def even():
            for copy in self.ends(u):
                copy.wait()
            total = self.kept_sum[slot, self.z]
            for k in range(GRID[0] - 1):
                total += self.coming[u, k].astype(F32)
            self.out[u] = total

        def turned_here():
            total = self.kept_sum[slot]
            for k in range(1, GRID[0]):
                self.turned_end(u, k).wait_recv()
                total += self.turned_in[k - 1].astype(F32)
            self.out[TURNED[0] : TURNED[1]] = total

        pl.when(jnp.logical_not(self.is_turned(u)))(even)
        ahead = lax.rem(self.z + 2 * GRID[0] - jnp.minimum(u, 2 * GRID[0]), GRID[0])
        pl.when(jnp.logical_and(self.is_turned(u), ahead == 0))(turned_here)
        for k in range(1, GRID[0]):
            pl.when(jnp.logical_and(self.is_turned(u), ahead == k))(lambda k=k: self.turned_end(u, k).wait_send())


def reduce_kernel(
    extents, vectors, x_ref, edge_ref, k_ref, v_ref, s_ref, y_ref, d_ref, state_ref, mid_ref, weights,
    sums_two, square, acts,
    stream_out, mixed, out, small_out,
    grow, shrink, carry, state, staged, sums_one, lefts, rights, sums, small_in,
    stage_sem, left_sem, right_sem, small_send, small_receive, *refs,
):
    tick = pl.program_id(0)
    z, y, x, c = place()
    rows = x_ref.shape[0]
    tiles = mixed.shape[1] // rows
    job = Reduce(out, *refs)
    partners = (
        (z, y, x, 1 - c),
        (z, y, 1 - x, c),
        (z, 1 - y, x, c),
        (z + 1 - 2 * lax.rem(z, 2), y, x, c),
        (lax.rem(z + 2, GRID[0]), y, x, c),
    )

    def exchange(step):
        return pltpu.make_async_remote_copy(
            src_ref=sums.at[step],
            dst_ref=small_in.at[step],
            send_sem=small_send.at[step],
            recv_sem=small_receive.at[step],
            device_id=device(*partners[step]),
            device_id_type=MESH,
        )

    def left_of(u):
        return lax.rem(jnp.maximum(u - 3, 0), 2)

    def right_of(u):
        return lax.rem(jnp.minimum(u, 4) + jnp.maximum(u - 7, 0), 2)

    def fetch_left(u, late):
        source = mixed.at[u - FIRST_UNITS] if late else acts.at[jnp.maximum(u - 3, 0)]
        return pltpu.make_async_copy(source, lefts.at[left_of(u)], left_sem.at[left_of(u)])

    def fetch_right(u, late):
        if late:
            source = mixed.at[u - FIRST_UNITS + 3]
        else:
            source = acts.at[7 + jnp.minimum(u, 4) + jnp.maximum(u - 7, 0)]
        return pltpu.make_async_copy(source, rights.at[right_of(u)], right_sem.at[right_of(u)])

    def fetches(u, work):
        early, late = u < FIRST_UNITS, jnp.logical_and(u >= FIRST_UNITS, u < UNITS)
        pl.when(jnp.logical_and(early, jnp.logical_or(u == 0, u >= 4)))(lambda: work(fetch_left(u, False)))
        pl.when(jnp.logical_and(early, jnp.logical_or(u <= 4, u >= 8)))(lambda: work(fetch_right(u, False)))
        pl.when(late)(lambda: work(fetch_left(u, True)))
        pl.when(late)(lambda: work(fetch_right(u, True)))

    def keep(number):
        two = lax.rem(number, 2)
        where = pl.ds(pl.multiple_of((tiles - 1 - number) * rows, rows), rows)
        return pltpu.make_async_copy(staged.at[two], mixed.at[:, where], stage_sem.at[two])

    def start(copy):
        copy.start()

    def wait(copy):
        copy.wait()

    @pl.when(tick == 0)
    def _():
        fetches(tick, start)
        greet()

    number = tick - FIRST_TILE
    pl.when(jnp.logical_and(number >= 2, number < tiles + 2))(lambda: keep(number - 2).wait())
    fetches(tick + 1, start)
    fetches(tick, wait)

    inputs = (extents, vectors, x_ref, edge_ref, k_ref, v_ref, s_ref, y_ref, d_ref, state_ref, mid_ref, weights)

    def pieces():
        return job.pieces(tick, lefts.at[left_of(tick)], rights.at[right_of(tick)])

    busy = jnp.logical_and(number >= 0, number < tiles)

    @pl.when(busy)
    def _():
        back_tile(
            tiles - 1 - number, number == 0, *inputs, stream_out, staged.at[lax.rem(number, 2)], sums_one,
            grow, shrink, carry, state, between=pieces(),
        )
        keep(number).start()
        job.pair(tick).start()

    @pl.when(jnp.logical_and(jnp.logical_not(busy), tick < UNITS))
    def _():
        for piece in pieces():
            piece()
        job.pair(tick).start()

    for lag, work in zip(LAGS, (job.add_pair, job.add_sides, job.add_blocks, job.add_ends)):
        job.stage(tick, lag, work)

    @pl.when(number == tiles)
    def _():
        sums[0] = small_grads(vectors, sums_one, sums_two, square)
        exchange(0).start()

    for step in range(1, 6):

        @pl.when(number == tiles + step)
        def _():
            exchange(step - 1).wait()
            total = sums[step - 1] + small_in[step - 1]
            if step == 5:
                small_out[...] = total
            else:
                sums[step] = total
                exchange(step).start()


def whole(shape):
    return pl.BlockSpec(shape, lambda i: (0,) * len(shape), pipeline_mode=pl.Buffered(1))


def kept(shape):
    return pl.BlockSpec(shape, lambda i: (0,) * len(shape))


def smem():
    return pl.BlockSpec(memory_space=pltpu.SMEM)


ROWS = 256
UNITS = 13
SLOTS = 6
LAGS = (1, 2, 3, 6)
PIECES = (2, 1)
FIRST_UNITS = 10
FIRST_TILE = 0
TURNED = (4, 8)
FEED_ACTS = 14


def four(packed):
    return pl.BlockSpec((4, *packed.shape[1:]), lambda i: (0,) * len(packed.shape), pipeline_mode=pl.Buffered(1))


def front_shapes(tokens, width):
    wide = jax.ShapeDtypeStruct((tokens, width), F32)
    low = jax.ShapeDtypeStruct((tokens, width), LOW)
    states = jax.ShapeDtypeStruct((tokens // BLOCK, 8, width), F32)
    return [wide] * 5 + [low, wide, states, jax.ShapeDtypeStruct((8, width), F32)]


def front_specs(width, index):
    tile = pl.BlockSpec((ROWS, width), lambda i: (index(i), 0))
    states = pl.BlockSpec((ROWS // BLOCK, 8, width), lambda i: (index(i), 0, 0))
    return [tile] * 7 + [states, kept((8, width))]


def front_scratch(width):
    return [
        pltpu.VMEM((BLOCK, width), F32),
        pltpu.VMEM((BLOCK + EDGE, width), F32),
        pltpu.VMEM((8, width), F32),
        pltpu.VMEM((8, width), F32),
    ]


def front(extents, vectors, x, packed):
    tokens, width = x.shape
    return pl.pallas_call(
        front_kernel,
        name="front",
        grid=(tokens // ROWS,),
        in_specs=[smem(), whole(vectors.shape), pl.BlockSpec((ROWS, width), lambda i: (i, 0)), four(packed)],
        out_specs=front_specs(width, lambda i: i),
        out_shape=front_shapes(tokens, width),
        scratch_shapes=front_scratch(width),
        compiler_params=pltpu.CompilerParams(vmem_limit_bytes=56 * MIB),
    )(extents, vectors, x, packed)


def gather_front(extents, small, shards, x):
    tokens, width = x.shape
    tiles = tokens // ROWS
    depth = shards[0].shape[0]
    anywhere = pl.BlockSpec(memory_space=pl.ANY)

    def index(i):
        return jnp.clip(i - 7, 0, tiles - 1)

    dma = pltpu.SemaphoreType.DMA
    return pl.pallas_call(
        functools.partial(gather_kernel, tiles),
        name="gather_front",
        grid=(max(UNITS + 5, tiles + 7),),
        in_specs=[smem()]
        + [whole(part.shape) for part in (small, *shards)]
        + [pl.BlockSpec((ROWS, width), lambda i: (index(i), 0))],
        out_specs=[anywhere, kept((SMALL_ROWS, width))] + front_specs(width, index),
        out_shape=[
            jax.ShapeDtypeStruct((UNITS, *GRID, depth, width), LOW),
            jax.ShapeDtypeStruct((SMALL_ROWS, width), F32),
        ]
        + front_shapes(tokens, width),
        scratch_shapes=[
            pltpu.VMEM((*GRID, *small.shape), LOW),
            pltpu.VMEM((UNITS, depth, width), LOW),
            pltpu.VMEM((4, *GRID, depth, width), LOW),
        ]
        + front_scratch(width)
        + [dma((UNITS,)), dma((4,)), dma((6, HOPS)), dma((UNITS, HOPS)), dma((HOPS,)), dma((HOPS,))],
        compiler_params=pltpu.CompilerParams(vmem_limit_bytes=56 * MIB, collective_id=0, has_side_effects=True),
    )(extents, small, *shards, x)


def feed(extents, vectors, mid, upstream, blend, packed):
    tokens, width = mid.shape
    hidden = 4 * width
    rows, tiles = ROWS, tokens // ROWS
    tile = pl.BlockSpec((rows, width), lambda i: (tiles - 1 - i, 0))
    edge = pl.BlockSpec((EDGE, width), lambda i: (jnp.maximum((tiles - 1 - i) * (rows // EDGE) - 1, 0), 0))
    block = packed.shape[1:]
    return pl.pallas_call(
        feed_kernel,
        name="feed",
        grid=(tiles,),
        in_specs=[smem(), whole(vectors.shape), tile, edge, tile, tile, pl.BlockSpec(memory_space=pl.ANY)],
        out_specs=[
            tile,
            tile,
            pl.BlockSpec((FEED_ACTS, rows, width), lambda i: (0, tiles - 1 - i, 0)),
            kept((48, width)),
        ],
        out_shape=[
            jax.ShapeDtypeStruct((tokens, width), LOW),
            jax.ShapeDtypeStruct((tokens, width), F32),
            jax.ShapeDtypeStruct((FEED_ACTS, tokens, width), LOW),
            jax.ShapeDtypeStruct((48, width), F32),
        ],
        scratch_shapes=[
            pltpu.VMEM((rows, hidden), F32),
            pltpu.VMEM((8, width), F32),
            pltpu.VMEM(block, LOW),
            pltpu.VMEM((4, *block), LOW),
            pltpu.VMEM((*block[:4], 4, *block[4:]), LOW),
            pltpu.SemaphoreType.DMA((6,)),
        ],
        compiler_params=pltpu.CompilerParams(vmem_limit_bytes=60 * MIB),
    )(extents, vectors, mid, mid, upstream, blend, packed)


def back_specs(tokens, width, packed, index):
    blocks = ROWS // BLOCK
    tile = pl.BlockSpec((ROWS, width), lambda i: (index(i), 0))
    edge = pl.BlockSpec((16, width), lambda i: (jnp.maximum(index(i) * (ROWS // 16) - 1, 0), 0))
    states = pl.BlockSpec((blocks, 8, width), lambda i: (index(i), 0, 0))
    inputs = [smem(), whole((SMALL_ROWS, width)), tile, edge] + [tile] * 5 + [states, tile, four(packed)]
    outputs = [tile, pl.BlockSpec((6, ROWS, width), lambda i: (0, index(i), 0)), kept((56, width))]
    shapes = [
        jax.ShapeDtypeStruct((tokens, width), LOW),
        jax.ShapeDtypeStruct((6, tokens, width), LOW),
        jax.ShapeDtypeStruct((56, width), F32),
    ]
    scratch = [
        pltpu.VMEM((BLOCK + EDGE, width), F32),
        pltpu.VMEM((BLOCK, width), F32),
        pltpu.VMEM((8, width), F32),
        pltpu.VMEM((8, width), F32),
    ]
    return inputs, outputs, shapes, scratch


def back(extents, vectors, x, saved, states, back_mid, packed):
    tokens, width = x.shape
    tiles = tokens // ROWS
    inputs, outputs, shapes, scratch = back_specs(tokens, width, packed, lambda i: tiles - 1 - i)
    return pl.pallas_call(
        back_kernel,
        name="back",
        grid=(tiles,),
        in_specs=inputs,
        out_specs=outputs,
        out_shape=shapes,
        scratch_shapes=scratch,
        compiler_params=pltpu.CompilerParams(vmem_limit_bytes=56 * MIB),
    )(extents, vectors, x, x, *saved, states, back_mid, packed)


def reduce(extents, vectors, x, saved, states, back_mid, packed, acts, sums_two, square):
    tokens, width = x.shape
    tiles, depth = tokens // ROWS, packed.shape[-2]
    inputs, outputs, shapes, scratch = back_specs(
        tokens, width, packed, lambda i: tiles - 1 - jnp.clip(i - FIRST_TILE, 0, tiles - 1)
    )
    stream, mixed, sums_one = shapes
    anywhere = pl.BlockSpec(memory_space=pl.ANY)
    z, y, x_size, c = GRID
    dma = pltpu.SemaphoreType.DMA
    small = (SMALL_ROWS, width)
    return pl.pallas_call(
        reduce_kernel,
        name="reduce",
        grid=(UNITS + LAGS[3],),
        in_specs=inputs + [whole(sums_two.shape), whole(square.shape), anywhere],
        out_specs=[outputs[0], anywhere, kept((UNITS, depth, width)), kept(small)],
        out_shape=[
            stream,
            mixed,
            jax.ShapeDtypeStruct((UNITS, depth, width), F32),
            jax.ShapeDtypeStruct(small, F32),
        ],
        scratch_shapes=scratch
        + [
            pltpu.VMEM((2, 6, ROWS, width), LOW),
            pltpu.VMEM(sums_one.shape, F32),
            pltpu.VMEM((2, tokens, width), LOW),
            pltpu.VMEM((2, tokens, width), LOW),
            pltpu.VMEM((5, *small), F32),
            pltpu.VMEM((5, *small), F32),
            dma((2,)),
            dma((2,)),
            dma((2,)),
            dma((5,)),
            dma((5,)),
            pltpu.VMEM((SLOTS, c, z, y, x_size, depth, width), LOW),
            pltpu.VMEM((SLOTS, z, y, x_size, depth, width), LOW),
            pltpu.VMEM((UNITS, z // 2, depth, width), LOW),
            pltpu.VMEM((UNITS, z // 2, depth, width), LOW),
            pltpu.VMEM((UNITS, z, depth, width), LOW),
            pltpu.VMEM((UNITS, z, depth, width), LOW),
            pltpu.VMEM((SLOTS, z, depth, width), F32),
            pltpu.VMEM((SLOTS, z, depth, width), LOW),
            pltpu.VMEM((UNITS, z - 1, depth, width), LOW),
            pltpu.VMEM((z - 1, z, depth, width), LOW),
            dma((SLOTS, 8)),
            dma((UNITS, 8)),
            dma((z - 1,)),
        ],
        compiler_params=pltpu.CompilerParams(vmem_limit_bytes=63 * MIB, collective_id=1, has_side_effects=True),
    )(extents, vectors, x, x, *saved, states, back_mid, packed, sums_two, square, acts)


def small_grads(vectors, sums_one, sums_two, square):
    width = vectors.shape[1]
    one = [jnp.sum(sums_one[8 * i : 8 * i + 8, :], axis=0, keepdims=True) for i in range(7)]
    two = [jnp.sum(sums_two[8 * i : 8 * i + 8, :], axis=0, keepdims=True) for i in range(6)]
    decay = one[4] * jnp.exp(vec(vectors, FADING))
    lane = rows_of((1, width), 1)
    squares = jnp.zeros((1, width), F32)
    for place_of, total in enumerate((two[4], jnp.sum(square[...], axis=0, keepdims=True), two[5])):
        squares = jnp.where(lane == place_of, jnp.sum(total, axis=1, keepdims=True), squares)
    rows = [one[0], one[1], one[2], decay, one[3], two[0], two[1], one[5], one[6], two[2], two[3], squares]
    return jnp.concatenate(rows + [jnp.zeros((SMALL_ROWS - len(rows), width), F32)], axis=0)


def pack(weights):
    *square, w1, w2 = weights
    depth, width = square[0].shape[-2:]
    parts = list(square)
    parts += [w1[..., j * width : (j + 1) * width] for j in range(4)]
    parts += [w2[..., j * depth : (j + 1) * depth, :] for j in range(4)]
    return jnp.stack(parts)


SMALL = (0, 1, 2, 3, 4, 9, 10, 14, 15, 16, 17)
LARGE = (5, 6, 7, 8, 13, 11, 12)


def finish(outcome, stream, large, small, squares, entries):
    shards = [None] * 18
    for row, i in enumerate(SMALL):
        shards[i] = small[row]
    for grad, i in zip(large, LARGE):
        shards[i] = grad
    return (outcome, stream, *shards, jnp.sqrt(squares / entries))


def body_any(residual_input, extents, *rest):
    parameters, upstream = rest[:18], rest[18]
    devices = lax.axis_size(AXES)
    held = jnp.stack([parameters[i] for i in SMALL])
    width = held.shape[1] * devices
    vectors = lax.all_gather(held, AXES, axis=1, tiled=True).astype(F32)
    vectors = jnp.pad(vectors, ((0, SMALL_ROWS - len(SMALL)), (0, 0)))
    blocks = 1
    for size in GRID:
        blocks *= size
    weights = [lax.all_gather(parameters[i], AXES, axis=0, tiled=True) for i in LARGE]
    packed = pack([w.reshape(blocks, -1, w.shape[1]) for w in weights])
    packed = packed.reshape(UNITS, *GRID, *packed.shape[2:])
    *saved, blend, mid, states, square = front(extents, vectors, residual_input, packed)
    outcome, back_mid, acts, sums_two = feed(extents, vectors, mid, upstream, blend, packed)
    stream, mixed, sums_one = back(extents, vectors, residual_input, saved, states, back_mid, packed)
    small = small_grads(vectors, sums_one, sums_two, square)
    grads = [dot_tn(mixed[i], mixed[3 + i]) for i in range(3)] + [dot_tn(acts[6], acts[13]), dot_tn(acts[5], acts[12])]
    grads.append(jnp.concatenate([dot_tn(acts[0], acts[7 + j]) for j in range(4)], axis=1))
    grads.append(jnp.concatenate([dot_tn(acts[1 + j], acts[11]) for j in range(4)], axis=0))
    squares = lax.psum(small[len(SMALL), :3], AXES)
    small = lax.psum_scatter(small[: len(SMALL)], AXES, scatter_dimension=1, tiled=True)
    large = [lax.psum_scatter(grad, AXES, scatter_dimension=0, tiled=True) for grad in grads]
    return finish(outcome, stream, large, small, squares, residual_input.shape[0] * width * devices)


def body(residual_input, extents, *rest):
    parameters, upstream = rest[:18], rest[18]
    devices = lax.axis_size(AXES)
    width = residual_input.shape[1]
    share = width // devices
    small = jnp.stack([parameters[i] for i in SMALL])
    small = jnp.pad(small, ((0, SMALL_ROWS - len(SMALL)), (0, 128 - share)))
    shards = [parameters[i] for i in LARGE]
    shards[6] = shards[6].reshape(4, share, width)
    packed, vectors, *saved, blend, mid, states, square = gather_front(extents, small, shards, residual_input)
    outcome, back_mid, acts, sums_two = feed(extents, vectors, mid, upstream, blend, packed)
    stream, _, total, small = reduce(
        extents, vectors, residual_input, saved, states, back_mid, packed, acts, sums_two, square
    )
    mine = lax.axis_index(AXES)
    squares = small[len(SMALL), :3]
    small = lax.dynamic_slice(small, (0, mine * share), (len(SMALL), share))
    large = [total[10], total[11], total[12], total[9], total[8]]
    large.append(jnp.concatenate([total[j] for j in range(4)], axis=1))
    large.append(total[4:8].reshape(4 * share, width))
    return finish(outcome, stream, large, small, squares, residual_input.shape[0] * width * devices)


def solution(mesh):
    rows, vector = P(AXES, None), P(AXES)
    kinds = [vector] * 5 + [rows] * 4 + [vector] * 2 + [rows] * 3 + [vector] * 4
    sizes = (mesh.shape["wide"], mesh.shape["narrow"])
    return jax.shard_map(
        body if sizes == (GRID[0] * GRID[1], GRID[2] * GRID[3]) else body_any,
        mesh=mesh,
        in_specs=(rows, rows, *kinds, rows),
        out_specs=(rows, rows, *kinds, P()),
        check_vma=False,
    )
```

```python
import functools

import jax
import jax.numpy as jnp
from jax import lax
from jax.experimental import pallas as pl
from jax.experimental.pallas import tpu as pltpu
from jax.sharding import PartitionSpec as P

F32 = jnp.float32
LOW = jnp.bfloat16
AXES = ("wide", "narrow")
BLOCK = 128
EDGE = 8
MIB = 2**20

(KEY_MIX, VALUE_MIX, GATE_MIX, FADING, REWARD, FEED_MIX, GATING_MIX, GAIN_ONE, BIAS_ONE, GAIN_TWO, BIAS_TWO) = range(11)
VECTORS = 16


def dot(left, right):
    return jnp.dot(left, right, preferred_element_type=F32)


def dot_nt(left, right):
    return lax.dot_general(left, right, (((1,), (1,)), ((), ())), preferred_element_type=F32)


def dot_tn(left, right):
    return lax.dot_general(left, right, (((0,), (0,)), ((), ())), preferred_element_type=F32)


def offsets_of(extents):
    offsets, total = [], 0
    for j in range(extents.shape[1] - 1):
        total = total + extents[0, j]
        offsets.append(total)
    return offsets


def start_of(places, offsets):
    begun = jnp.zeros_like(places)
    for offset in offsets:
        begun = jnp.where(places >= offset, offset, begun)
    return begun


def normed(x):
    centered = x - jnp.mean(x, axis=1, keepdims=True)
    scale = lax.rsqrt(jnp.mean(centered * centered, axis=1, keepdims=True) + 1e-05)
    return centered * scale, scale


def fold(x):
    return jnp.sum(x.reshape(x.shape[0] // 8, 8, x.shape[1]), axis=0)


def rows_of(shape, axis=0):
    return lax.broadcasted_iota(jnp.int32, shape, axis)


def shift_down(x, first, keep):
    return jnp.where(rows_of((x.shape[0], 1)) == 0, first, pltpu.roll(x, 1, 0)) * keep


def shift_up(x, last):
    rows = x.shape[0]
    return jnp.where(rows_of((rows, 1)) == rows - 1, last, pltpu.roll(x, rows - 1, 0))


def split(top, bottom):
    both = jnp.concatenate([top, bottom], axis=1)
    high = both.astype(LOW)
    low = (both - high.astype(F32)).astype(LOW)
    return jnp.concatenate([high, low], axis=0)


def norm_grad(back_normed, hat, scale, gain):
    back_hat = back_normed * gain
    return scale * (
        back_hat
        - jnp.mean(back_hat, axis=1, keepdims=True)
        - hat * jnp.mean(back_hat * hat, axis=1, keepdims=True)
    )


def vec(vectors, row):
    return vectors[row : row + 1, :]


def matrix(ref):
    return ref[...].reshape(-1, ref.shape[-1])


def front_tile(
    tile, extents, vectors, x_ref, wk, wv, wr, wo,
    k_out, v_out, s_out, y_out, d_out, blend_out, mid_out, state_out, square_out,
    grow, shrink, last, state,
):
    rows, width = x_ref.shape
    half = BLOCK // 2
    offsets = offsets_of(extents)
    rate = jnp.exp(vec(vectors, FADING))

    @pl.when(tile == 0)
    def _():
        local = rows_of((BLOCK + EDGE, 1)).astype(F32)
        shrink[...] = jnp.exp((half - local) * rate)
        grow[...] = jnp.exp((local[:BLOCK] + (1 - half)) * rate)
        last[...] = jnp.zeros_like(last)
        state[...] = jnp.zeros_like(state)
        square_out[...] = jnp.zeros_like(square_out)

    x = x_ref[...].astype(F32)
    hat, _ = normed(x)
    norm = hat * vec(vectors, GAIN_ONE) + vec(vectors, BIAS_ONE)
    places = tile * rows + rows_of((rows, 1))
    keep = (places != start_of(places, offsets)).astype(F32)
    before = shift_down(norm, last[0:1, :], keep)
    last[0:1, :] = norm[rows - 1 : rows, :]

    def mixed(row):
        mix = vec(vectors, row)
        return (norm * mix + before * (1.0 - mix)).astype(LOW)

    keys = dot(mixed(KEY_MIX), matrix(wk))
    values = dot(mixed(VALUE_MIX), matrix(wv))
    sig = jax.nn.sigmoid(dot(mixed(GATE_MIX), matrix(wr)))
    k_out[...] = keys
    v_out[...] = values
    s_out[...] = sig
    fade_half = jnp.exp(-half * rate)
    reward = vec(vectors, REWARD)
    for block in range(rows // BLOCK):
        here = slice(block * BLOCK, (block + 1) * BLOCK)
        key, value = keys[here], values[here]
        weight = grow[...] * jnp.exp(key)
        first = tile * rows + block * BLOCK
        after = first + rows_of((BLOCK + EDGE, 1))
        column = rows_of((1, 2 * BLOCK), 1)
        source = first + jnp.where(column >= BLOCK, column - BLOCK, column)
        begun = start_of(after, offsets)
        paired = ((source < after) & (source >= begun)).astype(LOW)
        sums = dot(paired, split(weight * value, weight))
        inherit = (begun < first).astype(F32)
        top = shrink[...] * (sums[:, :width] + inherit * (fade_half * state[0:1, :]))
        bottom = shrink[...] * (sums[:, width:] + inherit * (fade_half * state[1:2, :]))
        state[0:1, :] = top[BLOCK : BLOCK + 1]
        state[1:2, :] = bottom[BLOCK : BLOCK + 1]
        state_out[block, :, :] = state[...]
        own = jnp.exp(reward + key)
        inverse = 1.0 / (bottom[:BLOCK] + own)
        wkv = (top[:BLOCK] + own * value) * inverse
        y_out[here, :] = wkv
        d_out[here, :] = inverse
        blend_out[here, :] = (sig[here] * wkv).astype(LOW)
    attended = dot(blend_out[...], matrix(wo))
    mid_out[...] = x + attended
    square_out[...] += fold(attended * attended)


def front_kernel(extents, vectors, x_ref, weights, *rest):
    front_tile(pl.program_id(0), extents, vectors, x_ref, *[weights.at[u] for u in range(4)], *rest)


def feed_kernel(
    extents, vectors, mid_ref, edge_ref, up_ref, blend_ref, packed,
    out_out, back_out, acts, sums_out,
    lift, carry, wg, w1, w2, load,
):
    step = pl.program_id(0)
    tile = pl.num_programs(0) - 1 - step
    rows, width = mid_ref.shape
    hidden = lift.shape[1]
    offsets = offsets_of(extents)

    @pl.when(step == 0)
    def _():
        copies = [(packed.at[4], wg), (packed.at[5:9], w1)]
        copies += [(packed.at[9 + j], w2.at[:, :, :, :, j]) for j in range(4)]
        copies = [pltpu.make_async_copy(a, b, load.at[i]) for i, (a, b) in enumerate(copies)]
        for copy in copies:
            copy.start()
        for copy in copies:
            copy.wait()
        carry[...] = jnp.zeros_like(carry)
        sums_out[...] = jnp.zeros_like(sums_out)

    gain, bias = vec(vectors, GAIN_TWO), vec(vectors, BIAS_TWO)
    mid = mid_ref[...]
    hat, scale = normed(mid)
    norm = hat * gain + bias
    edge_hat, _ = normed(edge_ref[...])
    edge = (edge_hat * gain + bias)[EDGE - 1 : EDGE]
    places = tile * rows + rows_of((rows, 1))
    keep = (places != start_of(places, offsets)).astype(F32)
    before = shift_down(norm, edge, keep)
    mix_k, mix_g = vec(vectors, FEED_MIX), vec(vectors, GATING_MIX)
    feed_key = (norm * mix_k + before * (1.0 - mix_k)).astype(LOW)
    feed_gate = (norm * mix_g + before * (1.0 - mix_g)).astype(LOW)
    acts[0] = feed_key
    acts[5] = feed_gate
    acts[6] = blend_ref[...]
    lowered = None
    for j in range(hidden // width):
        chunk = slice(j * width, (j + 1) * width)
        lifted = jnp.maximum(dot(feed_key, matrix(w1.at[j])), 0.0)
        lift[:, chunk] = lifted
        squared = (lifted * lifted).astype(LOW)
        acts[1 + j] = squared
        part = dot(squared, matrix(w2.at[j]))
        lowered = part if lowered is None else lowered + part
    sig = jax.nn.sigmoid(dot(feed_gate, matrix(wg)))
    feed_out = sig * lowered
    result = mid + feed_out
    out_out[...] = result.astype(LOW)
    upstream = up_ref[...].astype(F32)
    back_lowered = (upstream * sig).astype(LOW)
    back_gate = (upstream * lowered * sig * (1.0 - sig)).astype(LOW)
    acts[11] = back_lowered
    acts[12] = back_gate
    back_key = None
    for j in range(hidden // width):
        chunk = slice(j * width, (j + 1) * width)
        back_lifted = (2.0 * lift[:, chunk] * dot_nt(back_lowered, matrix(w2.at[j]))).astype(LOW)
        acts[7 + j] = back_lifted
        part = dot_nt(back_lifted, matrix(w1.at[j]))
        back_key = part if back_key is None else back_key + part
    back_gating = dot_nt(back_gate, matrix(wg))
    late = norm - before
    back_before = keep * (back_key * (1.0 - mix_k) + back_gating * (1.0 - mix_g))
    back_norm = back_key * mix_k + back_gating * mix_g + shift_up(back_before, carry[0:1, :])
    carry[0:1, :] = back_before[0:1]
    back_mid = upstream + norm_grad(back_norm, hat, scale, gain)
    back_out[...] = back_mid
    acts[13] = back_mid.astype(LOW)
    for row, piece in enumerate(
        (back_key * late, back_gating * late, back_norm * hat, back_norm, result * result, feed_out * feed_out)
    ):
        sums_out[8 * row : 8 * row + 8, :] += fold(piece)


def back_tile(
    tile, begins, extents, vectors, x_ref, edge_ref, k_ref, v_ref, s_ref, y_ref, d_ref, state_ref, mid_ref, weights,
    stream_out, acts, sums_out,
    grow, shrink, carry, state, between=(),
):
    rows, width = x_ref.shape
    half = BLOCK // 2
    offsets = offsets_of(extents)
    rate = jnp.exp(vec(vectors, FADING))

    @pl.when(begins)
    def _():
        local = rows_of((BLOCK + EDGE, 1)).astype(F32)
        shrink[...] = jnp.exp((half - local[:BLOCK]) * rate)
        grow[...] = jnp.exp((local + (1 - EDGE - half)) * rate)
        carry[...] = jnp.zeros_like(carry)
        state[...] = jnp.zeros_like(state)
        sums_out[...] = jnp.zeros_like(sums_out)

    between = iter(between)
    back_mid = mid_ref[...]
    back_attended = back_mid.astype(LOW)
    back_blend = dot_nt(back_attended, matrix(weights.at[3]))
    sig = s_ref[...]
    wkv = y_ref[...]
    acts[5] = (back_blend * wkv * sig * (1.0 - sig)).astype(LOW)
    back_top = back_blend * sig * d_ref[...]
    fade_half = jnp.exp(-half * rate)
    reward = vec(vectors, REWARD)
    for block in reversed(range(rows // BLOCK)):
        next(between, int)()
        here = slice(block * BLOCK, (block + 1) * BLOCK)
        key, value = k_ref[here, :], v_ref[here, :]
        first = tile * rows + block * BLOCK
        source = first - EDGE + rows_of((BLOCK + EDGE, 1))
        column = rows_of((1, 2 * BLOCK), 1)
        after = first + jnp.where(column >= BLOCK, column - BLOCK, column)
        paired = ((source < after) & (source >= start_of(after, offsets))).astype(LOW)
        bt = back_top[here]
        weighted = shrink[...] * bt
        sums = dot(paired, split(weighted, -weighted * wkv[here]))
        following = start_of(first + BLOCK + jnp.zeros((1, 1), jnp.int32), offsets)
        tail = (source >= following).astype(F32)
        top = grow[...] * (sums[:, :width] + tail * (fade_half * state[0:1, :]))
        bottom = grow[...] * (sums[:, width:] + tail * (fade_half * state[1:2, :]))
        next(between, int)()
        crossing = state_ref[block, :, :] * state[...]
        sums_out[32:40, :] += jnp.where(rows_of((8, 1)) < 2, crossing * (-1.0 * BLOCK), 0.0)
        state[0:1, :] = top[EDGE - 1 : EDGE]
        state[1:2, :] = bottom[EDGE - 1 : EDGE]
        weight = jnp.exp(key)
        own = jnp.exp(reward + key) * bt
        passed = weight * (value * top[EDGE:] + bottom[EDGE:])
        bonus = own * (value - wkv[here])
        back_key = passed + bonus
        acts[3, here, :] = back_key.astype(LOW)
        acts[4, here, :] = (weight * top[EDGE:] + own).astype(LOW)
        local = rows_of((BLOCK, 1)).astype(F32)
        sums_out[24:32, :] += fold(bonus)
        sums_out[32:40, :] += fold(local * back_key + passed)

    gain, bias = vec(vectors, GAIN_ONE), vec(vectors, BIAS_ONE)
    hat, scale = normed(x_ref[...].astype(F32))
    norm = hat * gain + bias
    edge_hat, _ = normed(edge_ref[...].astype(F32))
    edge = (edge_hat * gain + bias)[edge_ref.shape[0] - 1 : edge_ref.shape[0]]
    places = tile * rows + rows_of((rows, 1))
    keep = (places != start_of(places, offsets)).astype(F32)
    before = shift_down(norm, edge, keep)
    late = norm - before
    back_norm, back_before = None, None
    for number, mix_row in enumerate((KEY_MIX, VALUE_MIX, GATE_MIX)):
        next(between, int)()
        mix = vec(vectors, mix_row)
        acts[number] = (norm * mix + before * (1.0 - mix)).astype(LOW)
        back_mixed = dot_nt(acts[3 + number], matrix(weights.at[number]))
        sums_out[8 * number : 8 * number + 8, :] += fold(back_mixed * late)
        one, two = back_mixed * mix, back_mixed * (1.0 - mix)
        back_norm = one if back_norm is None else back_norm + one
        back_before = two if back_before is None else back_before + two
    back_before = back_before * keep
    back_norm = back_norm + shift_up(back_before, carry[0:1, :])
    carry[0:1, :] = back_before[0:1]
    sums_out[40:48, :] += fold(back_norm * hat)
    sums_out[48:56, :] += fold(back_norm)
    stream_out[...] = (back_mid + norm_grad(back_norm, hat, scale, gain)).astype(LOW)


def back_kernel(*refs):
    step = pl.program_id(0)
    back_tile(pl.num_programs(0) - 1 - step, step == 0, *refs)


MESH = pl.DeviceIdType.MESH
GRID = (4, 2, 2, 2)
SMALL_ROWS = 16
HOPS = 13


def place():
    wide, narrow = lax.axis_index("wide"), lax.axis_index("narrow")
    return wide // 2, wide % 2, narrow // 2, narrow % 2


def device(z, y, x, c):
    return (z * 2 + y, x * 2 + c)


def greet():
    z, y, x, c = place()
    others = [(z, y, x, 1 - c), (z, y, 1 - x, c), (z, 1 - y, x, c)]
    others += [(lax.rem(z + k, GRID[0]), y, x, c) for k in range(1, GRID[0])]
    barrier = pltpu.get_barrier_semaphore()
    for other in others:
        pl.semaphore_signal(barrier, inc=1, device_id=device(*other), device_id_type=MESH)
    pl.semaphore_wait(barrier, len(others))


class Gather:
    def __init__(self, own, held, send, receive):
        self.own, self.held, self.send, self.receive = own, held, send, receive
        self.z, self.y, self.x, self.c = place()

    def copy(self, number, source, target, to):
        return pltpu.make_async_remote_copy(
            src_ref=source,
            dst_ref=target,
            send_sem=self.send.at[number],
            recv_sem=self.receive.at[number],
            device_id=device(*to),
            device_id_type=MESH,
        )

    def along(self, k, mine):
        z = self.z if mine else lax.rem(self.z + GRID[0] - k, GRID[0])
        view = self.held.at[z, self.y, self.x, self.c]
        return self.copy(k - 1, self.own, view, (lax.rem(self.z + k, GRID[0]), self.y, self.x, self.c))

    def hop(self, number, mine):
        z, y, x, c = self.z, self.y, self.x, self.c
        if number < 3:
            return self.along(number + 1, mine)
        partner = (z + 1 - 2 * lax.rem(z, 2), y, x, c)
        everything = slice(None)
        one = lax.rem(z, 2)
        two = one + 2
        core = (z, y, x, 1 - c)
        sent = (
            ((everything, y, x, c), (z, y, 1 - x, c)),
            ((everything, y, x, c), (z, 1 - y, x, c)),
            ((one, y, 1 - x, c), (z, 1 - y, x, c)),
            ((two, 1 - y, x, c), (z, y, 1 - x, c)),
            ((everything, y, x, c), core),
            ((everything, y, 1 - x, c), core),
            ((everything, 1 - y, x, c), core),
            ((everything, 1 - y, 1 - x, c), core),
            ((one, 1 - y, 1 - x, c), partner),
            ((two, 1 - y, 1 - x, c), partner),
        )
        landing = (
            (everything, y, 1 - x, c),
            (everything, 1 - y, x, c),
            (one, 1 - y, 1 - x, c),
            (two, 1 - y, 1 - x, c),
            (everything, y, x, 1 - c),
            (everything, y, 1 - x, 1 - c),
            (everything, 1 - y, x, 1 - c),
            (everything, 1 - y, 1 - x, 1 - c),
            (1 - one, 1 - y, 1 - x, c),
            (3 - one, 1 - y, 1 - x, c),
        )
        source, to = sent[number - 3]
        view = self.held.at[source if mine else landing[number - 3]]
        return self.copy(number, view, view, to)

    def start(self, *numbers):
        for number in numbers:
            self.hop(number, True).start()

    def arrived(self, *numbers):
        for number in numbers:
            self.hop(number, False).wait_recv()

    def sent(self):
        for number in range(HOPS):
            self.hop(number, True).wait_send()


def gather_kernel(
    tiles, extents, small, wk, wv, wr, wo, wg, w1, w2, x_ref,
    held, vectors, k_out, v_out, s_out, y_out, d_out, blend_out, mid_out, state_out, square_out,
    small_held, own, weights, grow, shrink, last, state, own_sem, load_sem, send, receive, small_send, small_receive,
):
    tick = pl.program_id(0)
    z, y, x, c = place()
    units = held.shape[0]
    width = x_ref.shape[1]
    first_tile = 8

    def unit(u):
        return Gather(own.at[u], held.at[u], send.at[lax.rem(u, 9)], receive.at[u])

    def small_unit():
        return Gather(small, small_held, small_send, small_receive)

    def keep(u):
        return pltpu.make_async_copy(own.at[u], held.at[u, z, y, x, c], own_sem.at[u])

    def load(u):
        return pltpu.make_async_copy(held.at[u], weights.at[u], load_sem.at[u])

    @pl.when(tick == 0)
    def _():
        for u, ref in enumerate((wk, wv, wr, wo, wg)):
            own[u] = ref[...]
        for j in range(4):
            own[5 + j] = w1[:, j * width : (j + 1) * width]
            own[9 + j] = w2[j]
        small_held[z, y, x, c] = small[...]
        for u in range(units):
            keep(u).start()
        greet()
        small_unit().start(0, 1, 2)
        unit(0).start(0, 1, 2)
        unit(1).start(0, 1, 2)

    @pl.when(tick < units)
    def _():
        keep(tick).wait()
        unit(tick).arrived(0, 1, 2)
        unit(tick).start(3, 4, 7)

    @pl.when(tick + 2 < units)
    def _():
        unit(tick + 2).start(0, 1, 2)

    @pl.when(tick == 0)
    def _():
        small_unit().arrived(0, 1, 2)
        small_unit().start(3, 4, 7)

    @pl.when(jnp.logical_and(tick >= 1, tick < units + 1))
    def _():
        unit(tick - 1).arrived(3, 4)
        unit(tick - 1).start(5, 6, 8, 9)

    @pl.when(tick == 1)
    def _():
        small_unit().arrived(3, 4)
        small_unit().start(5, 6, 8, 9)

    def diagonal(u):
        unit(u).arrived(5, 6)
        unit(u).start(11, 12)

    def partners(u):
        unit(u).arrived(11, 12)
        unit(u).start(10)

    def complete(u):
        unit(u).arrived(7, 8, 9, 10)
        unit(u).sent()

    def within(u, first, end):
        return jnp.logical_and(u >= first, u < end)

    pl.when(within(tick - 2, 0, 4))(lambda: diagonal(tick - 2))
    pl.when(within(tick - 3, 4, units))(lambda: diagonal(tick - 3))

    @pl.when(tick == 2)
    def _():
        small_unit().arrived(5, 6)
        small_unit().start(11, 12)

    pl.when(within(tick - 3, 0, 4))(lambda: partners(tick - 3))
    pl.when(within(tick - 5, 4, units))(lambda: partners(tick - 5))

    @pl.when(tick == 3)
    def _():
        small_unit().arrived(11, 12)
        small_unit().start(10)

    pl.when(within(tick - 4, 0, 4))(lambda: complete(tick - 4))
    pl.when(within(tick - 6, 4, units))(lambda: complete(tick - 6))

    @pl.when(jnp.logical_and(tick >= 4, tick < 8))
    def _():
        load(tick - 4).start()

    @pl.when(tick == first_tile)
    def _():
        for u in range(4):
            load(u).wait()

    @pl.when(tick == 4)
    def _():
        small_unit().arrived(7, 8, 9, 10)
        small_unit().sent()
        share = width // (GRID[0] * 8)
        total = jnp.zeros((SMALL_ROWS, width), F32)
        empty = jnp.zeros((SMALL_ROWS, width - 128), F32)
        for number in range(GRID[0] * 8):
            block = small_held[number // 8, number // 4 % 2, number // 2 % 2, number % 2].astype(F32)
            total += pltpu.roll(jnp.concatenate([block, empty], axis=1), number * share, 1)
        vectors[...] = total

    @pl.when(jnp.logical_and(tick >= first_tile, tick < first_tile + tiles))
    def _():
        front_tile(
            tick - first_tile, extents, vectors, x_ref, *[weights.at[u] for u in range(4)],
            k_out, v_out, s_out, y_out, d_out, blend_out, mid_out, state_out, square_out,
            grow, shrink, last, state,
        )


class Reduce:
    def __init__(self, out, mine, pairs, sides_x, sides_y, blocks_x, blocks_y, kept_sum, going, coming,
                 turned_in, send, receive, turned_receive):
        self.out = out
        self.mine, self.pairs, self.sides_x, self.sides_y = mine, pairs, sides_x, sides_y
        self.blocks_x, self.blocks_y, self.kept_sum, self.going, self.coming = blocks_x, blocks_y, kept_sum, going, coming
        self.send, self.receive, self.turned_in, self.turned_receive = send, receive, turned_in, turned_receive
        z, y, x, c = place()
        self.z, self.y, self.x, self.c = z, y, x, c
        self.core, self.over_x, self.over_y = (z, y, x, 1 - c), (z, y, 1 - x, c), (z, 1 - y, x, c)
        part = GRID[0] // 2
        self.low, self.high = pl.ds(0, part), pl.ds(part, part)

    def slot(self, u):
        return lax.rem(u, SLOTS)

    def remote(self, u, number, source, target, to, receive=None):
        return pltpu.make_async_remote_copy(
            src_ref=source,
            dst_ref=target,
            send_sem=self.send.at[self.slot(u), number],
            recv_sem=self.receive.at[u, number] if receive is None else receive,
            device_id=device(*to),
            device_id_type=MESH,
        )

    def pair(self, u):
        return self.remote(u, 0, self.mine.at[self.slot(u), 1 - self.c], self.pairs.at[self.slot(u)], self.core)

    def sides(self, u):
        held = self.mine.at[self.slot(u), self.c]
        y, x = 1 - self.y, 1 - self.x
        return (
            self.remote(u, 1, held.at[self.low, y, x], self.sides_x.at[u], self.over_x),
            self.remote(u, 2, held.at[self.high, y, x], self.sides_y.at[u], self.over_y),
        )

    def blocks(self, u):
        held = self.mine.at[self.slot(u), self.c]
        return (
            self.remote(u, 3, held.at[:, self.y, 1 - self.x], self.blocks_x.at[u], self.over_x),
            self.remote(u, 4, held.at[:, 1 - self.y, self.x], self.blocks_y.at[u], self.over_y),
        )

    def ends(self, u):
        found = []
        for k in range(1, GRID[0]):
            to = lax.rem(self.z + k, GRID[0])
            going = self.going.at[self.slot(u), to]
            found.append(self.remote(u, 4 + k, going, self.coming.at[u, k - 1], (to, self.y, self.x, self.c)))
        return found

    def turned_end(self, u, k):
        to = u - TURNED[0]
        return self.remote(
            u, 5, self.going.at[self.slot(u)], self.turned_in.at[k - 1], (to, self.y, self.x, self.c),
            self.turned_receive.at[k - 1],
        )

    def is_turned(self, u):
        return jnp.logical_and(u >= TURNED[0], u < TURNED[1])

    def pieces(self, u, left, right):
        slot, depth = self.slot(u), self.out.shape[-2]
        z, y, x, c = GRID
        turned = jnp.logical_and(u >= TURNED[0], u < TURNED[1]).astype(jnp.int32)

        def piece(part, columns):
            many = left.shape[-1] // PIECES[0]
            wide = right.shape[-1] // PIECES[1]
            lanes = slice(columns * wide, (columns + 1) * wide)
            grad = dot_tn(left[:, part * many : (part + 1) * many], right[:, lanes]).astype(LOW)
            blocks = grad.reshape(many // depth, depth, grad.shape[1])
            for number in range(many // depth):
                b = part * (many // depth) + number
                even = (b % c, b // (x * y * c), b // (x * c) % y, b // c % x)
                other = (b // z % c, b % z, b // (z * c * x), b // (z * c) % x)
                where = [i + turned * (j - i) for i, j in zip(even, other)]
                self.mine[slot, where[0], where[1], where[2], where[3], :, lanes] = blocks[number]

        return [functools.partial(piece, i, j) for i in range(PIECES[0]) for j in range(PIECES[1])]

    def stage(self, tick, lag, work):
        pl.when(jnp.logical_and(tick >= lag, tick < lag + UNITS))(functools.partial(work, tick - lag))

    def add_pair(self, u):
        slot, c = self.slot(u), self.c
        self.pair(u).wait()
        self.mine[slot, c] = (self.mine[slot, c].astype(F32) + self.pairs[slot].astype(F32)).astype(LOW)
        for copy in self.sides(u):
            copy.start()

    def add_sides(self, u):
        for copy in self.sides(u):
            copy.wait()
        held = self.mine.at[self.slot(u), self.c]
        low, high, y, x = self.low, self.high, self.y, self.x
        held[low, 1 - y, x] = (held[low, 1 - y, x].astype(F32) + self.sides_x[u].astype(F32)).astype(LOW)
        held[high, y, 1 - x] = (held[high, y, 1 - x].astype(F32) + self.sides_y[u].astype(F32)).astype(LOW)
        for copy in self.blocks(u):
            copy.start()

    def add_blocks(self, u):
        slot = self.slot(u)
        for copy in self.blocks(u):
            copy.wait()
        total = self.mine[slot, self.c, :, self.y, self.x].astype(F32)
        total = total + self.blocks_x[u].astype(F32) + self.blocks_y[u].astype(F32)
        self.kept_sum[slot] = total
        self.going[slot] = total.astype(LOW)

        def even():
            for copy in self.ends(u):
                copy.start()

        pl.when(jnp.logical_not(self.is_turned(u)))(even)
        for k in range(1, GRID[0]):
            away = lax.rem(self.z + 2 * GRID[0] - jnp.minimum(u, 2 * GRID[0]), GRID[0]) == k
            pl.when(jnp.logical_and(self.is_turned(u), away))(lambda k=k: self.turned_end(u, k).start())

    def add_ends(self, u):
        slot = self.slot(u)

        def even():
            for copy in self.ends(u):
                copy.wait()
            total = self.kept_sum[slot, self.z]
            for k in range(GRID[0] - 1):
                total += self.coming[u, k].astype(F32)
            self.out[u] = total

        def turned_here():
            total = self.kept_sum[slot]
            for k in range(1, GRID[0]):
                self.turned_end(u, k).wait_recv()
                total += self.turned_in[k - 1].astype(F32)
            self.out[TURNED[0] : TURNED[1]] = total

        pl.when(jnp.logical_not(self.is_turned(u)))(even)
        ahead = lax.rem(self.z + 2 * GRID[0] - jnp.minimum(u, 2 * GRID[0]), GRID[0])
        pl.when(jnp.logical_and(self.is_turned(u), ahead == 0))(turned_here)
        for k in range(1, GRID[0]):
            pl.when(jnp.logical_and(self.is_turned(u), ahead == k))(lambda k=k: self.turned_end(u, k).wait_send())


def reduce_kernel(
    extents, vectors, x_ref, edge_ref, k_ref, v_ref, s_ref, y_ref, d_ref, state_ref, mid_ref, weights,
    sums_two, square, acts,
    stream_out, mixed, out, small_out,
    grow, shrink, carry, state, staged, sums_one, lefts, rights, sums, small_in,
    stage_sem, left_sem, right_sem, small_send, small_receive, *refs,
):
    tick = pl.program_id(0)
    z, y, x, c = place()
    rows = x_ref.shape[0]
    tiles = mixed.shape[1] // rows
    job = Reduce(out, *refs)
    partners = (
        (z, y, x, 1 - c),
        (z, y, 1 - x, c),
        (z, 1 - y, x, c),
        (z + 1 - 2 * lax.rem(z, 2), y, x, c),
        (lax.rem(z + 2, GRID[0]), y, x, c),
    )

    def exchange(step):
        return pltpu.make_async_remote_copy(
            src_ref=sums.at[step],
            dst_ref=small_in.at[step],
            send_sem=small_send.at[step],
            recv_sem=small_receive.at[step],
            device_id=device(*partners[step]),
            device_id_type=MESH,
        )

    def left_of(u):
        return lax.rem(jnp.maximum(u - 3, 0), 2)

    def right_of(u):
        return lax.rem(jnp.minimum(u, 4) + jnp.maximum(u - 7, 0), 2)

    def fetch_left(u, late):
        source = mixed.at[u - FIRST_UNITS] if late else acts.at[jnp.maximum(u - 3, 0)]
        return pltpu.make_async_copy(source, lefts.at[left_of(u)], left_sem.at[left_of(u)])

    def fetch_right(u, late):
        if late:
            source = mixed.at[u - FIRST_UNITS + 3]
        else:
            source = acts.at[7 + jnp.minimum(u, 4) + jnp.maximum(u - 7, 0)]
        return pltpu.make_async_copy(source, rights.at[right_of(u)], right_sem.at[right_of(u)])

    def fetches(u, work):
        early, late = u < FIRST_UNITS, jnp.logical_and(u >= FIRST_UNITS, u < UNITS)
        pl.when(jnp.logical_and(early, jnp.logical_or(u == 0, u >= 4)))(lambda: work(fetch_left(u, False)))
        pl.when(jnp.logical_and(early, jnp.logical_or(u <= 4, u >= 8)))(lambda: work(fetch_right(u, False)))
        pl.when(late)(lambda: work(fetch_left(u, True)))
        pl.when(late)(lambda: work(fetch_right(u, True)))

    def keep(number):
        two = lax.rem(number, 2)
        where = pl.ds(pl.multiple_of((tiles - 1 - number) * rows, rows), rows)
        return pltpu.make_async_copy(staged.at[two], mixed.at[:, where], stage_sem.at[two])

    def start(copy):
        copy.start()

    def wait(copy):
        copy.wait()

    @pl.when(tick == 0)
    def _():
        fetches(tick, start)
        greet()

    number = tick - FIRST_TILE
    pl.when(jnp.logical_and(number >= 2, number < tiles + 1))(lambda: keep(number - 2).wait())
    pl.when(number == tiles)(lambda: keep(number - 1).wait())
    fetches(tick + 1, start)
    fetches(tick, wait)

    inputs = (extents, vectors, x_ref, edge_ref, k_ref, v_ref, s_ref, y_ref, d_ref, state_ref, mid_ref, weights)

    def pieces():
        return job.pieces(tick, lefts.at[left_of(tick)], rights.at[right_of(tick)])

    busy = jnp.logical_and(number >= 0, number < tiles)

    @pl.when(busy)
    def _():
        back_tile(
            tiles - 1 - number, number == 0, *inputs, stream_out, staged.at[lax.rem(number, 2)], sums_one,
            grow, shrink, carry, state, between=pieces(),
        )
        keep(number).start()
        job.pair(tick).start()

    @pl.when(jnp.logical_and(jnp.logical_not(busy), tick < UNITS))
    def _():
        for piece in pieces():
            piece()
        job.pair(tick).start()

    for lag, work in zip(LAGS, (job.add_pair, job.add_sides, job.add_blocks, job.add_ends)):
        job.stage(tick, lag, work)

    @pl.when(number == tiles)
    def _():
        sums[0] = small_grads(vectors, sums_one, sums_two, square)
        exchange(0).start()

    for step in range(1, 6):

        @pl.when(number == tiles + step)
        def _():
            exchange(step - 1).wait()
            total = sums[step - 1] + small_in[step - 1]
            if step == 5:
                small_out[...] = total
            else:
                sums[step] = total
                exchange(step).start()


def whole(shape):
    return pl.BlockSpec(shape, lambda i: (0,) * len(shape), pipeline_mode=pl.Buffered(1))


def kept(shape):
    return pl.BlockSpec(shape, lambda i: (0,) * len(shape))


def smem():
    return pl.BlockSpec(memory_space=pltpu.SMEM)


ROWS = 256
UNITS = 13
SLOTS = 6
LAGS = (1, 2, 3, 6)
PIECES = (2, 1)
FIRST_UNITS = 10
FIRST_TILE = 1
TURNED = (4, 8)
FEED_ACTS = 14


def four(packed):
    return pl.BlockSpec((4, *packed.shape[1:]), lambda i: (0,) * len(packed.shape), pipeline_mode=pl.Buffered(1))


def front_shapes(tokens, width):
    wide = jax.ShapeDtypeStruct((tokens, width), F32)
    low = jax.ShapeDtypeStruct((tokens, width), LOW)
    states = jax.ShapeDtypeStruct((tokens // BLOCK, 8, width), F32)
    return [wide] * 5 + [low, wide, states, jax.ShapeDtypeStruct((8, width), F32)]


def front_specs(width, index):
    tile = pl.BlockSpec((ROWS, width), lambda i: (index(i), 0))
    states = pl.BlockSpec((ROWS // BLOCK, 8, width), lambda i: (index(i), 0, 0))
    return [tile] * 7 + [states, kept((8, width))]


def front_scratch(width):
    return [
        pltpu.VMEM((BLOCK, width), F32),
        pltpu.VMEM((BLOCK + EDGE, width), F32),
        pltpu.VMEM((8, width), F32),
        pltpu.VMEM((8, width), F32),
    ]


def front(extents, vectors, x, packed):
    tokens, width = x.shape
    return pl.pallas_call(
        front_kernel,
        name="front",
        grid=(tokens // ROWS,),
        in_specs=[smem(), whole(vectors.shape), pl.BlockSpec((ROWS, width), lambda i: (i, 0)), four(packed)],
        out_specs=front_specs(width, lambda i: i),
        out_shape=front_shapes(tokens, width),
        scratch_shapes=front_scratch(width),
        compiler_params=pltpu.CompilerParams(vmem_limit_bytes=56 * MIB),
    )(extents, vectors, x, packed)


def gather_front(extents, small, shards, x):
    tokens, width = x.shape
    tiles = tokens // ROWS
    depth = shards[0].shape[0]
    anywhere = pl.BlockSpec(memory_space=pl.ANY)

    def index(i):
        return jnp.clip(i - 8, 0, tiles - 1)

    dma = pltpu.SemaphoreType.DMA
    return pl.pallas_call(
        functools.partial(gather_kernel, tiles),
        name="gather_front",
        grid=(max(UNITS + 6, tiles + 8),),
        in_specs=[smem()]
        + [whole(part.shape) for part in (small, *shards)]
        + [pl.BlockSpec((ROWS, width), lambda i: (index(i), 0))],
        out_specs=[anywhere, kept((SMALL_ROWS, width))] + front_specs(width, index),
        out_shape=[
            jax.ShapeDtypeStruct((UNITS, *GRID, depth, width), LOW),
            jax.ShapeDtypeStruct((SMALL_ROWS, width), F32),
        ]
        + front_shapes(tokens, width),
        scratch_shapes=[
            pltpu.VMEM((*GRID, *small.shape), LOW),
            pltpu.VMEM((UNITS, depth, width), LOW),
            pltpu.VMEM((4, *GRID, depth, width), LOW),
        ]
        + front_scratch(width)
        + [dma((UNITS,)), dma((4,)), dma((9, HOPS)), dma((UNITS, HOPS)), dma((HOPS,)), dma((HOPS,))],
        compiler_params=pltpu.CompilerParams(vmem_limit_bytes=56 * MIB, collective_id=0, has_side_effects=True),
    )(extents, small, *shards, x)


def feed(extents, vectors, mid, upstream, blend, packed):
    tokens, width = mid.shape
    hidden = 4 * width
    rows, tiles = ROWS, tokens // ROWS
    tile = pl.BlockSpec((rows, width), lambda i: (tiles - 1 - i, 0))
    edge = pl.BlockSpec((EDGE, width), lambda i: (jnp.maximum((tiles - 1 - i) * (rows // EDGE) - 1, 0), 0))
    block = packed.shape[1:]
    return pl.pallas_call(
        feed_kernel,
        name="feed",
        grid=(tiles,),
        in_specs=[smem(), whole(vectors.shape), tile, edge, tile, tile, pl.BlockSpec(memory_space=pl.ANY)],
        out_specs=[
            tile,
            tile,
            pl.BlockSpec((FEED_ACTS, rows, width), lambda i: (0, tiles - 1 - i, 0)),
            kept((48, width)),
        ],
        out_shape=[
            jax.ShapeDtypeStruct((tokens, width), LOW),
            jax.ShapeDtypeStruct((tokens, width), F32),
            jax.ShapeDtypeStruct((FEED_ACTS, tokens, width), LOW),
            jax.ShapeDtypeStruct((48, width), F32),
        ],
        scratch_shapes=[
            pltpu.VMEM((rows, hidden), F32),
            pltpu.VMEM((8, width), F32),
            pltpu.VMEM(block, LOW),
            pltpu.VMEM((4, *block), LOW),
            pltpu.VMEM((*block[:4], 4, *block[4:]), LOW),
            pltpu.SemaphoreType.DMA((6,)),
        ],
        compiler_params=pltpu.CompilerParams(vmem_limit_bytes=60 * MIB),
    )(extents, vectors, mid, mid, upstream, blend, packed)


def back_specs(tokens, width, packed, index):
    blocks = ROWS // BLOCK
    tile = pl.BlockSpec((ROWS, width), lambda i: (index(i), 0))
    edge = pl.BlockSpec((16, width), lambda i: (jnp.maximum(index(i) * (ROWS // 16) - 1, 0), 0))
    states = pl.BlockSpec((blocks, 8, width), lambda i: (index(i), 0, 0))
    inputs = [smem(), whole((SMALL_ROWS, width)), tile, edge] + [tile] * 5 + [states, tile, four(packed)]
    outputs = [tile, pl.BlockSpec((6, ROWS, width), lambda i: (0, index(i), 0)), kept((56, width))]
    shapes = [
        jax.ShapeDtypeStruct((tokens, width), LOW),
        jax.ShapeDtypeStruct((6, tokens, width), LOW),
        jax.ShapeDtypeStruct((56, width), F32),
    ]
    scratch = [
        pltpu.VMEM((BLOCK + EDGE, width), F32),
        pltpu.VMEM((BLOCK, width), F32),
        pltpu.VMEM((8, width), F32),
        pltpu.VMEM((8, width), F32),
    ]
    return inputs, outputs, shapes, scratch


def back(extents, vectors, x, saved, states, back_mid, packed):
    tokens, width = x.shape
    tiles = tokens // ROWS
    inputs, outputs, shapes, scratch = back_specs(tokens, width, packed, lambda i: tiles - 1 - i)
    return pl.pallas_call(
        back_kernel,
        name="back",
        grid=(tiles,),
        in_specs=inputs,
        out_specs=outputs,
        out_shape=shapes,
        scratch_shapes=scratch,
        compiler_params=pltpu.CompilerParams(vmem_limit_bytes=56 * MIB),
    )(extents, vectors, x, x, *saved, states, back_mid, packed)


def reduce(extents, vectors, x, saved, states, back_mid, packed, acts, sums_two, square):
    tokens, width = x.shape
    tiles, depth = tokens // ROWS, packed.shape[-2]
    inputs, outputs, shapes, scratch = back_specs(
        tokens, width, packed, lambda i: tiles - 1 - jnp.clip(i - FIRST_TILE, 0, tiles - 1)
    )
    stream, mixed, sums_one = shapes
    anywhere = pl.BlockSpec(memory_space=pl.ANY)
    z, y, x_size, c = GRID
    dma = pltpu.SemaphoreType.DMA
    small = (SMALL_ROWS, width)
    return pl.pallas_call(
        reduce_kernel,
        name="reduce",
        grid=(UNITS + LAGS[3],),
        in_specs=inputs + [whole(sums_two.shape), whole(square.shape), anywhere],
        out_specs=[outputs[0], anywhere, kept((UNITS, depth, width)), kept(small)],
        out_shape=[
            stream,
            mixed,
            jax.ShapeDtypeStruct((UNITS, depth, width), F32),
            jax.ShapeDtypeStruct(small, F32),
        ],
        scratch_shapes=scratch
        + [
            pltpu.VMEM((2, 6, ROWS, width), LOW),
            pltpu.VMEM(sums_one.shape, F32),
            pltpu.VMEM((2, tokens, width), LOW),
            pltpu.VMEM((2, tokens, width), LOW),
            pltpu.VMEM((5, *small), F32),
            pltpu.VMEM((5, *small), F32),
            dma((2,)),
            dma((2,)),
            dma((2,)),
            dma((5,)),
            dma((5,)),
            pltpu.VMEM((SLOTS, c, z, y, x_size, depth, width), LOW),
            pltpu.VMEM((SLOTS, z, y, x_size, depth, width), LOW),
            pltpu.VMEM((UNITS, z // 2, depth, width), LOW),
            pltpu.VMEM((UNITS, z // 2, depth, width), LOW),
            pltpu.VMEM((UNITS, z, depth, width), LOW),
            pltpu.VMEM((UNITS, z, depth, width), LOW),
            pltpu.VMEM((SLOTS, z, depth, width), F32),
            pltpu.VMEM((SLOTS, z, depth, width), LOW),
            pltpu.VMEM((UNITS, z - 1, depth, width), LOW),
            pltpu.VMEM((z - 1, z, depth, width), LOW),
            dma((SLOTS, 8)),
            dma((UNITS, 8)),
            dma((z - 1,)),
        ],
        compiler_params=pltpu.CompilerParams(vmem_limit_bytes=63 * MIB, collective_id=1, has_side_effects=True),
    )(extents, vectors, x, x, *saved, states, back_mid, packed, sums_two, square, acts)


def finish_kernel(entries, share, stream_ref, total, small, stream_out, *outs):
    *squares, w1, w2, rms = outs[:8]
    lines = outs[8:]
    stream_out[...] = stream_ref[...]

    @pl.when(pl.program_id(0) == 0)
    def _():
        width = small.shape[1]
        for out, u in zip(squares, (10, 11, 12, 9, 8)):
            out[...] = total[u]
        for j in range(4):
            w1[:, j * width : (j + 1) * width] = total[j]
            w2[j] = total[4 + j]
        sums = small[...]
        rms[...] = jnp.sqrt(sums[len(SMALL), :3] / entries)
        mine = lax.axis_index("wide") * lax.axis_size("narrow") + lax.axis_index("narrow")
        turned = pltpu.roll(sums, lax.rem(width - mine * share, width), 1)
        for row, out in enumerate(lines):
            out[...] = turned[row, :share]


def finish_up(stream, total, small, entries):
    tokens, width = stream.shape
    depth = total.shape[1]
    parts = 4
    tile = pl.BlockSpec((tokens // parts, width), lambda i: (i, 0))
    shapes = [(depth, width)] * 5 + [(depth, 4 * width), (4, depth, width), (3,)] + [(depth,)] * len(SMALL)
    return pl.pallas_call(
        functools.partial(finish_kernel, entries, depth),
        name="finish_up",
        grid=(parts,),
        in_specs=[tile, whole(total.shape), whole(small.shape)],
        out_specs=[tile] + [kept(shape) for shape in shapes],
        out_shape=[jax.ShapeDtypeStruct(stream.shape, LOW)] + [jax.ShapeDtypeStruct(shape, F32) for shape in shapes],
        compiler_params=pltpu.CompilerParams(vmem_limit_bytes=60 * MIB),
    )(stream, total, small)


def small_grads(vectors, sums_one, sums_two, square):
    width = vectors.shape[1]
    one = [jnp.sum(sums_one[8 * i : 8 * i + 8, :], axis=0, keepdims=True) for i in range(7)]
    two = [jnp.sum(sums_two[8 * i : 8 * i + 8, :], axis=0, keepdims=True) for i in range(6)]
    decay = one[4] * jnp.exp(vec(vectors, FADING))
    lane = rows_of((1, width), 1)
    squares = jnp.zeros((1, width), F32)
    for place_of, total in enumerate((two[4], jnp.sum(square[...], axis=0, keepdims=True), two[5])):
        squares = jnp.where(lane == place_of, jnp.sum(total, axis=1, keepdims=True), squares)
    rows = [one[0], one[1], one[2], decay, one[3], two[0], two[1], one[5], one[6], two[2], two[3], squares]
    return jnp.concatenate(rows + [jnp.zeros((SMALL_ROWS - len(rows), width), F32)], axis=0)


def pack(weights):
    *square, w1, w2 = weights
    depth, width = square[0].shape[-2:]
    parts = list(square)
    parts += [w1[..., j * width : (j + 1) * width] for j in range(4)]
    parts += [w2[..., j * depth : (j + 1) * depth, :] for j in range(4)]
    return jnp.stack(parts)


SMALL = (0, 1, 2, 3, 4, 9, 10, 14, 15, 16, 17)
LARGE = (5, 6, 7, 8, 13, 11, 12)


def finish(outcome, stream, large, small, squares, entries):
    shards = [None] * 18
    for row, i in enumerate(SMALL):
        shards[i] = small[row]
    for grad, i in zip(large, LARGE):
        shards[i] = grad
    return (outcome, stream, *shards, jnp.sqrt(squares / entries))


def body_any(residual_input, extents, *rest):
    parameters, upstream = rest[:18], rest[18]
    devices = lax.axis_size(AXES)
    held = jnp.stack([parameters[i] for i in SMALL])
    width = held.shape[1] * devices
    vectors = lax.all_gather(held, AXES, axis=1, tiled=True).astype(F32)
    vectors = jnp.pad(vectors, ((0, SMALL_ROWS - len(SMALL)), (0, 0)))
    blocks = 1
    for size in GRID:
        blocks *= size
    weights = [lax.all_gather(parameters[i], AXES, axis=0, tiled=True) for i in LARGE]
    packed = pack([w.reshape(blocks, -1, w.shape[1]) for w in weights])
    packed = packed.reshape(UNITS, *GRID, *packed.shape[2:])
    *saved, blend, mid, states, square = front(extents, vectors, residual_input, packed)
    outcome, back_mid, acts, sums_two = feed(extents, vectors, mid, upstream, blend, packed)
    stream, mixed, sums_one = back(extents, vectors, residual_input, saved, states, back_mid, packed)
    small = small_grads(vectors, sums_one, sums_two, square)
    grads = [dot_tn(mixed[i], mixed[3 + i]) for i in range(3)] + [dot_tn(acts[6], acts[13]), dot_tn(acts[5], acts[12])]
    grads.append(jnp.concatenate([dot_tn(acts[0], acts[7 + j]) for j in range(4)], axis=1))
    grads.append(jnp.concatenate([dot_tn(acts[1 + j], acts[11]) for j in range(4)], axis=0))
    squares = lax.psum(small[len(SMALL), :3], AXES)
    small = lax.psum_scatter(small[: len(SMALL)], AXES, scatter_dimension=1, tiled=True)
    large = [lax.psum_scatter(grad, AXES, scatter_dimension=0, tiled=True) for grad in grads]
    return finish(outcome, stream, large, small, squares, residual_input.shape[0] * width * devices)


def body(residual_input, extents, *rest):
    parameters, upstream = rest[:18], rest[18]
    devices = lax.axis_size(AXES)
    width = residual_input.shape[1]
    share = width // devices
    small = jnp.stack([parameters[i] for i in SMALL])
    small = jnp.pad(small, ((0, SMALL_ROWS - len(SMALL)), (0, 128 - share)))
    shards = [parameters[i] for i in LARGE]
    shards[6] = shards[6].reshape(4, share, width)
    packed, vectors, *saved, blend, mid, states, square = gather_front(extents, small, shards, residual_input)
    outcome, back_mid, acts, sums_two = feed(extents, vectors, mid, upstream, blend, packed)
    stream, _, total, small = reduce(
        extents, vectors, residual_input, saved, states, back_mid, packed, acts, sums_two, square
    )
    stream, *rest = finish_up(stream, total, small, residual_input.shape[0] * width * devices)
    large, rms, lines = rest[:7], rest[7], rest[8:]
    large[6] = large[6].reshape(4 * share, width)
    shards = [None] * 18
    for line, i in zip(lines, SMALL):
        shards[i] = line
    for grad, i in zip(large, LARGE):
        shards[i] = grad
    return (outcome, stream, *shards, rms)


def solution(mesh):
    rows, vector = P(AXES, None), P(AXES)
    kinds = [vector] * 5 + [rows] * 4 + [vector] * 2 + [rows] * 3 + [vector] * 4
    sizes = (mesh.shape["wide"], mesh.shape["narrow"])
    return jax.shard_map(
        body if sizes == (GRID[0] * GRID[1], GRID[2] * GRID[3]) else body_any,
        mesh=mesh,
        in_specs=(rows, rows, *kinds, rows),
        out_specs=(rows, rows, *kinds, P()),
        check_vma=False,
    )
```

```python
import functools

import jax
import jax.numpy as jnp
from jax import lax
from jax.experimental import pallas as pl
from jax.experimental.pallas import tpu as pltpu
from jax.sharding import PartitionSpec as P

F32 = jnp.float32
LOW = jnp.bfloat16
AXES = ("wide", "narrow")
BLOCK = 128
EDGE = 8
MIB = 2**20

(KEY_MIX, VALUE_MIX, GATE_MIX, FADING, REWARD, FEED_MIX, GATING_MIX, GAIN_ONE, BIAS_ONE, GAIN_TWO, BIAS_TWO) = range(11)
VECTORS = 16


def dot(left, right):
    return jnp.dot(left, right, preferred_element_type=F32)


def dot_nt(left, right):
    return lax.dot_general(left, right, (((1,), (1,)), ((), ())), preferred_element_type=F32)


def dot_tn(left, right):
    return lax.dot_general(left, right, (((0,), (0,)), ((), ())), preferred_element_type=F32)


def offsets_of(extents):
    offsets, total = [], 0
    for j in range(extents.shape[1] - 1):
        total = total + extents[0, j]
        offsets.append(total)
    return offsets


def start_of(places, offsets):
    begun = jnp.zeros_like(places)
    for offset in offsets:
        begun = jnp.where(places >= offset, offset, begun)
    return begun


def normed(x):
    centered = x - jnp.mean(x, axis=1, keepdims=True)
    scale = lax.rsqrt(jnp.mean(centered * centered, axis=1, keepdims=True) + 1e-05)
    return centered * scale, scale


def fold(x):
    return jnp.sum(x.reshape(x.shape[0] // 8, 8, x.shape[1]), axis=0)


def rows_of(shape, axis=0):
    return lax.broadcasted_iota(jnp.int32, shape, axis)


def shift_down(x, first, keep):
    return jnp.where(rows_of((x.shape[0], 1)) == 0, first, pltpu.roll(x, 1, 0)) * keep


def shift_up(x, last):
    rows = x.shape[0]
    return jnp.where(rows_of((rows, 1)) == rows - 1, last, pltpu.roll(x, rows - 1, 0))


def split(top, bottom):
    both = jnp.concatenate([top, bottom], axis=1)
    high = both.astype(LOW)
    low = (both - high.astype(F32)).astype(LOW)
    return jnp.concatenate([high, low], axis=0)


def norm_grad(back_normed, hat, scale, gain):
    back_hat = back_normed * gain
    return scale * (
        back_hat
        - jnp.mean(back_hat, axis=1, keepdims=True)
        - hat * jnp.mean(back_hat * hat, axis=1, keepdims=True)
    )


def vec(vectors, row):
    return vectors[row : row + 1, :]


def matrix(ref):
    return ref[...].reshape(-1, ref.shape[-1])


def front_tile(
    tile, extents, vectors, x_ref, wk, wv, wr, wo,
    k_out, v_out, s_out, y_out, d_out, blend_out, mid_out, state_out, square_out,
    grow, shrink, last, state,
):
    rows, width = x_ref.shape
    half = BLOCK // 2
    offsets = offsets_of(extents)
    rate = jnp.exp(vec(vectors, FADING))

    @pl.when(tile == 0)
    def _():
        local = rows_of((BLOCK + EDGE, 1)).astype(F32)
        shrink[...] = jnp.exp((half - local) * rate)
        grow[...] = jnp.exp((local[:BLOCK] + (1 - half)) * rate)
        last[...] = jnp.zeros_like(last)
        state[...] = jnp.zeros_like(state)
        square_out[...] = jnp.zeros_like(square_out)

    x = x_ref[...].astype(F32)
    hat, _ = normed(x)
    norm = hat * vec(vectors, GAIN_ONE) + vec(vectors, BIAS_ONE)
    places = tile * rows + rows_of((rows, 1))
    keep = (places != start_of(places, offsets)).astype(F32)
    before = shift_down(norm, last[0:1, :], keep)
    last[0:1, :] = norm[rows - 1 : rows, :]

    def mixed(row):
        mix = vec(vectors, row)
        return (norm * mix + before * (1.0 - mix)).astype(LOW)

    keys = dot(mixed(KEY_MIX), matrix(wk))
    values = dot(mixed(VALUE_MIX), matrix(wv))
    sig = jax.nn.sigmoid(dot(mixed(GATE_MIX), matrix(wr)))
    k_out[...] = keys
    v_out[...] = values
    s_out[...] = sig
    fade_half = jnp.exp(-half * rate)
    reward = vec(vectors, REWARD)
    for block in range(rows // BLOCK):
        here = slice(block * BLOCK, (block + 1) * BLOCK)
        key, value = keys[here], values[here]
        weight = grow[...] * jnp.exp(key)
        first = tile * rows + block * BLOCK
        after = first + rows_of((BLOCK + EDGE, 1))
        column = rows_of((1, 2 * BLOCK), 1)
        source = first + jnp.where(column >= BLOCK, column - BLOCK, column)
        begun = start_of(after, offsets)
        paired = ((source < after) & (source >= begun)).astype(LOW)
        sums = dot(paired, split(weight * value, weight))
        inherit = (begun < first).astype(F32)
        top = shrink[...] * (sums[:, :width] + inherit * (fade_half * state[0:1, :]))
        bottom = shrink[...] * (sums[:, width:] + inherit * (fade_half * state[1:2, :]))
        state[0:1, :] = top[BLOCK : BLOCK + 1]
        state[1:2, :] = bottom[BLOCK : BLOCK + 1]
        state_out[block, :, :] = state[...]
        own = jnp.exp(reward + key)
        inverse = 1.0 / (bottom[:BLOCK] + own)
        wkv = (top[:BLOCK] + own * value) * inverse
        y_out[here, :] = wkv
        d_out[here, :] = inverse
        blend_out[here, :] = (sig[here] * wkv).astype(LOW)
    attended = dot(blend_out[...], matrix(wo))
    mid_out[...] = x + attended
    square_out[...] += fold(attended * attended)


def front_kernel(extents, vectors, x_ref, weights, *rest):
    front_tile(pl.program_id(0), extents, vectors, x_ref, *[weights.at[u] for u in range(4)], *rest)


def feed_kernel(
    extents, vectors, mid_ref, edge_ref, up_ref, blend_ref, packed,
    out_out, back_out, acts, sums_out,
    lift, carry, wg, w1, w2, load,
):
    step = pl.program_id(0)
    tile = pl.num_programs(0) - 1 - step
    rows, width = mid_ref.shape
    hidden = lift.shape[1]
    offsets = offsets_of(extents)

    @pl.when(step == 0)
    def _():
        copies = [(packed.at[4], wg), (packed.at[5:9], w1)]
        copies += [(packed.at[9 + j], w2.at[:, :, :, :, j]) for j in range(4)]
        copies = [pltpu.make_async_copy(a, b, load.at[i]) for i, (a, b) in enumerate(copies)]
        for copy in copies:
            copy.start()
        for copy in copies:
            copy.wait()
        carry[...] = jnp.zeros_like(carry)
        sums_out[...] = jnp.zeros_like(sums_out)

    gain, bias = vec(vectors, GAIN_TWO), vec(vectors, BIAS_TWO)
    mid = mid_ref[...]
    hat, scale = normed(mid)
    norm = hat * gain + bias
    edge_hat, _ = normed(edge_ref[...])
    edge = (edge_hat * gain + bias)[EDGE - 1 : EDGE]
    places = tile * rows + rows_of((rows, 1))
    keep = (places != start_of(places, offsets)).astype(F32)
    before = shift_down(norm, edge, keep)
    mix_k, mix_g = vec(vectors, FEED_MIX), vec(vectors, GATING_MIX)
    feed_key = (norm * mix_k + before * (1.0 - mix_k)).astype(LOW)
    feed_gate = (norm * mix_g + before * (1.0 - mix_g)).astype(LOW)
    acts[0] = feed_key
    acts[5] = feed_gate
    acts[6] = blend_ref[...]
    lowered = None
    for j in range(hidden // width):
        chunk = slice(j * width, (j + 1) * width)
        lifted = jnp.maximum(dot(feed_key, matrix(w1.at[j])), 0.0)
        lift[:, chunk] = lifted
        squared = (lifted * lifted).astype(LOW)
        acts[1 + j] = squared
        part = dot(squared, matrix(w2.at[j]))
        lowered = part if lowered is None else lowered + part
    sig = jax.nn.sigmoid(dot(feed_gate, matrix(wg)))
    feed_out = sig * lowered
    result = mid + feed_out
    out_out[...] = result.astype(LOW)
    upstream = up_ref[...].astype(F32)
    back_lowered = (upstream * sig).astype(LOW)
    back_gate = (upstream * lowered * sig * (1.0 - sig)).astype(LOW)
    acts[11] = back_lowered
    acts[12] = back_gate
    back_key = None
    for j in range(hidden // width):
        chunk = slice(j * width, (j + 1) * width)
        back_lifted = (2.0 * lift[:, chunk] * dot_nt(back_lowered, matrix(w2.at[j]))).astype(LOW)
        acts[7 + j] = back_lifted
        part = dot_nt(back_lifted, matrix(w1.at[j]))
        back_key = part if back_key is None else back_key + part
    back_gating = dot_nt(back_gate, matrix(wg))
    late = norm - before
    back_before = keep * (back_key * (1.0 - mix_k) + back_gating * (1.0 - mix_g))
    back_norm = back_key * mix_k + back_gating * mix_g + shift_up(back_before, carry[0:1, :])
    carry[0:1, :] = back_before[0:1]
    back_mid = upstream + norm_grad(back_norm, hat, scale, gain)
    back_out[...] = back_mid
    acts[13] = back_mid.astype(LOW)
    for row, piece in enumerate(
        (back_key * late, back_gating * late, back_norm * hat, back_norm, result * result, feed_out * feed_out)
    ):
        sums_out[8 * row : 8 * row + 8, :] += fold(piece)


def back_tile(
    tile, begins, extents, vectors, x_ref, edge_ref, k_ref, v_ref, s_ref, y_ref, d_ref, state_ref, mid_ref, weights,
    stream_out, acts, sums_out,
    grow, shrink, carry, state, between=(),
):
    rows, width = x_ref.shape
    half = BLOCK // 2
    offsets = offsets_of(extents)
    rate = jnp.exp(vec(vectors, FADING))

    @pl.when(begins)
    def _():
        local = rows_of((BLOCK + EDGE, 1)).astype(F32)
        shrink[...] = jnp.exp((half - local[:BLOCK]) * rate)
        grow[...] = jnp.exp((local + (1 - EDGE - half)) * rate)
        carry[...] = jnp.zeros_like(carry)
        state[...] = jnp.zeros_like(state)
        sums_out[...] = jnp.zeros_like(sums_out)

    between = iter(between)
    back_mid = mid_ref[...]
    back_attended = back_mid.astype(LOW)
    back_blend = dot_nt(back_attended, matrix(weights.at[3]))
    sig = s_ref[...]
    wkv = y_ref[...]
    acts[5] = (back_blend * wkv * sig * (1.0 - sig)).astype(LOW)
    back_top = back_blend * sig * d_ref[...]
    fade_half = jnp.exp(-half * rate)
    reward = vec(vectors, REWARD)
    for block in reversed(range(rows // BLOCK)):
        next(between, int)()
        here = slice(block * BLOCK, (block + 1) * BLOCK)
        key, value = k_ref[here, :], v_ref[here, :]
        first = tile * rows + block * BLOCK
        source = first - EDGE + rows_of((BLOCK + EDGE, 1))
        column = rows_of((1, 2 * BLOCK), 1)
        after = first + jnp.where(column >= BLOCK, column - BLOCK, column)
        paired = ((source < after) & (source >= start_of(after, offsets))).astype(LOW)
        bt = back_top[here]
        weighted = shrink[...] * bt
        sums = dot(paired, split(weighted, -weighted * wkv[here]))
        following = start_of(first + BLOCK + jnp.zeros((1, 1), jnp.int32), offsets)
        tail = (source >= following).astype(F32)
        top = grow[...] * (sums[:, :width] + tail * (fade_half * state[0:1, :]))
        bottom = grow[...] * (sums[:, width:] + tail * (fade_half * state[1:2, :]))
        next(between, int)()
        crossing = state_ref[block, :, :] * state[...]
        sums_out[32:40, :] += jnp.where(rows_of((8, 1)) < 2, crossing * (-1.0 * BLOCK), 0.0)
        state[0:1, :] = top[EDGE - 1 : EDGE]
        state[1:2, :] = bottom[EDGE - 1 : EDGE]
        weight = jnp.exp(key)
        own = jnp.exp(reward + key) * bt
        passed = weight * (value * top[EDGE:] + bottom[EDGE:])
        bonus = own * (value - wkv[here])
        back_key = passed + bonus
        acts[3, here, :] = back_key.astype(LOW)
        acts[4, here, :] = (weight * top[EDGE:] + own).astype(LOW)
        local = rows_of((BLOCK, 1)).astype(F32)
        sums_out[24:32, :] += fold(bonus)
        sums_out[32:40, :] += fold(local * back_key + passed)

    gain, bias = vec(vectors, GAIN_ONE), vec(vectors, BIAS_ONE)
    hat, scale = normed(x_ref[...].astype(F32))
    norm = hat * gain + bias
    edge_hat, _ = normed(edge_ref[...].astype(F32))
    edge = (edge_hat * gain + bias)[edge_ref.shape[0] - 1 : edge_ref.shape[0]]
    places = tile * rows + rows_of((rows, 1))
    keep = (places != start_of(places, offsets)).astype(F32)
    before = shift_down(norm, edge, keep)
    late = norm - before
    back_norm, back_before = None, None
    for number, mix_row in enumerate((KEY_MIX, VALUE_MIX, GATE_MIX)):
        next(between, int)()
        mix = vec(vectors, mix_row)
        acts[number] = (norm * mix + before * (1.0 - mix)).astype(LOW)
        back_mixed = dot_nt(acts[3 + number], matrix(weights.at[number]))
        sums_out[8 * number : 8 * number + 8, :] += fold(back_mixed * late)
        one, two = back_mixed * mix, back_mixed * (1.0 - mix)
        back_norm = one if back_norm is None else back_norm + one
        back_before = two if back_before is None else back_before + two
    back_before = back_before * keep
    back_norm = back_norm + shift_up(back_before, carry[0:1, :])
    carry[0:1, :] = back_before[0:1]
    sums_out[40:48, :] += fold(back_norm * hat)
    sums_out[48:56, :] += fold(back_norm)
    stream_out[...] = (back_mid + norm_grad(back_norm, hat, scale, gain)).astype(LOW)


def back_kernel(*refs):
    step = pl.program_id(0)
    back_tile(pl.num_programs(0) - 1 - step, step == 0, *refs)


MESH = pl.DeviceIdType.MESH
GRID = (4, 2, 2, 2)
SMALL_ROWS = 16
HOPS = 13
LATE = 11


def place():
    wide, narrow = lax.axis_index("wide"), lax.axis_index("narrow")
    return wide // 2, wide % 2, narrow // 2, narrow % 2


def device(z, y, x, c):
    return (z * 2 + y, x * 2 + c)


def greet():
    z, y, x, c = place()
    others = [(z, y, x, 1 - c), (z, y, 1 - x, c), (z, 1 - y, x, c)]
    others += [(lax.rem(z + k, GRID[0]), y, x, c) for k in range(1, GRID[0])]
    barrier = pltpu.get_barrier_semaphore()
    for other in others:
        pl.semaphore_signal(barrier, inc=1, device_id=device(*other), device_id_type=MESH)
    pl.semaphore_wait(barrier, len(others))


class Gather:
    def __init__(self, own, held, send, receive):
        self.own, self.held, self.send, self.receive = own, held, send, receive
        self.z, self.y, self.x, self.c = place()

    def copy(self, number, source, target, to):
        return pltpu.make_async_remote_copy(
            src_ref=source,
            dst_ref=target,
            send_sem=self.send.at[number],
            recv_sem=self.receive.at[number],
            device_id=device(*to),
            device_id_type=MESH,
        )

    def along(self, k, mine):
        z = self.z if mine else lax.rem(self.z + GRID[0] - k, GRID[0])
        view = self.held.at[z, self.y, self.x, self.c]
        return self.copy(k - 1, self.own, view, (lax.rem(self.z + k, GRID[0]), self.y, self.x, self.c))

    def hop(self, number, mine):
        z, y, x, c = self.z, self.y, self.x, self.c
        if number < 3:
            return self.along(number + 1, mine)
        partner = (z + 1 - 2 * lax.rem(z, 2), y, x, c)
        everything = slice(None)
        one = lax.rem(z, 2)
        two = one + 2
        core = (z, y, x, 1 - c)
        sent = (
            ((everything, y, x, c), (z, y, 1 - x, c)),
            ((everything, y, x, c), (z, 1 - y, x, c)),
            ((one, y, 1 - x, c), (z, 1 - y, x, c)),
            ((two, 1 - y, x, c), (z, y, 1 - x, c)),
            ((everything, y, x, c), core),
            ((everything, y, 1 - x, c), core),
            ((everything, 1 - y, x, c), core),
            ((everything, 1 - y, 1 - x, c), core),
            ((one, 1 - y, 1 - x, c), partner),
            ((two, 1 - y, 1 - x, c), partner),
        )
        landing = (
            (everything, y, 1 - x, c),
            (everything, 1 - y, x, c),
            (one, 1 - y, 1 - x, c),
            (two, 1 - y, 1 - x, c),
            (everything, y, x, 1 - c),
            (everything, y, 1 - x, 1 - c),
            (everything, 1 - y, x, 1 - c),
            (everything, 1 - y, 1 - x, 1 - c),
            (1 - one, 1 - y, 1 - x, c),
            (3 - one, 1 - y, 1 - x, c),
        )
        source, to = sent[number - 3]
        view = self.held.at[source if mine else landing[number - 3]]
        return self.copy(number, view, view, to)

    def start(self, *numbers):
        for number in numbers:
            self.hop(number, True).start()

    def arrived(self, *numbers):
        for number in numbers:
            self.hop(number, False).wait_recv()

    def sent(self):
        for number in range(HOPS):
            self.hop(number, True).wait_send()


def gather_kernel(
    tiles, extents, wk, wv, wr, wo, wg, w1, w2, x_ref, *refs
):
    lines, refs = refs[: len(SMALL)], refs[len(SMALL) :]
    gather_steps(tiles, lines, extents, wk, wv, wr, wo, wg, w1, w2, x_ref, *refs)


def gather_steps(
    tiles, lines, extents, wk, wv, wr, wo, wg, w1, w2, x_ref,
    held, vectors, k_out, v_out, s_out, y_out, d_out, blend_out, mid_out, state_out, square_out,
    small, small_held, own, weights, grow, shrink, last, state, own_sem, load_sem, send, receive, small_send, small_receive,
):
    tick = pl.program_id(0)
    z, y, x, c = place()
    units = held.shape[0]
    width = x_ref.shape[1]
    first_tile = 8

    def unit(u):
        return Gather(own.at[u], held.at[u], send.at[lax.rem(u, 9)], receive.at[u])

    def small_unit():
        return Gather(small, small_held, small_send, small_receive)

    def keep(u):
        return pltpu.make_async_copy(own.at[u], held.at[u, z, y, x, c], own_sem.at[u])

    def load(u):
        return pltpu.make_async_copy(held.at[u], weights.at[u], load_sem.at[u])

    @pl.when(tick == 0)
    def _():
        small[...] = jnp.zeros_like(small)
        for row, line in enumerate(lines):
            small[row, : line.shape[0]] = line[...].astype(F32)
        for u, ref in enumerate((wk, wv, wr, wo, wg)):
            own[u] = ref[...]
        for j in range(4):
            own[5 + j] = w1[:, j * width : (j + 1) * width]
            own[9 + j] = w2[j]
        small_held[z, y, x, c] = small[...]
        for u in range(units):
            keep(u).start()
        greet()
        small_unit().start(0, 1, 2)
        unit(0).start(0, 1, 2)
        unit(1).start(0, 1, 2)

    @pl.when(tick < units)
    def _():
        keep(tick).wait()
        unit(tick).arrived(0, 1, 2)
        unit(tick).start(3, 4, 7)

    @pl.when(tick + 2 < units)
    def _():
        unit(tick + 2).start(0, 1, 2)

    @pl.when(tick == 0)
    def _():
        small_unit().arrived(0, 1, 2)
        small_unit().start(3, 4, 7)

    @pl.when(jnp.logical_and(tick >= 1, tick < units + 1))
    def _():
        unit(tick - 1).arrived(3, 4)
        unit(tick - 1).start(5, 6, 8, 9)

    @pl.when(tick == 1)
    def _():
        small_unit().arrived(3, 4)
        small_unit().start(5, 6, 8, 9)

    def diagonal(u):
        unit(u).arrived(5, 6)
        unit(u).start(11, 12)

    def partners(u):
        unit(u).arrived(11, 12)
        unit(u).start(10)

    def complete(u):
        unit(u).arrived(7, 8, 9, 10)
        unit(u).sent()

    def within(u, first, end):
        return jnp.logical_and(u >= first, u < end)

    pl.when(jnp.logical_or(within(tick - 2, 0, 4), within(tick - 2, LATE, units)))(lambda: diagonal(tick - 2))
    pl.when(within(tick - 3, 4, LATE))(lambda: diagonal(tick - 3))

    @pl.when(tick == 2)
    def _():
        small_unit().arrived(5, 6)
        small_unit().start(11, 12)

    pl.when(jnp.logical_or(within(tick - 3, 0, 4), within(tick - 3, LATE, units)))(lambda: partners(tick - 3))
    pl.when(within(tick - 5, 4, LATE))(lambda: partners(tick - 5))

    @pl.when(tick == 3)
    def _():
        small_unit().arrived(11, 12)
        small_unit().start(10)

    pl.when(jnp.logical_or(within(tick - 4, 0, 4), within(tick - 4, LATE, units)))(lambda: complete(tick - 4))
    pl.when(within(tick - 6, 4, LATE))(lambda: complete(tick - 6))

    @pl.when(jnp.logical_and(tick >= 4, tick < 8))
    def _():
        load(tick - 4).start()

    @pl.when(tick == first_tile)
    def _():
        for u in range(4):
            load(u).wait()

    @pl.when(tick == 4)
    def _():
        small_unit().arrived(7, 8, 9, 10)
        small_unit().sent()
        share = width // (GRID[0] * 8)
        total = jnp.zeros((SMALL_ROWS, width), F32)
        empty = jnp.zeros((SMALL_ROWS, width - 128), F32)
        for number in range(GRID[0] * 8):
            block = small_held[number // 8, number // 4 % 2, number // 2 % 2, number % 2]
            total += pltpu.roll(jnp.concatenate([block, empty], axis=1), number * share, 1)
        vectors[...] = total

    @pl.when(jnp.logical_and(tick >= first_tile, tick < first_tile + tiles))
    def _():
        front_tile(
            tick - first_tile, extents, vectors, x_ref, *[weights.at[u] for u in range(4)],
            k_out, v_out, s_out, y_out, d_out, blend_out, mid_out, state_out, square_out,
            grow, shrink, last, state,
        )


class Reduce:
    def __init__(self, out, mine, pairs, sides_x, sides_y, blocks_x, blocks_y, kept_sum, going, coming,
                 turned_in, send, receive, turned_receive):
        self.out = out
        self.mine, self.pairs, self.sides_x, self.sides_y = mine, pairs, sides_x, sides_y
        self.blocks_x, self.blocks_y, self.kept_sum, self.going, self.coming = blocks_x, blocks_y, kept_sum, going, coming
        self.send, self.receive, self.turned_in, self.turned_receive = send, receive, turned_in, turned_receive
        z, y, x, c = place()
        self.z, self.y, self.x, self.c = z, y, x, c
        self.core, self.over_x, self.over_y = (z, y, x, 1 - c), (z, y, 1 - x, c), (z, 1 - y, x, c)
        part = GRID[0] // 2
        self.low, self.high = pl.ds(0, part), pl.ds(part, part)

    def slot(self, u):
        return lax.rem(u, SLOTS)

    def remote(self, u, number, source, target, to, receive=None):
        return pltpu.make_async_remote_copy(
            src_ref=source,
            dst_ref=target,
            send_sem=self.send.at[self.slot(u), number],
            recv_sem=self.receive.at[u, number] if receive is None else receive,
            device_id=device(*to),
            device_id_type=MESH,
        )

    def pair(self, u):
        return self.remote(u, 0, self.mine.at[self.slot(u), 1 - self.c], self.pairs.at[self.slot(u)], self.core)

    def sides(self, u):
        held = self.mine.at[self.slot(u), self.c]
        y, x = 1 - self.y, 1 - self.x
        return (
            self.remote(u, 1, held.at[self.low, y, x], self.sides_x.at[u], self.over_x),
            self.remote(u, 2, held.at[self.high, y, x], self.sides_y.at[u], self.over_y),
        )

    def blocks(self, u):
        held = self.mine.at[self.slot(u), self.c]
        return (
            self.remote(u, 3, held.at[:, self.y, 1 - self.x], self.blocks_x.at[u], self.over_x),
            self.remote(u, 4, held.at[:, 1 - self.y, self.x], self.blocks_y.at[u], self.over_y),
        )

    def ends(self, u):
        found = []
        for k in range(1, GRID[0]):
            to = lax.rem(self.z + k, GRID[0])
            going = self.going.at[self.slot(u), to]
            found.append(self.remote(u, 4 + k, going, self.coming.at[u, k - 1], (to, self.y, self.x, self.c)))
        return found

    def turned_end(self, u, k):
        to = u - TURNED[0]
        return self.remote(
            u, 5, self.going.at[self.slot(u)], self.turned_in.at[k - 1], (to, self.y, self.x, self.c),
            self.turned_receive.at[k - 1],
        )

    def is_turned(self, u):
        return jnp.logical_and(u >= TURNED[0], u < TURNED[1])

    def pieces(self, u, left, right):
        slot, depth = self.slot(u), self.out.shape[-2]
        z, y, x, c = GRID
        turned = jnp.logical_and(u >= TURNED[0], u < TURNED[1]).astype(jnp.int32)

        def piece(part, columns):
            many = left.shape[-1] // PIECES[0]
            wide = right.shape[-1] // PIECES[1]
            lanes = slice(columns * wide, (columns + 1) * wide)
            grad = dot_tn(left[:, part * many : (part + 1) * many], right[:, lanes]).astype(LOW)
            blocks = grad.reshape(many // depth, depth, grad.shape[1])
            for number in range(many // depth):
                b = part * (many // depth) + number
                even = (b % c, b // (x * y * c), b // (x * c) % y, b // c % x)
                other = (b // z % c, b % z, b // (z * c * x), b // (z * c) % x)
                where = [i + turned * (j - i) for i, j in zip(even, other)]
                self.mine[slot, where[0], where[1], where[2], where[3], :, lanes] = blocks[number]

        return [functools.partial(piece, i, j) for i in range(PIECES[0]) for j in range(PIECES[1])]

    def stage(self, tick, lag, work):
        pl.when(jnp.logical_and(tick >= lag, tick < lag + UNITS))(functools.partial(work, tick - lag))

    def add_pair(self, u):
        slot, c = self.slot(u), self.c
        self.pair(u).wait()
        self.mine[slot, c] = (self.mine[slot, c].astype(F32) + self.pairs[slot].astype(F32)).astype(LOW)
        for copy in self.sides(u):
            copy.start()

    def add_sides(self, u):
        for copy in self.sides(u):
            copy.wait()
        held = self.mine.at[self.slot(u), self.c]
        low, high, y, x = self.low, self.high, self.y, self.x
        held[low, 1 - y, x] = (held[low, 1 - y, x].astype(F32) + self.sides_x[u].astype(F32)).astype(LOW)
        held[high, y, 1 - x] = (held[high, y, 1 - x].astype(F32) + self.sides_y[u].astype(F32)).astype(LOW)
        for copy in self.blocks(u):
            copy.start()

    def add_blocks(self, u):
        slot = self.slot(u)
        for copy in self.blocks(u):
            copy.wait()
        total = self.mine[slot, self.c, :, self.y, self.x].astype(F32)
        total = total + self.blocks_x[u].astype(F32) + self.blocks_y[u].astype(F32)
        self.kept_sum[slot] = total
        self.going[slot] = total.astype(LOW)

        def even():
            for copy in self.ends(u):
                copy.start()

        pl.when(jnp.logical_not(self.is_turned(u)))(even)
        for k in range(1, GRID[0]):
            away = lax.rem(self.z + 2 * GRID[0] - jnp.minimum(u, 2 * GRID[0]), GRID[0]) == k
            pl.when(jnp.logical_and(self.is_turned(u), away))(lambda k=k: self.turned_end(u, k).start())

    def add_ends(self, u):
        slot = self.slot(u)

        def even():
            for copy in self.ends(u):
                copy.wait()
            total = self.kept_sum[slot, self.z]
            for k in range(GRID[0] - 1):
                total += self.coming[u, k].astype(F32)
            self.out[u] = total

        def turned_here():
            total = self.kept_sum[slot]
            for k in range(1, GRID[0]):
                self.turned_end(u, k).wait_recv()
                total += self.turned_in[k - 1].astype(F32)
            self.out[TURNED[0] : TURNED[1]] = total

        pl.when(jnp.logical_not(self.is_turned(u)))(even)
        ahead = lax.rem(self.z + 2 * GRID[0] - jnp.minimum(u, 2 * GRID[0]), GRID[0])
        pl.when(jnp.logical_and(self.is_turned(u), ahead == 0))(turned_here)
        for k in range(1, GRID[0]):
            pl.when(jnp.logical_and(self.is_turned(u), ahead == k))(lambda k=k: self.turned_end(u, k).wait_send())


def reduce_kernel(
    extents, vectors, x_ref, edge_ref, k_ref, v_ref, s_ref, y_ref, d_ref, state_ref, mid_ref, packed,
    sums_two, square, acts,
    stream_out, mixed, out, small_out,
    grow, shrink, carry, state, weights, weight_sem, staged, sums_one, lefts, rights, sums, small_in,
    stage_sem, left_sem, right_sem, small_send, small_receive, *refs,
):
    tick = pl.program_id(0)
    z, y, x, c = place()
    rows = x_ref.shape[0]
    tiles = mixed.shape[1] // rows
    job = Reduce(out, *refs)
    partners = (
        (z, y, x, 1 - c),
        (z, y, 1 - x, c),
        (z, 1 - y, x, c),
        (z + 1 - 2 * lax.rem(z, 2), y, x, c),
        (lax.rem(z + 2, GRID[0]), y, x, c),
    )

    def exchange(step):
        return pltpu.make_async_remote_copy(
            src_ref=sums.at[step],
            dst_ref=small_in.at[step],
            send_sem=small_send.at[step],
            recv_sem=small_receive.at[step],
            device_id=device(*partners[step]),
            device_id_type=MESH,
        )

    def left_of(u):
        return lax.rem(jnp.maximum(u - 3, 0), 2)

    def right_of(u):
        return lax.rem(jnp.minimum(u, 4) + jnp.maximum(u - 7, 0), 2)

    def fetch_left(u, late):
        source = mixed.at[u - FIRST_UNITS] if late else acts.at[jnp.maximum(u - 3, 0)]
        return pltpu.make_async_copy(source, lefts.at[left_of(u)], left_sem.at[left_of(u)])

    def fetch_right(u, late):
        if late:
            source = mixed.at[u - FIRST_UNITS + 3]
        else:
            source = acts.at[7 + jnp.minimum(u, 4) + jnp.maximum(u - 7, 0)]
        return pltpu.make_async_copy(source, rights.at[right_of(u)], right_sem.at[right_of(u)])

    def fetches(u, work):
        early, late = u < FIRST_UNITS, jnp.logical_and(u >= FIRST_UNITS, u < UNITS)
        pl.when(jnp.logical_and(early, jnp.logical_or(u == 0, u >= 4)))(lambda: work(fetch_left(u, False)))
        pl.when(jnp.logical_and(early, jnp.logical_or(u <= 4, u >= 8)))(lambda: work(fetch_right(u, False)))
        pl.when(late)(lambda: work(fetch_left(u, True)))
        pl.when(late)(lambda: work(fetch_right(u, True)))

    def keep(number):
        two = lax.rem(number, 2)
        where = pl.ds(pl.multiple_of((tiles - 1 - number) * rows, rows), rows)
        return pltpu.make_async_copy(staged.at[two], mixed.at[:, where], stage_sem.at[two])

    def start(copy):
        copy.start()

    def wait(copy):
        copy.wait()

    @pl.when(tick == 0)
    def _():
        fetches(tick, start)
        pltpu.make_async_copy(packed.at[0:4], weights, weight_sem).start()
        greet()

    @pl.when(tick == FIRST_TILE)
    def _():
        pltpu.make_async_copy(packed.at[0:4], weights, weight_sem).wait()

    number = tick - FIRST_TILE
    pl.when(jnp.logical_and(number >= 2, number < tiles + 1))(lambda: keep(number - 2).wait())
    pl.when(number == tiles)(lambda: keep(number - 1).wait())
    fetches(tick + 1, start)
    fetches(tick, wait)

    inputs = (extents, vectors, x_ref, edge_ref, k_ref, v_ref, s_ref, y_ref, d_ref, state_ref, mid_ref, weights)

    def pieces():
        return job.pieces(tick, lefts.at[left_of(tick)], rights.at[right_of(tick)])

    busy = jnp.logical_and(number >= 0, number < tiles)

    @pl.when(busy)
    def _():
        back_tile(
            tiles - 1 - number, number == 0, *inputs, stream_out, staged.at[lax.rem(number, 2)], sums_one,
            grow, shrink, carry, state, between=pieces(),
        )
        keep(number).start()
        job.pair(tick).start()

    @pl.when(jnp.logical_and(jnp.logical_not(busy), tick < UNITS))
    def _():
        for piece in pieces():
            piece()
        job.pair(tick).start()

    for lag, work in zip(LAGS, (job.add_pair, job.add_sides, job.add_blocks, job.add_ends)):
        job.stage(tick, lag, work)

    @pl.when(number == tiles)
    def _():
        sums[0] = small_grads(vectors, sums_one, sums_two, square)
        exchange(0).start()

    for step in range(1, 6):

        @pl.when(number == tiles + step)
        def _():
            exchange(step - 1).wait()
            total = sums[step - 1] + small_in[step - 1]
            if step == 5:
                small_out[...] = total
            else:
                sums[step] = total
                exchange(step).start()


def whole(shape):
    return pl.BlockSpec(shape, lambda i: (0,) * len(shape), pipeline_mode=pl.Buffered(1))


def kept(shape):
    return pl.BlockSpec(shape, lambda i: (0,) * len(shape))


def smem():
    return pl.BlockSpec(memory_space=pltpu.SMEM)


ROWS = 256
UNITS = 13
SLOTS = 6
LAGS = (1, 2, 3, 6)
PIECES = (2, 1)
FIRST_UNITS = 10
FIRST_TILE = 1
TURNED = (4, 8)
FEED_ACTS = 14


def four(packed):
    return pl.BlockSpec((4, *packed.shape[1:]), lambda i: (0,) * len(packed.shape), pipeline_mode=pl.Buffered(1))


def front_shapes(tokens, width):
    wide = jax.ShapeDtypeStruct((tokens, width), F32)
    low = jax.ShapeDtypeStruct((tokens, width), LOW)
    states = jax.ShapeDtypeStruct((tokens // BLOCK, 8, width), F32)
    return [wide] * 5 + [low, wide, states, jax.ShapeDtypeStruct((8, width), F32)]


def front_specs(width, index):
    tile = pl.BlockSpec((ROWS, width), lambda i: (index(i), 0))
    states = pl.BlockSpec((ROWS // BLOCK, 8, width), lambda i: (index(i), 0, 0))
    return [tile] * 7 + [states, kept((8, width))]


def front_scratch(width):
    return [
        pltpu.VMEM((BLOCK, width), F32),
        pltpu.VMEM((BLOCK + EDGE, width), F32),
        pltpu.VMEM((8, width), F32),
        pltpu.VMEM((8, width), F32),
    ]


def front(extents, vectors, x, packed):
    tokens, width = x.shape
    return pl.pallas_call(
        front_kernel,
        name="front",
        grid=(tokens // ROWS,),
        in_specs=[smem(), whole(vectors.shape), pl.BlockSpec((ROWS, width), lambda i: (i, 0)), four(packed)],
        out_specs=front_specs(width, lambda i: i),
        out_shape=front_shapes(tokens, width),
        scratch_shapes=front_scratch(width),
        compiler_params=pltpu.CompilerParams(vmem_limit_bytes=56 * MIB),
    )(extents, vectors, x, packed)


def gather_front(extents, lines, shards, x):
    tokens, width = x.shape
    tiles = tokens // ROWS
    depth = shards[0].shape[0]
    anywhere = pl.BlockSpec(memory_space=pl.ANY)

    def index(i):
        return jnp.clip(i - 8, 0, tiles - 1)

    dma = pltpu.SemaphoreType.DMA
    return pl.pallas_call(
        functools.partial(gather_kernel, tiles),
        name="gather_front",
        grid=(max(UNITS + 4, LATE + 6, tiles + 8),),
        in_specs=[smem()]
        + [whole(part.shape) for part in shards]
        + [pl.BlockSpec((ROWS, width), lambda i: (index(i), 0))]
        + [whole(line.shape) for line in lines],
        out_specs=[anywhere, kept((SMALL_ROWS, width))] + front_specs(width, index),
        out_shape=[
            jax.ShapeDtypeStruct((UNITS, *GRID, depth, width), LOW),
            jax.ShapeDtypeStruct((SMALL_ROWS, width), F32),
        ]
        + front_shapes(tokens, width),
        scratch_shapes=[
            pltpu.VMEM((SMALL_ROWS, 128), F32),
            pltpu.VMEM((*GRID, SMALL_ROWS, 128), F32),
            pltpu.VMEM((UNITS, depth, width), LOW),
            pltpu.VMEM((4, *GRID, depth, width), LOW),
        ]
        + front_scratch(width)
        + [dma((UNITS,)), dma((4,)), dma((9, HOPS)), dma((UNITS, HOPS)), dma((HOPS,)), dma((HOPS,))],
        compiler_params=pltpu.CompilerParams(vmem_limit_bytes=56 * MIB, collective_id=0, has_side_effects=True),
    )(extents, *shards, x, *lines)


def feed(extents, vectors, mid, upstream, blend, packed):
    tokens, width = mid.shape
    hidden = 4 * width
    rows, tiles = ROWS, tokens // ROWS
    tile = pl.BlockSpec((rows, width), lambda i: (tiles - 1 - i, 0))
    edge = pl.BlockSpec((EDGE, width), lambda i: (jnp.maximum((tiles - 1 - i) * (rows // EDGE) - 1, 0), 0))
    block = packed.shape[1:]
    return pl.pallas_call(
        feed_kernel,
        name="feed",
        grid=(tiles,),
        in_specs=[smem(), whole(vectors.shape), tile, edge, tile, tile, pl.BlockSpec(memory_space=pl.ANY)],
        out_specs=[
            tile,
            tile,
            pl.BlockSpec((FEED_ACTS, rows, width), lambda i: (0, tiles - 1 - i, 0)),
            kept((48, width)),
        ],
        out_shape=[
            jax.ShapeDtypeStruct((tokens, width), LOW),
            jax.ShapeDtypeStruct((tokens, width), F32),
            jax.ShapeDtypeStruct((FEED_ACTS, tokens, width), LOW),
            jax.ShapeDtypeStruct((48, width), F32),
        ],
        scratch_shapes=[
            pltpu.VMEM((rows, hidden), F32),
            pltpu.VMEM((8, width), F32),
            pltpu.VMEM(block, LOW),
            pltpu.VMEM((4, *block), LOW),
            pltpu.VMEM((*block[:4], 4, *block[4:]), LOW),
            pltpu.SemaphoreType.DMA((6,)),
        ],
        compiler_params=pltpu.CompilerParams(vmem_limit_bytes=60 * MIB),
    )(extents, vectors, mid, mid, upstream, blend, packed)


def back_specs(tokens, width, packed, index):
    blocks = ROWS // BLOCK
    tile = pl.BlockSpec((ROWS, width), lambda i: (index(i), 0))
    edge = pl.BlockSpec((16, width), lambda i: (jnp.maximum(index(i) * (ROWS // 16) - 1, 0), 0))
    states = pl.BlockSpec((blocks, 8, width), lambda i: (index(i), 0, 0))
    inputs = [smem(), whole((SMALL_ROWS, width)), tile, edge] + [tile] * 5 + [states, tile, four(packed)]
    outputs = [tile, pl.BlockSpec((6, ROWS, width), lambda i: (0, index(i), 0)), kept((56, width))]
    shapes = [
        jax.ShapeDtypeStruct((tokens, width), LOW),
        jax.ShapeDtypeStruct((6, tokens, width), LOW),
        jax.ShapeDtypeStruct((56, width), F32),
    ]
    scratch = [
        pltpu.VMEM((BLOCK + EDGE, width), F32),
        pltpu.VMEM((BLOCK, width), F32),
        pltpu.VMEM((8, width), F32),
        pltpu.VMEM((8, width), F32),
    ]
    return inputs, outputs, shapes, scratch


def back(extents, vectors, x, saved, states, back_mid, packed):
    tokens, width = x.shape
    tiles = tokens // ROWS
    inputs, outputs, shapes, scratch = back_specs(tokens, width, packed, lambda i: tiles - 1 - i)
    return pl.pallas_call(
        back_kernel,
        name="back",
        grid=(tiles,),
        in_specs=inputs,
        out_specs=outputs,
        out_shape=shapes,
        scratch_shapes=scratch,
        compiler_params=pltpu.CompilerParams(vmem_limit_bytes=56 * MIB),
    )(extents, vectors, x, x, *saved, states, back_mid, packed)


def reduce(extents, vectors, x, saved, states, back_mid, packed, acts, sums_two, square):
    tokens, width = x.shape
    tiles, depth = tokens // ROWS, packed.shape[-2]
    inputs, outputs, shapes, scratch = back_specs(
        tokens, width, packed, lambda i: tiles - 1 - jnp.clip(i - FIRST_TILE, 0, tiles - 1)
    )
    stream, mixed, sums_one = shapes
    anywhere = pl.BlockSpec(memory_space=pl.ANY)
    z, y, x_size, c = GRID
    dma = pltpu.SemaphoreType.DMA
    small = (SMALL_ROWS, width)
    return pl.pallas_call(
        reduce_kernel,
        name="reduce",
        grid=(UNITS + LAGS[3],),
        in_specs=inputs[:-1] + [anywhere, whole(sums_two.shape), whole(square.shape), anywhere],
        out_specs=[outputs[0], anywhere, kept((UNITS, depth, width)), kept(small)],
        out_shape=[
            stream,
            mixed,
            jax.ShapeDtypeStruct((UNITS, depth, width), F32),
            jax.ShapeDtypeStruct(small, F32),
        ],
        scratch_shapes=scratch
        + [
            pltpu.VMEM((4, *packed.shape[1:]), LOW),
            dma,
            pltpu.VMEM((2, 6, ROWS, width), LOW),
            pltpu.VMEM(sums_one.shape, F32),
            pltpu.VMEM((2, tokens, width), LOW),
            pltpu.VMEM((2, tokens, width), LOW),
            pltpu.VMEM((5, *small), F32),
            pltpu.VMEM((5, *small), F32),
            dma((2,)),
            dma((2,)),
            dma((2,)),
            dma((5,)),
            dma((5,)),
            pltpu.VMEM((SLOTS, c, z, y, x_size, depth, width), LOW),
            pltpu.VMEM((SLOTS, z, y, x_size, depth, width), LOW),
            pltpu.VMEM((UNITS, z // 2, depth, width), LOW),
            pltpu.VMEM((UNITS, z // 2, depth, width), LOW),
            pltpu.VMEM((UNITS, z, depth, width), LOW),
            pltpu.VMEM((UNITS, z, depth, width), LOW),
            pltpu.VMEM((SLOTS, z, depth, width), F32),
            pltpu.VMEM((SLOTS, z, depth, width), LOW),
            pltpu.VMEM((UNITS, z - 1, depth, width), LOW),
            pltpu.VMEM((z - 1, z, depth, width), LOW),
            dma((SLOTS, 8)),
            dma((UNITS, 8)),
            dma((z - 1,)),
        ],
        compiler_params=pltpu.CompilerParams(vmem_limit_bytes=63 * MIB, collective_id=1, has_side_effects=True),
    )(extents, vectors, x, x, *saved, states, back_mid, packed, sums_two, square, acts)


def finish_kernel(entries, share, stream_ref, total, small, stream_out, *outs):
    *squares, w1, w2, rms = outs[:8]
    lines = outs[8:]
    stream_out[...] = stream_ref[...]

    @pl.when(pl.program_id(0) == 0)
    def _():
        width = small.shape[1]
        for out, u in zip(squares, (10, 11, 12, 9, 8)):
            out[...] = total[u]
        for j in range(4):
            w1[:, j * width : (j + 1) * width] = total[j]
            w2[j] = total[4 + j]
        sums = small[...]
        rms[...] = jnp.sqrt(sums[len(SMALL), :3] / entries)
        mine = lax.axis_index("wide") * lax.axis_size("narrow") + lax.axis_index("narrow")
        turned = pltpu.roll(sums, lax.rem(width - mine * share, width), 1)
        for row, out in enumerate(lines):
            out[...] = turned[row, :share]


def finish_up(stream, total, small, entries):
    tokens, width = stream.shape
    depth = total.shape[1]
    parts = 2
    tile = pl.BlockSpec((tokens // parts, width), lambda i: (i, 0))
    shapes = [(depth, width)] * 5 + [(depth, 4 * width), (4, depth, width), (3,)] + [(depth,)] * len(SMALL)
    return pl.pallas_call(
        functools.partial(finish_kernel, entries, depth),
        name="finish_up",
        grid=(parts,),
        in_specs=[tile, whole(total.shape), whole(small.shape)],
        out_specs=[tile] + [kept(shape) for shape in shapes],
        out_shape=[jax.ShapeDtypeStruct(stream.shape, LOW)] + [jax.ShapeDtypeStruct(shape, F32) for shape in shapes],
        compiler_params=pltpu.CompilerParams(vmem_limit_bytes=60 * MIB),
    )(stream, total, small)


def small_grads(vectors, sums_one, sums_two, square):
    width = vectors.shape[1]
    one = [jnp.sum(sums_one[8 * i : 8 * i + 8, :], axis=0, keepdims=True) for i in range(7)]
    two = [jnp.sum(sums_two[8 * i : 8 * i + 8, :], axis=0, keepdims=True) for i in range(6)]
    decay = one[4] * jnp.exp(vec(vectors, FADING))
    lane = rows_of((1, width), 1)
    squares = jnp.zeros((1, width), F32)
    for place_of, total in enumerate((two[4], jnp.sum(square[...], axis=0, keepdims=True), two[5])):
        squares = jnp.where(lane == place_of, jnp.sum(total, axis=1, keepdims=True), squares)
    rows = [one[0], one[1], one[2], decay, one[3], two[0], two[1], one[5], one[6], two[2], two[3], squares]
    return jnp.concatenate(rows + [jnp.zeros((SMALL_ROWS - len(rows), width), F32)], axis=0)


def pack(weights):
    *square, w1, w2 = weights
    depth, width = square[0].shape[-2:]
    parts = list(square)
    parts += [w1[..., j * width : (j + 1) * width] for j in range(4)]
    parts += [w2[..., j * depth : (j + 1) * depth, :] for j in range(4)]
    return jnp.stack(parts)


SMALL = (0, 1, 2, 3, 4, 9, 10, 14, 15, 16, 17)
LARGE = (5, 6, 7, 8, 13, 11, 12)


def finish(outcome, stream, large, small, squares, entries):
    shards = [None] * 18
    for row, i in enumerate(SMALL):
        shards[i] = small[row]
    for grad, i in zip(large, LARGE):
        shards[i] = grad
    return (outcome, stream, *shards, jnp.sqrt(squares / entries))


def body_any(residual_input, extents, *rest):
    parameters, upstream = rest[:18], rest[18]
    devices = lax.axis_size(AXES)
    held = jnp.stack([parameters[i] for i in SMALL])
    width = held.shape[1] * devices
    vectors = lax.all_gather(held, AXES, axis=1, tiled=True).astype(F32)
    vectors = jnp.pad(vectors, ((0, SMALL_ROWS - len(SMALL)), (0, 0)))
    blocks = 1
    for size in GRID:
        blocks *= size
    weights = [lax.all_gather(parameters[i], AXES, axis=0, tiled=True) for i in LARGE]
    packed = pack([w.reshape(blocks, -1, w.shape[1]) for w in weights])
    packed = packed.reshape(UNITS, *GRID, *packed.shape[2:])
    *saved, blend, mid, states, square = front(extents, vectors, residual_input, packed)
    outcome, back_mid, acts, sums_two = feed(extents, vectors, mid, upstream, blend, packed)
    stream, mixed, sums_one = back(extents, vectors, residual_input, saved, states, back_mid, packed)
    small = small_grads(vectors, sums_one, sums_two, square)
    grads = [dot_tn(mixed[i], mixed[3 + i]) for i in range(3)] + [dot_tn(acts[6], acts[13]), dot_tn(acts[5], acts[12])]
    grads.append(jnp.concatenate([dot_tn(acts[0], acts[7 + j]) for j in range(4)], axis=1))
    grads.append(jnp.concatenate([dot_tn(acts[1 + j], acts[11]) for j in range(4)], axis=0))
    squares = lax.psum(small[len(SMALL), :3], AXES)
    small = lax.psum_scatter(small[: len(SMALL)], AXES, scatter_dimension=1, tiled=True)
    large = [lax.psum_scatter(grad, AXES, scatter_dimension=0, tiled=True) for grad in grads]
    return finish(outcome, stream, large, small, squares, residual_input.shape[0] * width * devices)


def body(residual_input, extents, *rest):
    parameters, upstream = rest[:18], rest[18]
    devices = lax.axis_size(AXES)
    width = residual_input.shape[1]
    share = width // devices
    shards = [parameters[i] for i in LARGE]
    shards[6] = shards[6].reshape(4, share, width)
    packed, vectors, *saved, blend, mid, states, square = gather_front(
        extents, [parameters[i] for i in SMALL], shards, residual_input
    )
    outcome, back_mid, acts, sums_two = feed(extents, vectors, mid, upstream, blend, packed)
    stream, _, total, small = reduce(
        extents, vectors, residual_input, saved, states, back_mid, packed, acts, sums_two, square
    )
    stream, *rest = finish_up(stream, total, small, residual_input.shape[0] * width * devices)
    large, rms, lines = rest[:7], rest[7], rest[8:]
    large[6] = large[6].reshape(4 * share, width)
    shards = [None] * 18
    for line, i in zip(lines, SMALL):
        shards[i] = line
    for grad, i in zip(large, LARGE):
        shards[i] = grad
    return (outcome, stream, *shards, rms)


def solution(mesh):
    rows, vector = P(AXES, None), P(AXES)
    kinds = [vector] * 5 + [rows] * 4 + [vector] * 2 + [rows] * 3 + [vector] * 4
    sizes = (mesh.shape["wide"], mesh.shape["narrow"])
    return jax.shard_map(
        body if sizes == (GRID[0] * GRID[1], GRID[2] * GRID[3]) else body_any,
        mesh=mesh,
        in_specs=(rows, rows, *kinds, rows),
        out_specs=(rows, rows, *kinds, P()),
        check_vma=False,
    )
```

```python
import functools

import jax
import jax.numpy as jnp
from jax import lax
from jax.experimental import pallas as pl
from jax.experimental.pallas import tpu as pltpu
from jax.sharding import PartitionSpec as P

F32 = jnp.float32
LOW = jnp.bfloat16
AXES = ("wide", "narrow")
BLOCK = 128
EDGE = 8
MIB = 2**20

(KEY_MIX, VALUE_MIX, GATE_MIX, FADING, REWARD, FEED_MIX, GATING_MIX, GAIN_ONE, BIAS_ONE, GAIN_TWO, BIAS_TWO) = range(11)
VECTORS = 16


def dot(left, right):
    return jnp.dot(left, right, preferred_element_type=F32)


def dot_nt(left, right):
    return lax.dot_general(left, right, (((1,), (1,)), ((), ())), preferred_element_type=F32)


def dot_tn(left, right):
    return lax.dot_general(left, right, (((0,), (0,)), ((), ())), preferred_element_type=F32)


def offsets_of(extents):
    offsets, total = [], 0
    for j in range(extents.shape[1] - 1):
        total = total + extents[0, j]
        offsets.append(total)
    return offsets


def start_of(places, offsets):
    begun = jnp.zeros_like(places)
    for offset in offsets:
        begun = jnp.where(places >= offset, offset, begun)
    return begun


def normed(x):
    centered = x - jnp.mean(x, axis=1, keepdims=True)
    scale = lax.rsqrt(jnp.mean(centered * centered, axis=1, keepdims=True) + 1e-05)
    return centered * scale, scale


def fold(x):
    return jnp.sum(x.reshape(x.shape[0] // 8, 8, x.shape[1]), axis=0)


def rows_of(shape, axis=0):
    return lax.broadcasted_iota(jnp.int32, shape, axis)


def shift_down(x, first, keep):
    return jnp.where(rows_of((x.shape[0], 1)) == 0, first, pltpu.roll(x, 1, 0)) * keep


def shift_up(x, last):
    rows = x.shape[0]
    return jnp.where(rows_of((rows, 1)) == rows - 1, last, pltpu.roll(x, rows - 1, 0))


def split(top, bottom):
    both = jnp.concatenate([top, bottom], axis=1)
    high = both.astype(LOW)
    low = (both - high.astype(F32)).astype(LOW)
    return jnp.concatenate([high, low], axis=0)


def norm_grad(back_normed, hat, scale, gain):
    back_hat = back_normed * gain
    return scale * (
        back_hat
        - jnp.mean(back_hat, axis=1, keepdims=True)
        - hat * jnp.mean(back_hat * hat, axis=1, keepdims=True)
    )


def vec(vectors, row):
    return vectors[row : row + 1, :]


def matrix(ref):
    return ref[...].reshape(-1, ref.shape[-1])


def front_tile(
    tile, extents, vectors, x_ref, wk, wv, wr, wo,
    k_out, v_out, s_out, y_out, d_out, blend_out, mid_out, state_out, square_out,
    grow, shrink, last, state,
):
    rows, width = x_ref.shape
    half = BLOCK // 2
    offsets = offsets_of(extents)
    rate = jnp.exp(vec(vectors, FADING))

    @pl.when(tile == 0)
    def _():
        local = rows_of((BLOCK + EDGE, 1)).astype(F32)
        shrink[...] = jnp.exp((half - local) * rate)
        grow[...] = jnp.exp((local[:BLOCK] + (1 - half)) * rate)
        last[...] = jnp.zeros_like(last)
        state[...] = jnp.zeros_like(state)
        square_out[...] = jnp.zeros_like(square_out)

    x = x_ref[...].astype(F32)
    hat, _ = normed(x)
    norm = hat * vec(vectors, GAIN_ONE) + vec(vectors, BIAS_ONE)
    places = tile * rows + rows_of((rows, 1))
    keep = (places != start_of(places, offsets)).astype(F32)
    before = shift_down(norm, last[0:1, :], keep)
    last[0:1, :] = norm[rows - 1 : rows, :]

    def mixed(row):
        mix = vec(vectors, row)
        return (norm * mix + before * (1.0 - mix)).astype(LOW)

    keys = dot(mixed(KEY_MIX), matrix(wk))
    values = dot(mixed(VALUE_MIX), matrix(wv))
    sig = jax.nn.sigmoid(dot(mixed(GATE_MIX), matrix(wr)))
    k_out[...] = keys
    v_out[...] = values
    s_out[...] = sig
    fade_half = jnp.exp(-half * rate)
    reward = vec(vectors, REWARD)
    for block in range(rows // BLOCK):
        here = slice(block * BLOCK, (block + 1) * BLOCK)
        key, value = keys[here], values[here]
        weight = grow[...] * jnp.exp(key)
        first = tile * rows + block * BLOCK
        after = first + rows_of((BLOCK + EDGE, 1))
        column = rows_of((1, 2 * BLOCK), 1)
        source = first + jnp.where(column >= BLOCK, column - BLOCK, column)
        begun = start_of(after, offsets)
        paired = ((source < after) & (source >= begun)).astype(LOW)
        sums = dot(paired, split(weight * value, weight))
        inherit = (begun < first).astype(F32)
        top = shrink[...] * (sums[:, :width] + inherit * (fade_half * state[0:1, :]))
        bottom = shrink[...] * (sums[:, width:] + inherit * (fade_half * state[1:2, :]))
        state[0:1, :] = top[BLOCK : BLOCK + 1]
        state[1:2, :] = bottom[BLOCK : BLOCK + 1]
        state_out[block, :, :] = state[...]
        own = jnp.exp(reward + key)
        inverse = 1.0 / (bottom[:BLOCK] + own)
        wkv = (top[:BLOCK] + own * value) * inverse
        y_out[here, :] = wkv
        d_out[here, :] = inverse
        blend_out[here, :] = (sig[here] * wkv).astype(LOW)
    attended = dot(blend_out[...], matrix(wo))
    mid_out[...] = x + attended
    square_out[...] += fold(attended * attended)


def front_kernel(extents, vectors, x_ref, weights, *rest):
    front_tile(pl.program_id(0), extents, vectors, x_ref, *[weights.at[u] for u in range(4)], *rest)


def feed_kernel(
    extents, vectors, mid_ref, edge_ref, up_ref, packed,
    out_out, back_out, acts, sums_out,
    lift, carry, wg, w1, w2, load,
):
    step = pl.program_id(0)
    tile = pl.num_programs(0) - 1 - step
    rows, width = mid_ref.shape
    hidden = lift.shape[1]
    offsets = offsets_of(extents)

    @pl.when(step == 0)
    def _():
        copies = [(packed.at[4], wg), (packed.at[5:9], w1)]
        copies += [(packed.at[9 + j], w2.at[:, :, :, :, j]) for j in range(4)]
        copies = [pltpu.make_async_copy(a, b, load.at[i]) for i, (a, b) in enumerate(copies)]
        for copy in copies:
            copy.start()
        for copy in copies:
            copy.wait()
        carry[...] = jnp.zeros_like(carry)
        sums_out[...] = jnp.zeros_like(sums_out)

    gain, bias = vec(vectors, GAIN_TWO), vec(vectors, BIAS_TWO)
    mid = mid_ref[...]
    hat, scale = normed(mid)
    norm = hat * gain + bias
    edge_hat, _ = normed(edge_ref[...])
    edge = (edge_hat * gain + bias)[EDGE - 1 : EDGE]
    places = tile * rows + rows_of((rows, 1))
    keep = (places != start_of(places, offsets)).astype(F32)
    before = shift_down(norm, edge, keep)
    mix_k, mix_g = vec(vectors, FEED_MIX), vec(vectors, GATING_MIX)
    feed_key = (norm * mix_k + before * (1.0 - mix_k)).astype(LOW)
    feed_gate = (norm * mix_g + before * (1.0 - mix_g)).astype(LOW)
    acts[0] = feed_key
    acts[5] = feed_gate
    lowered = None
    group = []
    for j in range(hidden // width):
        chunk = slice(j * width, (j + 1) * width)
        lifted = jnp.maximum(dot(feed_key, matrix(w1.at[j])), 0.0)
        lift[:, chunk] = lifted.astype(LOW)
        squared = (lifted * lifted).astype(LOW)
        acts[1 + j] = squared
        group.append(squared)
        if len(group) == GROUP:
            part = dot(jnp.concatenate(group, axis=1), matrix(w2.at[j + 1 - GROUP : j + 1]))
            lowered = part if lowered is None else lowered + part
            group = []
    sig = jax.nn.sigmoid(dot(feed_gate, matrix(wg)))
    feed_out = sig * lowered
    result = mid + feed_out
    out_out[...] = result.astype(LOW)
    upstream = up_ref[...].astype(F32)
    back_lowered = (upstream * sig).astype(LOW)
    back_gate = (upstream * lowered * sig * (1.0 - sig)).astype(LOW)
    acts[10] = back_lowered
    acts[11] = back_gate
    group = []
    for j in range(hidden // width):
        chunk = slice(j * width, (j + 1) * width)
        back_lifted = (2.0 * lift[:, chunk].astype(F32) * dot_nt(back_lowered, matrix(w2.at[j]))).astype(LOW)
        acts[6 + j] = back_lifted
        group.append(back_lifted)
    back_key = dot_nt(
        jnp.concatenate(group, axis=1),
        jnp.concatenate([matrix(w1.at[j]) for j in range(hidden // width)], axis=1),
    )
    back_gating = dot_nt(back_gate, matrix(wg))
    late = norm - before
    back_before = keep * (back_key * (1.0 - mix_k) + back_gating * (1.0 - mix_g))
    back_norm = back_key * mix_k + back_gating * mix_g + shift_up(back_before, carry[0:1, :])
    carry[0:1, :] = back_before[0:1]
    back_mid = upstream + norm_grad(back_norm, hat, scale, gain)
    back_out[...] = back_mid
    acts[12] = back_mid.astype(LOW)
    for row, piece in enumerate(
        (back_key * late, back_gating * late, back_norm * hat, back_norm, result * result, feed_out * feed_out)
    ):
        sums_out[8 * row : 8 * row + 8, :] += fold(piece)


def back_tile(
    tile, begins, extents, vectors, x_ref, edge_ref, k_ref, v_ref, s_ref, y_ref, d_ref, state_ref, mid_ref, weights,
    stream_out, acts, sums_out,
    grow, shrink, carry, state, between=(),
):
    rows, width = x_ref.shape
    half = BLOCK // 2
    offsets = offsets_of(extents)
    rate = jnp.exp(vec(vectors, FADING))

    @pl.when(begins)
    def _():
        local = rows_of((BLOCK + EDGE, 1)).astype(F32)
        shrink[...] = jnp.exp((half - local[:BLOCK]) * rate)
        grow[...] = jnp.exp((local + (1 - EDGE - half)) * rate)
        carry[...] = jnp.zeros_like(carry)
        state[...] = jnp.zeros_like(state)
        sums_out[...] = jnp.zeros_like(sums_out)

    between = iter(between)
    back_mid = mid_ref[...]
    back_attended = back_mid.astype(LOW)
    back_blend = dot_nt(back_attended, matrix(weights.at[3]))
    sig = s_ref[...]
    wkv = y_ref[...]
    acts[5] = (back_blend * wkv * sig * (1.0 - sig)).astype(LOW)
    back_top = back_blend * sig * d_ref[...]
    fade_half = jnp.exp(-half * rate)
    reward = vec(vectors, REWARD)
    for block in reversed(range(rows // BLOCK)):
        next(between, int)()
        here = slice(block * BLOCK, (block + 1) * BLOCK)
        key, value = k_ref[here, :], v_ref[here, :]
        first = tile * rows + block * BLOCK
        source = first - EDGE + rows_of((BLOCK + EDGE, 1))
        column = rows_of((1, 2 * BLOCK), 1)
        after = first + jnp.where(column >= BLOCK, column - BLOCK, column)
        paired = ((source < after) & (source >= start_of(after, offsets))).astype(LOW)
        bt = back_top[here]
        weighted = shrink[...] * bt
        sums = dot(paired, split(weighted, -weighted * wkv[here]))
        following = start_of(first + BLOCK + jnp.zeros((1, 1), jnp.int32), offsets)
        tail = (source >= following).astype(F32)
        top = grow[...] * (sums[:, :width] + tail * (fade_half * state[0:1, :]))
        bottom = grow[...] * (sums[:, width:] + tail * (fade_half * state[1:2, :]))
        next(between, int)()
        crossing = state_ref[block, :, :] * state[...]
        sums_out[32:40, :] += jnp.where(rows_of((8, 1)) < 2, crossing * (-1.0 * BLOCK), 0.0)
        state[0:1, :] = top[EDGE - 1 : EDGE]
        state[1:2, :] = bottom[EDGE - 1 : EDGE]
        weight = jnp.exp(key)
        own = jnp.exp(reward + key) * bt
        passed = weight * (value * top[EDGE:] + bottom[EDGE:])
        bonus = own * (value - wkv[here])
        back_key = passed + bonus
        acts[3, here, :] = back_key.astype(LOW)
        acts[4, here, :] = (weight * top[EDGE:] + own).astype(LOW)
        local = rows_of((BLOCK, 1)).astype(F32)
        sums_out[24:32, :] += fold(bonus)
        sums_out[32:40, :] += fold(local * back_key + passed)

    gain, bias = vec(vectors, GAIN_ONE), vec(vectors, BIAS_ONE)
    hat, scale = normed(x_ref[...].astype(F32))
    norm = hat * gain + bias
    edge_hat, _ = normed(edge_ref[...].astype(F32))
    edge = (edge_hat * gain + bias)[edge_ref.shape[0] - 1 : edge_ref.shape[0]]
    places = tile * rows + rows_of((rows, 1))
    keep = (places != start_of(places, offsets)).astype(F32)
    before = shift_down(norm, edge, keep)
    late = norm - before
    back_norm, back_before = None, None
    for number, mix_row in enumerate((KEY_MIX, VALUE_MIX, GATE_MIX)):
        next(between, int)()
        mix = vec(vectors, mix_row)
        acts[number] = (norm * mix + before * (1.0 - mix)).astype(LOW)
        back_mixed = dot_nt(acts[3 + number], matrix(weights.at[number]))
        sums_out[8 * number : 8 * number + 8, :] += fold(back_mixed * late)
        one, two = back_mixed * mix, back_mixed * (1.0 - mix)
        back_norm = one if back_norm is None else back_norm + one
        back_before = two if back_before is None else back_before + two
    back_before = back_before * keep
    back_norm = back_norm + shift_up(back_before, carry[0:1, :])
    carry[0:1, :] = back_before[0:1]
    sums_out[40:48, :] += fold(back_norm * hat)
    sums_out[48:56, :] += fold(back_norm)
    stream_out[...] = (back_mid + norm_grad(back_norm, hat, scale, gain)).astype(LOW)


def back_kernel(*refs):
    step = pl.program_id(0)
    back_tile(pl.num_programs(0) - 1 - step, step == 0, *refs)


MESH = pl.DeviceIdType.MESH
GRID = (4, 2, 2, 2)
SMALL_ROWS = 16
HOPS = 13
LATE = 11


def place():
    wide, narrow = lax.axis_index("wide"), lax.axis_index("narrow")
    return wide // 2, wide % 2, narrow // 2, narrow % 2


def device(z, y, x, c):
    return (z * 2 + y, x * 2 + c)


def greet():
    z, y, x, c = place()
    others = [(z, y, x, 1 - c), (z, y, 1 - x, c), (z, 1 - y, x, c)]
    others += [(lax.rem(z + k, GRID[0]), y, x, c) for k in range(1, GRID[0])]
    barrier = pltpu.get_barrier_semaphore()
    for other in others:
        pl.semaphore_signal(barrier, inc=1, device_id=device(*other), device_id_type=MESH)
    pl.semaphore_wait(barrier, len(others))


class Gather:
    def __init__(self, own, held, send, receive):
        self.own, self.held, self.send, self.receive = own, held, send, receive
        self.z, self.y, self.x, self.c = place()

    def copy(self, number, source, target, to):
        return pltpu.make_async_remote_copy(
            src_ref=source,
            dst_ref=target,
            send_sem=self.send.at[number],
            recv_sem=self.receive.at[number],
            device_id=device(*to),
            device_id_type=MESH,
        )

    def along(self, k, mine):
        z = self.z if mine else lax.rem(self.z + GRID[0] - k, GRID[0])
        view = self.held.at[z, self.y, self.x, self.c]
        return self.copy(k - 1, self.own, view, (lax.rem(self.z + k, GRID[0]), self.y, self.x, self.c))

    def hop(self, number, mine):
        z, y, x, c = self.z, self.y, self.x, self.c
        if number < 3:
            return self.along(number + 1, mine)
        partner = (z + 1 - 2 * lax.rem(z, 2), y, x, c)
        everything = slice(None)
        one = lax.rem(z, 2)
        two = one + 2
        core = (z, y, x, 1 - c)
        sent = (
            ((everything, y, x, c), (z, y, 1 - x, c)),
            ((everything, y, x, c), (z, 1 - y, x, c)),
            ((one, y, 1 - x, c), (z, 1 - y, x, c)),
            ((two, 1 - y, x, c), (z, y, 1 - x, c)),
            ((everything, y, x, c), core),
            ((everything, y, 1 - x, c), core),
            ((everything, 1 - y, x, c), core),
            ((everything, 1 - y, 1 - x, c), core),
            ((one, 1 - y, 1 - x, c), partner),
            ((two, 1 - y, 1 - x, c), partner),
        )
        landing = (
            (everything, y, 1 - x, c),
            (everything, 1 - y, x, c),
            (one, 1 - y, 1 - x, c),
            (two, 1 - y, 1 - x, c),
            (everything, y, x, 1 - c),
            (everything, y, 1 - x, 1 - c),
            (everything, 1 - y, x, 1 - c),
            (everything, 1 - y, 1 - x, 1 - c),
            (1 - one, 1 - y, 1 - x, c),
            (3 - one, 1 - y, 1 - x, c),
        )
        source, to = sent[number - 3]
        view = self.held.at[source if mine else landing[number - 3]]
        return self.copy(number, view, view, to)

    def start(self, *numbers):
        for number in numbers:
            self.hop(number, True).start()

    def arrived(self, *numbers):
        for number in numbers:
            self.hop(number, False).wait_recv()

    def sent(self):
        for number in range(HOPS):
            self.hop(number, True).wait_send()


def gather_kernel(
    tiles, extents, wk, wv, wr, wo, wg, w1, w2, x_ref, *refs
):
    lines, refs = refs[: len(SMALL)], refs[len(SMALL) :]
    gather_steps(tiles, lines, extents, wk, wv, wr, wo, wg, w1, w2, x_ref, *refs)


def gather_steps(
    tiles, lines, extents, wk, wv, wr, wo, wg, w1, w2, x_ref,
    held, vectors, k_out, v_out, s_out, y_out, d_out, blend_out, mid_out, state_out, square_out,
    small, small_held, own, weights, grow, shrink, last, state, own_sem, load_sem, send, receive, small_send, small_receive,
):
    tick = pl.program_id(0)
    z, y, x, c = place()
    units = held.shape[0]
    width = x_ref.shape[1]
    first_tile = 8

    def unit(u):
        return Gather(own.at[u], held.at[u], send.at[lax.rem(u, 9)], receive.at[u])

    def small_unit():
        return Gather(small, small_held, small_send, small_receive)

    def keep(u):
        return pltpu.make_async_copy(own.at[u], held.at[u, z, y, x, c], own_sem.at[u])

    def load(u):
        return pltpu.make_async_copy(held.at[u], weights.at[u], load_sem.at[u])

    @pl.when(tick == 0)
    def _():
        small[...] = jnp.zeros_like(small)
        for row, line in enumerate(lines):
            small[row, : line.shape[0]] = line[...].astype(F32)
        for u, ref in enumerate((wk, wv, wr, wo, wg)):
            own[u] = ref[...]
        for j in range(4):
            own[5 + j] = w1[:, j * width : (j + 1) * width]
            own[9 + j] = w2[j]
        small_held[z, y, x, c] = small[...]
        for u in range(units):
            keep(u).start()
        greet()
        small_unit().start(0, 1, 2)
        unit(0).start(0, 1, 2)
        unit(1).start(0, 1, 2)

    @pl.when(tick < units)
    def _():
        keep(tick).wait()
        unit(tick).arrived(0, 1, 2)
        unit(tick).start(3, 4, 7)

    @pl.when(tick + 2 < units)
    def _():
        unit(tick + 2).start(0, 1, 2)

    @pl.when(tick == 0)
    def _():
        small_unit().arrived(0, 1, 2)
        small_unit().start(3, 4, 7)

    @pl.when(jnp.logical_and(tick >= 1, tick < units + 1))
    def _():
        unit(tick - 1).arrived(3, 4)
        unit(tick - 1).start(5, 6, 8, 9)

    @pl.when(tick == 1)
    def _():
        small_unit().arrived(3, 4)
        small_unit().start(5, 6, 8, 9)

    def diagonal(u):
        unit(u).arrived(5, 6)
        unit(u).start(11, 12)

    def partners(u):
        unit(u).arrived(11, 12)
        unit(u).start(10)

    def complete(u):
        unit(u).arrived(7, 8, 9, 10)
        unit(u).sent()

    def within(u, first, end):
        return jnp.logical_and(u >= first, u < end)

    pl.when(jnp.logical_or(within(tick - 2, 0, 4), within(tick - 2, LATE, units)))(lambda: diagonal(tick - 2))
    pl.when(within(tick - 3, 4, LATE))(lambda: diagonal(tick - 3))

    @pl.when(tick == 2)
    def _():
        small_unit().arrived(5, 6)
        small_unit().start(11, 12)

    pl.when(jnp.logical_or(within(tick - 3, 0, 4), within(tick - 3, LATE, units)))(lambda: partners(tick - 3))
    pl.when(within(tick - 5, 4, LATE))(lambda: partners(tick - 5))

    @pl.when(tick == 3)
    def _():
        small_unit().arrived(11, 12)
        small_unit().start(10)

    pl.when(jnp.logical_or(within(tick - 4, 0, 4), within(tick - 4, LATE, units)))(lambda: complete(tick - 4))
    pl.when(within(tick - 6, 4, LATE))(lambda: complete(tick - 6))

    @pl.when(jnp.logical_and(tick >= 4, tick < 8))
    def _():
        load(tick - 4).start()

    @pl.when(tick == first_tile)
    def _():
        for u in range(4):
            load(u).wait()

    @pl.when(tick == 4)
    def _():
        small_unit().arrived(7, 8, 9, 10)
        small_unit().sent()
        share = width // (GRID[0] * 8)
        total = jnp.zeros((SMALL_ROWS, width), F32)
        empty = jnp.zeros((SMALL_ROWS, width - 128), F32)
        for number in range(GRID[0] * 8):
            block = small_held[number // 8, number // 4 % 2, number // 2 % 2, number % 2]
            total += pltpu.roll(jnp.concatenate([block, empty], axis=1), number * share, 1)
        vectors[...] = total

    @pl.when(jnp.logical_and(tick >= first_tile, tick < first_tile + tiles))
    def _():
        front_tile(
            tick - first_tile, extents, vectors, x_ref, *[weights.at[u] for u in range(4)],
            k_out, v_out, s_out, y_out, d_out, blend_out, mid_out, state_out, square_out,
            grow, shrink, last, state,
        )


class Reduce:
    def __init__(self, out, mine, pairs, sides_x, sides_y, blocks_x, blocks_y, kept_sum, going, coming,
                 turned_in, send, receive, turned_receive):
        self.out = out
        self.mine, self.pairs, self.sides_x, self.sides_y = mine, pairs, sides_x, sides_y
        self.blocks_x, self.blocks_y, self.kept_sum, self.going, self.coming = blocks_x, blocks_y, kept_sum, going, coming
        self.send, self.receive, self.turned_in, self.turned_receive = send, receive, turned_in, turned_receive
        z, y, x, c = place()
        self.z, self.y, self.x, self.c = z, y, x, c
        self.core, self.over_x, self.over_y = (z, y, x, 1 - c), (z, y, 1 - x, c), (z, 1 - y, x, c)
        part = GRID[0] // 2
        self.low, self.high = pl.ds(0, part), pl.ds(part, part)

    def slot(self, u):
        return lax.rem(u, SLOTS)

    def remote(self, u, number, source, target, to, receive=None):
        return pltpu.make_async_remote_copy(
            src_ref=source,
            dst_ref=target,
            send_sem=self.send.at[self.slot(u), number],
            recv_sem=self.receive.at[u, number] if receive is None else receive,
            device_id=device(*to),
            device_id_type=MESH,
        )

    def pair(self, u):
        return self.remote(u, 0, self.mine.at[self.slot(u), 1 - self.c], self.pairs.at[self.slot(u)], self.core)

    def sides(self, u):
        held = self.mine.at[self.slot(u), self.c]
        y, x = 1 - self.y, 1 - self.x
        return (
            self.remote(u, 1, held.at[self.low, y, x], self.sides_x.at[u], self.over_x),
            self.remote(u, 2, held.at[self.high, y, x], self.sides_y.at[u], self.over_y),
        )

    def blocks(self, u):
        held = self.mine.at[self.slot(u), self.c]
        return (
            self.remote(u, 3, held.at[:, self.y, 1 - self.x], self.blocks_x.at[u], self.over_x),
            self.remote(u, 4, held.at[:, 1 - self.y, self.x], self.blocks_y.at[u], self.over_y),
        )

    def ends(self, u):
        found = []
        for k in range(1, GRID[0]):
            to = lax.rem(self.z + k, GRID[0])
            going = self.going.at[self.slot(u), to]
            found.append(self.remote(u, 4 + k, going, self.coming.at[u, k - 1], (to, self.y, self.x, self.c)))
        return found

    def turned_end(self, u, k):
        to = u - TURNED[0]
        return self.remote(
            u, 5, self.going.at[self.slot(u)], self.turned_in.at[k - 1], (to, self.y, self.x, self.c),
            self.turned_receive.at[k - 1],
        )

    def is_turned(self, u):
        return jnp.logical_and(u >= TURNED[0], u < TURNED[1])

    def pieces(self, u, left, right):
        slot, depth = self.slot(u), self.out.shape[-2]
        z, y, x, c = GRID
        turned = jnp.logical_and(u >= TURNED[0], u < TURNED[1]).astype(jnp.int32)

        def piece(part, columns):
            many = left.shape[-1] // PIECES[0]
            wide = right.shape[-1] // PIECES[1]
            lanes = slice(columns * wide, (columns + 1) * wide)
            grad = dot_tn(left[:, part * many : (part + 1) * many], right[:, lanes]).astype(LOW)
            blocks = grad.reshape(many // depth, depth, grad.shape[1])
            for number in range(many // depth):
                b = part * (many // depth) + number
                even = (b % c, b // (x * y * c), b // (x * c) % y, b // c % x)
                other = (b // z % c, b % z, b // (z * c * x), b // (z * c) % x)
                where = [i + turned * (j - i) for i, j in zip(even, other)]
                self.mine[slot, where[0], where[1], where[2], where[3], :, lanes] = blocks[number]

        return [functools.partial(piece, i, j) for i in range(PIECES[0]) for j in range(PIECES[1])]

    def stage(self, tick, lag, work):
        pl.when(jnp.logical_and(tick >= lag, tick < lag + UNITS))(functools.partial(work, tick - lag))

    def add_pair(self, u):
        slot, c = self.slot(u), self.c
        self.pair(u).wait()
        self.mine[slot, c] = (self.mine[slot, c].astype(F32) + self.pairs[slot].astype(F32)).astype(LOW)
        for copy in self.sides(u):
            copy.start()

    def add_sides(self, u):
        for copy in self.sides(u):
            copy.wait()
        held = self.mine.at[self.slot(u), self.c]
        low, high, y, x = self.low, self.high, self.y, self.x
        held[low, 1 - y, x] = (held[low, 1 - y, x].astype(F32) + self.sides_x[u].astype(F32)).astype(LOW)
        held[high, y, 1 - x] = (held[high, y, 1 - x].astype(F32) + self.sides_y[u].astype(F32)).astype(LOW)
        for copy in self.blocks(u):
            copy.start()

    def add_blocks(self, u):
        slot = self.slot(u)
        for copy in self.blocks(u):
            copy.wait()
        total = self.mine[slot, self.c, :, self.y, self.x].astype(F32)
        total = total + self.blocks_x[u].astype(F32) + self.blocks_y[u].astype(F32)
        self.kept_sum[slot] = total
        self.going[slot] = total.astype(LOW)

        def even():
            for copy in self.ends(u):
                copy.start()

        pl.when(jnp.logical_not(self.is_turned(u)))(even)
        for k in range(1, GRID[0]):
            away = lax.rem(self.z + 2 * GRID[0] - jnp.minimum(u, 2 * GRID[0]), GRID[0]) == k
            pl.when(jnp.logical_and(self.is_turned(u), away))(lambda k=k: self.turned_end(u, k).start())

    def add_ends(self, u):
        slot = self.slot(u)

        def even():
            for copy in self.ends(u):
                copy.wait()
            total = self.kept_sum[slot, self.z]
            for k in range(GRID[0] - 1):
                total += self.coming[u, k].astype(F32)
            self.out[u] = total

        def turned_here():
            total = self.kept_sum[slot]
            for k in range(1, GRID[0]):
                self.turned_end(u, k).wait_recv()
                total += self.turned_in[k - 1].astype(F32)
            self.out[TURNED[0] : TURNED[1]] = total

        pl.when(jnp.logical_not(self.is_turned(u)))(even)
        ahead = lax.rem(self.z + 2 * GRID[0] - jnp.minimum(u, 2 * GRID[0]), GRID[0])
        pl.when(jnp.logical_and(self.is_turned(u), ahead == 0))(turned_here)
        for k in range(1, GRID[0]):
            pl.when(jnp.logical_and(self.is_turned(u), ahead == k))(lambda k=k: self.turned_end(u, k).wait_send())


def reduce_kernel(
    extents, vectors, x_ref, edge_ref, k_ref, v_ref, s_ref, y_ref, d_ref, state_ref, mid_ref, packed,
    sums_two, square, acts, blend,
    stream_out, mixed, out, small_out,
    grow, shrink, carry, state, weights, weight_sem, staged, sums_one, lefts, rights, sums, small_in,
    stage_sem, left_sem, right_sem, small_send, small_receive, *refs,
):
    tick = pl.program_id(0)
    z, y, x, c = place()
    rows = x_ref.shape[0]
    tiles = mixed.shape[1] // rows
    job = Reduce(out, *refs)
    partners = (
        (z, y, x, 1 - c),
        (z, y, 1 - x, c),
        (z, 1 - y, x, c),
        (z + 1 - 2 * lax.rem(z, 2), y, x, c),
        (lax.rem(z + 2, GRID[0]), y, x, c),
    )

    def exchange(step):
        return pltpu.make_async_remote_copy(
            src_ref=sums.at[step],
            dst_ref=small_in.at[step],
            send_sem=small_send.at[step],
            recv_sem=small_receive.at[step],
            device_id=device(*partners[step]),
            device_id_type=MESH,
        )

    def left_of(u):
        return lax.rem(jnp.maximum(u - 3, 0), 2)

    def right_of(u):
        return lax.rem(jnp.minimum(u, 4) + jnp.maximum(u - 7, 0), 2)

    def fetch_left(u, late, last=False):
        if late:
            source = mixed.at[u - FIRST_UNITS]
        else:
            source = blend if last else acts.at[jnp.maximum(u - 3, 0)]
        return pltpu.make_async_copy(source, lefts.at[left_of(u)], left_sem.at[left_of(u)])

    def fetch_right(u, late):
        if late:
            source = mixed.at[u - FIRST_UNITS + 3]
        else:
            source = acts.at[6 + jnp.minimum(u, 4) + jnp.maximum(u - 7, 0)]
        return pltpu.make_async_copy(source, rights.at[right_of(u)], right_sem.at[right_of(u)])

    def fetches(u, work):
        early, late = u < FIRST_UNITS, jnp.logical_and(u >= FIRST_UNITS, u < UNITS)
        pl.when(jnp.logical_or(u == 0, jnp.logical_and(u >= 4, u < FIRST_UNITS - 1)))(lambda: work(fetch_left(u, False)))
        pl.when(u == FIRST_UNITS - 1)(lambda: work(fetch_left(u, False, True)))
        pl.when(jnp.logical_and(early, jnp.logical_or(u <= 4, u >= 8)))(lambda: work(fetch_right(u, False)))
        pl.when(late)(lambda: work(fetch_left(u, True)))
        pl.when(late)(lambda: work(fetch_right(u, True)))

    def keep(number):
        two = lax.rem(number, 2)
        where = pl.ds(pl.multiple_of((tiles - 1 - number) * rows, rows), rows)
        return pltpu.make_async_copy(staged.at[two], mixed.at[:, where], stage_sem.at[two])

    def start(copy):
        copy.start()

    def wait(copy):
        copy.wait()

    @pl.when(tick == 0)
    def _():
        fetches(tick, start)
        pltpu.make_async_copy(packed.at[0:4], weights, weight_sem).start()
        greet()

    @pl.when(tick == FIRST_TILE)
    def _():
        pltpu.make_async_copy(packed.at[0:4], weights, weight_sem).wait()

    number = tick - FIRST_TILE
    pl.when(jnp.logical_and(number >= 2, number < tiles + 1))(lambda: keep(number - 2).wait())
    pl.when(number == tiles)(lambda: keep(number - 1).wait())
    fetches(tick + 1, start)
    fetches(tick, wait)

    inputs = (extents, vectors, x_ref, edge_ref, k_ref, v_ref, s_ref, y_ref, d_ref, state_ref, mid_ref, weights)

    def pieces():
        return job.pieces(tick, lefts.at[left_of(tick)], rights.at[right_of(tick)])

    busy = jnp.logical_and(number >= 0, number < tiles)

    @pl.when(busy)
    def _():
        back_tile(
            tiles - 1 - number, number == 0, *inputs, stream_out, staged.at[lax.rem(number, 2)], sums_one,
            grow, shrink, carry, state, between=pieces(),
        )
        keep(number).start()
        job.pair(tick).start()

    @pl.when(jnp.logical_and(jnp.logical_not(busy), tick < UNITS))
    def _():
        for piece in pieces():
            piece()
        job.pair(tick).start()

    for lag, work in zip(LAGS, (job.add_pair, job.add_sides, job.add_blocks, job.add_ends)):
        job.stage(tick, lag, work)

    @pl.when(number == tiles - 1)
    def _():
        sums[0] = small_grads(vectors, sums_one, sums_two, square)
        exchange(0).start()

    for step in range(1, 6):

        @pl.when(number == tiles - 1 + step)
        def _():
            exchange(step - 1).wait()
            total = sums[step - 1] + small_in[step - 1]
            if step == 5:
                small_out[...] = total
            else:
                sums[step] = total
                exchange(step).start()


def whole(shape):
    return pl.BlockSpec(shape, lambda i: (0,) * len(shape), pipeline_mode=pl.Buffered(1))


def kept(shape):
    return pl.BlockSpec(shape, lambda i: (0,) * len(shape))


def smem():
    return pl.BlockSpec(memory_space=pltpu.SMEM)


ROWS = 256
UNITS = 13
SLOTS = 6
LAGS = (1, 2, 3, 6)
PIECES = (2, 1)
FIRST_UNITS = 10
FIRST_TILE = 1
TURNED = (4, 8)
FEED_ACTS = 13
GROUP = 4


def four(packed):
    return pl.BlockSpec((4, *packed.shape[1:]), lambda i: (0,) * len(packed.shape), pipeline_mode=pl.Buffered(1))


def front_shapes(tokens, width):
    wide = jax.ShapeDtypeStruct((tokens, width), F32)
    low = jax.ShapeDtypeStruct((tokens, width), LOW)
    states = jax.ShapeDtypeStruct((tokens // BLOCK, 8, width), F32)
    return [wide] * 5 + [low, wide, states, jax.ShapeDtypeStruct((8, width), F32)]


def front_specs(width, index):
    tile = pl.BlockSpec((ROWS, width), lambda i: (index(i), 0))
    states = pl.BlockSpec((ROWS // BLOCK, 8, width), lambda i: (index(i), 0, 0))
    return [tile] * 7 + [states, kept((8, width))]


def front_scratch(width):
    return [
        pltpu.VMEM((BLOCK, width), F32),
        pltpu.VMEM((BLOCK + EDGE, width), F32),
        pltpu.VMEM((8, width), F32),
        pltpu.VMEM((8, width), F32),
    ]


def front(extents, vectors, x, packed):
    tokens, width = x.shape
    return pl.pallas_call(
        front_kernel,
        name="front",
        grid=(tokens // ROWS,),
        in_specs=[smem(), whole(vectors.shape), pl.BlockSpec((ROWS, width), lambda i: (i, 0)), four(packed)],
        out_specs=front_specs(width, lambda i: i),
        out_shape=front_shapes(tokens, width),
        scratch_shapes=front_scratch(width),
        compiler_params=pltpu.CompilerParams(vmem_limit_bytes=56 * MIB),
    )(extents, vectors, x, packed)


def gather_front(extents, lines, shards, x):
    tokens, width = x.shape
    tiles = tokens // ROWS
    depth = shards[0].shape[0]
    anywhere = pl.BlockSpec(memory_space=pl.ANY)

    def index(i):
        return jnp.clip(i - 8, 0, tiles - 1)

    dma = pltpu.SemaphoreType.DMA
    return pl.pallas_call(
        functools.partial(gather_kernel, tiles),
        name="gather_front",
        grid=(max(UNITS + 4, LATE + 6, tiles + 8),),
        in_specs=[smem()]
        + [whole(part.shape) for part in shards]
        + [pl.BlockSpec((ROWS, width), lambda i: (index(i), 0))]
        + [whole(line.shape) for line in lines],
        out_specs=[anywhere, kept((SMALL_ROWS, width))] + front_specs(width, index),
        out_shape=[
            jax.ShapeDtypeStruct((UNITS, *GRID, depth, width), LOW),
            jax.ShapeDtypeStruct((SMALL_ROWS, width), F32),
        ]
        + front_shapes(tokens, width),
        scratch_shapes=[
            pltpu.VMEM((SMALL_ROWS, 128), F32),
            pltpu.VMEM((*GRID, SMALL_ROWS, 128), F32),
            pltpu.VMEM((UNITS, depth, width), LOW),
            pltpu.VMEM((4, *GRID, depth, width), LOW),
        ]
        + front_scratch(width)
        + [dma((UNITS,)), dma((4,)), dma((9, HOPS)), dma((UNITS, HOPS)), dma((HOPS,)), dma((HOPS,))],
        compiler_params=pltpu.CompilerParams(vmem_limit_bytes=56 * MIB, collective_id=0, has_side_effects=True),
    )(extents, *shards, x, *lines)


def feed(extents, vectors, mid, upstream, packed):
    tokens, width = mid.shape
    hidden = 4 * width
    rows, tiles = ROWS, tokens // ROWS
    tile = pl.BlockSpec((rows, width), lambda i: (tiles - 1 - i, 0))
    edge = pl.BlockSpec((EDGE, width), lambda i: (jnp.maximum((tiles - 1 - i) * (rows // EDGE) - 1, 0), 0))
    block = packed.shape[1:]
    return pl.pallas_call(
        feed_kernel,
        name="feed",
        grid=(tiles,),
        in_specs=[smem(), whole(vectors.shape), tile, edge, tile, pl.BlockSpec(memory_space=pl.ANY)],
        out_specs=[
            tile,
            tile,
            pl.BlockSpec((FEED_ACTS, rows, width), lambda i: (0, tiles - 1 - i, 0)),
            kept((48, width)),
        ],
        out_shape=[
            jax.ShapeDtypeStruct((tokens, width), LOW),
            jax.ShapeDtypeStruct((tokens, width), F32),
            jax.ShapeDtypeStruct((FEED_ACTS, tokens, width), LOW),
            jax.ShapeDtypeStruct((48, width), F32),
        ],
        scratch_shapes=[
            pltpu.VMEM((rows, hidden), LOW),
            pltpu.VMEM((8, width), F32),
            pltpu.VMEM(block, LOW),
            pltpu.VMEM((4, *block), LOW),
            pltpu.VMEM((*block[:4], 4, *block[4:]), LOW),
            pltpu.SemaphoreType.DMA((6,)),
        ],
        compiler_params=pltpu.CompilerParams(vmem_limit_bytes=60 * MIB),
    )(extents, vectors, mid, mid, upstream, packed)


def back_specs(tokens, width, packed, index):
    blocks = ROWS // BLOCK
    tile = pl.BlockSpec((ROWS, width), lambda i: (index(i), 0))
    edge = pl.BlockSpec((16, width), lambda i: (jnp.maximum(index(i) * (ROWS // 16) - 1, 0), 0))
    states = pl.BlockSpec((blocks, 8, width), lambda i: (index(i), 0, 0))
    inputs = [smem(), whole((SMALL_ROWS, width)), tile, edge] + [tile] * 5 + [states, tile, four(packed)]
    outputs = [tile, pl.BlockSpec((6, ROWS, width), lambda i: (0, index(i), 0)), kept((56, width))]
    shapes = [
        jax.ShapeDtypeStruct((tokens, width), LOW),
        jax.ShapeDtypeStruct((6, tokens, width), LOW),
        jax.ShapeDtypeStruct((56, width), F32),
    ]
    scratch = [
        pltpu.VMEM((BLOCK + EDGE, width), F32),
        pltpu.VMEM((BLOCK, width), F32),
        pltpu.VMEM((8, width), F32),
        pltpu.VMEM((8, width), F32),
    ]
    return inputs, outputs, shapes, scratch


def back(extents, vectors, x, saved, states, back_mid, packed):
    tokens, width = x.shape
    tiles = tokens // ROWS
    inputs, outputs, shapes, scratch = back_specs(tokens, width, packed, lambda i: tiles - 1 - i)
    return pl.pallas_call(
        back_kernel,
        name="back",
        grid=(tiles,),
        in_specs=inputs,
        out_specs=outputs,
        out_shape=shapes,
        scratch_shapes=scratch,
        compiler_params=pltpu.CompilerParams(vmem_limit_bytes=56 * MIB),
    )(extents, vectors, x, x, *saved, states, back_mid, packed)


def reduce(extents, vectors, x, saved, states, back_mid, packed, acts, blend, sums_two, square):
    tokens, width = x.shape
    tiles, depth = tokens // ROWS, packed.shape[-2]
    inputs, outputs, shapes, scratch = back_specs(
        tokens, width, packed, lambda i: tiles - 1 - jnp.clip(i - FIRST_TILE, 0, tiles - 1)
    )
    stream, mixed, sums_one = shapes
    anywhere = pl.BlockSpec(memory_space=pl.ANY)
    z, y, x_size, c = GRID
    dma = pltpu.SemaphoreType.DMA
    small = (SMALL_ROWS, width)
    return pl.pallas_call(
        reduce_kernel,
        name="reduce",
        grid=(UNITS + LAGS[3],),
        in_specs=inputs[:-1] + [anywhere, whole(sums_two.shape), whole(square.shape), anywhere, anywhere],
        out_specs=[outputs[0], anywhere, kept((UNITS, depth, width)), kept(small)],
        out_shape=[
            stream,
            mixed,
            jax.ShapeDtypeStruct((UNITS, depth, width), F32),
            jax.ShapeDtypeStruct(small, F32),
        ],
        scratch_shapes=scratch
        + [
            pltpu.VMEM((4, *packed.shape[1:]), LOW),
            dma,
            pltpu.VMEM((2, 6, ROWS, width), LOW),
            pltpu.VMEM(sums_one.shape, F32),
            pltpu.VMEM((2, tokens, width), LOW),
            pltpu.VMEM((2, tokens, width), LOW),
            pltpu.VMEM((5, *small), F32),
            pltpu.VMEM((5, *small), F32),
            dma((2,)),
            dma((2,)),
            dma((2,)),
            dma((5,)),
            dma((5,)),
            pltpu.VMEM((SLOTS, c, z, y, x_size, depth, width), LOW),
            pltpu.VMEM((SLOTS, z, y, x_size, depth, width), LOW),
            pltpu.VMEM((UNITS, z // 2, depth, width), LOW),
            pltpu.VMEM((UNITS, z // 2, depth, width), LOW),
            pltpu.VMEM((UNITS, z, depth, width), LOW),
            pltpu.VMEM((UNITS, z, depth, width), LOW),
            pltpu.VMEM((SLOTS, z, depth, width), F32),
            pltpu.VMEM((SLOTS, z, depth, width), LOW),
            pltpu.VMEM((UNITS, z - 1, depth, width), LOW),
            pltpu.VMEM((z - 1, z, depth, width), LOW),
            dma((SLOTS, 8)),
            dma((UNITS, 8)),
            dma((z - 1,)),
        ],
        compiler_params=pltpu.CompilerParams(vmem_limit_bytes=63 * MIB, collective_id=1, has_side_effects=True),
    )(extents, vectors, x, x, *saved, states, back_mid, packed, sums_two, square, acts, blend)


def finish_kernel(entries, share, stream_ref, total, small, stream_out, *outs):
    *squares, w1, w2, rms = outs[:8]
    lines = outs[8:]
    stream_out[...] = stream_ref[...]

    @pl.when(pl.program_id(0) == 0)
    def _():
        width = small.shape[1]
        for out, u in zip(squares, (10, 11, 12, 9, 8)):
            out[...] = total[u]
        for j in range(4):
            w1[:, j * width : (j + 1) * width] = total[j]
            w2[j] = total[4 + j]
        sums = small[...]
        rms[...] = jnp.sqrt(sums[len(SMALL), :3] / entries)
        mine = lax.axis_index("wide") * lax.axis_size("narrow") + lax.axis_index("narrow")
        turned = pltpu.roll(sums, lax.rem(width - mine * share, width), 1)
        for row, out in enumerate(lines):
            out[...] = turned[row, :share]


def finish_up(stream, total, small, entries):
    tokens, width = stream.shape
    depth = total.shape[1]
    parts = 2
    tile = pl.BlockSpec((tokens // parts, width), lambda i: (i, 0))
    shapes = [(depth, width)] * 5 + [(depth, 4 * width), (4, depth, width), (3,)] + [(depth,)] * len(SMALL)
    return pl.pallas_call(
        functools.partial(finish_kernel, entries, depth),
        name="finish_up",
        grid=(parts,),
        in_specs=[tile, whole(total.shape), whole(small.shape)],
        out_specs=[tile] + [kept(shape) for shape in shapes],
        out_shape=[jax.ShapeDtypeStruct(stream.shape, LOW)] + [jax.ShapeDtypeStruct(shape, F32) for shape in shapes],
        compiler_params=pltpu.CompilerParams(vmem_limit_bytes=60 * MIB),
    )(stream, total, small)


def small_grads(vectors, sums_one, sums_two, square):
    width = vectors.shape[1]
    one = [jnp.sum(sums_one[8 * i : 8 * i + 8, :], axis=0, keepdims=True) for i in range(7)]
    two = [jnp.sum(sums_two[8 * i : 8 * i + 8, :], axis=0, keepdims=True) for i in range(6)]
    decay = one[4] * jnp.exp(vec(vectors, FADING))
    lane = rows_of((1, width), 1)
    squares = jnp.zeros((1, width), F32)
    for place_of, total in enumerate((two[4], jnp.sum(square[...], axis=0, keepdims=True), two[5])):
        squares = jnp.where(lane == place_of, jnp.sum(total, axis=1, keepdims=True), squares)
    rows = [one[0], one[1], one[2], decay, one[3], two[0], two[1], one[5], one[6], two[2], two[3], squares]
    return jnp.concatenate(rows + [jnp.zeros((SMALL_ROWS - len(rows), width), F32)], axis=0)


def pack(weights):
    *square, w1, w2 = weights
    depth, width = square[0].shape[-2:]
    parts = list(square)
    parts += [w1[..., j * width : (j + 1) * width] for j in range(4)]
    parts += [w2[..., j * depth : (j + 1) * depth, :] for j in range(4)]
    return jnp.stack(parts)


SMALL = (0, 1, 2, 3, 4, 9, 10, 14, 15, 16, 17)
LARGE = (5, 6, 7, 8, 13, 11, 12)


def finish(outcome, stream, large, small, squares, entries):
    shards = [None] * 18
    for row, i in enumerate(SMALL):
        shards[i] = small[row]
    for grad, i in zip(large, LARGE):
        shards[i] = grad
    return (outcome, stream, *shards, jnp.sqrt(squares / entries))


def body_any(residual_input, extents, *rest):
    parameters, upstream = rest[:18], rest[18]
    devices = lax.axis_size(AXES)
    held = jnp.stack([parameters[i] for i in SMALL])
    width = held.shape[1] * devices
    vectors = lax.all_gather(held, AXES, axis=1, tiled=True).astype(F32)
    vectors = jnp.pad(vectors, ((0, SMALL_ROWS - len(SMALL)), (0, 0)))
    blocks = 1
    for size in GRID:
        blocks *= size
    weights = [lax.all_gather(parameters[i], AXES, axis=0, tiled=True) for i in LARGE]
    packed = pack([w.reshape(blocks, -1, w.shape[1]) for w in weights])
    packed = packed.reshape(UNITS, *GRID, *packed.shape[2:])
    *saved, blend, mid, states, square = front(extents, vectors, residual_input, packed)
    outcome, back_mid, acts, sums_two = feed(extents, vectors, mid, upstream, packed)
    stream, mixed, sums_one = back(extents, vectors, residual_input, saved, states, back_mid, packed)
    small = small_grads(vectors, sums_one, sums_two, square)
    grads = [dot_tn(mixed[i], mixed[3 + i]) for i in range(3)] + [dot_tn(blend, acts[12]), dot_tn(acts[5], acts[11])]
    grads.append(jnp.concatenate([dot_tn(acts[0], acts[6 + j]) for j in range(4)], axis=1))
    grads.append(jnp.concatenate([dot_tn(acts[1 + j], acts[10]) for j in range(4)], axis=0))
    squares = lax.psum(small[len(SMALL), :3], AXES)
    small = lax.psum_scatter(small[: len(SMALL)], AXES, scatter_dimension=1, tiled=True)
    large = [lax.psum_scatter(grad, AXES, scatter_dimension=0, tiled=True) for grad in grads]
    return finish(outcome, stream, large, small, squares, residual_input.shape[0] * width * devices)


def body(residual_input, extents, *rest):
    parameters, upstream = rest[:18], rest[18]
    devices = lax.axis_size(AXES)
    width = residual_input.shape[1]
    share = width // devices
    shards = [parameters[i] for i in LARGE]
    shards[6] = shards[6].reshape(4, share, width)
    packed, vectors, *saved, blend, mid, states, square = gather_front(
        extents, [parameters[i] for i in SMALL], shards, residual_input
    )
    outcome, back_mid, acts, sums_two = feed(extents, vectors, mid, upstream, packed)
    stream, _, total, small = reduce(
        extents, vectors, residual_input, saved, states, back_mid, packed, acts, blend, sums_two, square
    )
    stream, *rest = finish_up(stream, total, small, residual_input.shape[0] * width * devices)
    large, rms, lines = rest[:7], rest[7], rest[8:]
    large[6] = large[6].reshape(4 * share, width)
    shards = [None] * 18
    for line, i in zip(lines, SMALL):
        shards[i] = line
    for grad, i in zip(large, LARGE):
        shards[i] = grad
    return (outcome, stream, *shards, rms)


def solution(mesh):
    rows, vector = P(AXES, None), P(AXES)
    kinds = [vector] * 5 + [rows] * 4 + [vector] * 2 + [rows] * 3 + [vector] * 4
    sizes = (mesh.shape["wide"], mesh.shape["narrow"])
    return jax.shard_map(
        body if sizes == (GRID[0] * GRID[1], GRID[2] * GRID[3]) else body_any,
        mesh=mesh,
        in_specs=(rows, rows, *kinds, rows),
        out_specs=(rows, rows, *kinds, P()),
        check_vma=False,
    )
```

```python
import functools

import jax
import jax.numpy as jnp
from jax import lax
from jax.experimental import pallas as pl
from jax.experimental.pallas import tpu as pltpu
from jax.sharding import PartitionSpec as P

F32 = jnp.float32
LOW = jnp.bfloat16
AXES = ("wide", "narrow")
BLOCK = 128
EDGE = 8
MIB = 2**20

(KEY_MIX, VALUE_MIX, GATE_MIX, FADING, REWARD, FEED_MIX, GATING_MIX, GAIN_ONE, BIAS_ONE, GAIN_TWO, BIAS_TWO) = range(11)
VECTORS = 16


def dot(left, right):
    return jnp.dot(left, right, preferred_element_type=F32)


def dot_nt(left, right):
    return lax.dot_general(left, right, (((1,), (1,)), ((), ())), preferred_element_type=F32)


def dot_tn(left, right):
    return lax.dot_general(left, right, (((0,), (0,)), ((), ())), preferred_element_type=F32)


def offsets_of(extents):
    offsets, total = [], 0
    for j in range(extents.shape[1] - 1):
        total = total + extents[0, j]
        offsets.append(total)
    return offsets


def start_of(places, offsets):
    begun = jnp.zeros_like(places)
    for offset in offsets:
        begun = jnp.where(places >= offset, offset, begun)
    return begun


def normed(x):
    centered = x - jnp.mean(x, axis=1, keepdims=True)
    scale = lax.rsqrt(jnp.mean(centered * centered, axis=1, keepdims=True) + 1e-05)
    return centered * scale, scale


def fold(x):
    return jnp.sum(x.reshape(x.shape[0] // 8, 8, x.shape[1]), axis=0)


def rows_of(shape, axis=0):
    return lax.broadcasted_iota(jnp.int32, shape, axis)


def shift_down(x, first, keep):
    return jnp.where(rows_of((x.shape[0], 1)) == 0, first, pltpu.roll(x, 1, 0)) * keep


def shift_up(x, last):
    rows = x.shape[0]
    return jnp.where(rows_of((rows, 1)) == rows - 1, last, pltpu.roll(x, rows - 1, 0))


def split(top, bottom):
    both = jnp.concatenate([top, bottom], axis=1)
    high = both.astype(LOW)
    low = (both - high.astype(F32)).astype(LOW)
    return jnp.concatenate([high, low], axis=0)


def norm_grad(back_normed, hat, scale, gain):
    back_hat = back_normed * gain
    return scale * (
        back_hat
        - jnp.mean(back_hat, axis=1, keepdims=True)
        - hat * jnp.mean(back_hat * hat, axis=1, keepdims=True)
    )


def vec(vectors, row):
    return vectors[row : row + 1, :]


def matrix(ref):
    return ref[...].reshape(-1, ref.shape[-1])


def front_tile(
    tile, extents, vectors, x_ref, wk, wv, wr, wo,
    k_out, v_out, s_out, y_out, d_out, blend_out, mid_out, state_out, square_out,
    grow, shrink, last, state,
):
    rows, width = x_ref.shape
    half = BLOCK // 2
    offsets = offsets_of(extents)
    rate = jnp.exp(vec(vectors, FADING))

    @pl.when(tile == 0)
    def _():
        local = rows_of((BLOCK + EDGE, 1)).astype(F32)
        shrink[...] = jnp.exp((half - local) * rate)
        grow[...] = jnp.exp((local[:BLOCK] + (1 - half)) * rate)
        last[...] = jnp.zeros_like(last)
        state[...] = jnp.zeros_like(state)
        square_out[...] = jnp.zeros_like(square_out)

    x = x_ref[...].astype(F32)
    hat, _ = normed(x)
    norm = hat * vec(vectors, GAIN_ONE) + vec(vectors, BIAS_ONE)
    places = tile * rows + rows_of((rows, 1))
    keep = (places != start_of(places, offsets)).astype(F32)
    before = shift_down(norm, last[0:1, :], keep)
    last[0:1, :] = norm[rows - 1 : rows, :]

    def mixed(row):
        mix = vec(vectors, row)
        return (norm * mix + before * (1.0 - mix)).astype(LOW)

    keys = dot(mixed(KEY_MIX), matrix(wk))
    values = dot(mixed(VALUE_MIX), matrix(wv))
    sig = jax.nn.sigmoid(dot(mixed(GATE_MIX), matrix(wr)))
    k_out[...] = keys
    v_out[...] = values
    s_out[...] = sig
    fade_half = jnp.exp(-half * rate)
    reward = vec(vectors, REWARD)
    for block in range(rows // BLOCK):
        here = slice(block * BLOCK, (block + 1) * BLOCK)
        key, value = keys[here], values[here]
        weight = grow[...] * jnp.exp(key)
        first = tile * rows + block * BLOCK
        after = first + rows_of((BLOCK + EDGE, 1))
        column = rows_of((1, 2 * BLOCK), 1)
        source = first + jnp.where(column >= BLOCK, column - BLOCK, column)
        begun = start_of(after, offsets)
        paired = ((source < after) & (source >= begun)).astype(LOW)
        sums = dot(paired, split(weight * value, weight))
        inherit = (begun < first).astype(F32)
        top = shrink[...] * (sums[:, :width] + inherit * (fade_half * state[0:1, :]))
        bottom = shrink[...] * (sums[:, width:] + inherit * (fade_half * state[1:2, :]))
        state[0:1, :] = top[BLOCK : BLOCK + 1]
        state[1:2, :] = bottom[BLOCK : BLOCK + 1]
        state_out[block, :, :] = state[...]
        own = jnp.exp(reward + key)
        inverse = 1.0 / (bottom[:BLOCK] + own)
        wkv = (top[:BLOCK] + own * value) * inverse
        y_out[here, :] = wkv
        d_out[here, :] = inverse
        blend_out[here, :] = (sig[here] * wkv).astype(LOW)
    attended = dot(blend_out[...], matrix(wo))
    mid_out[...] = x + attended
    square_out[...] += fold(attended * attended)


def front_kernel(extents, vectors, x_ref, weights, *rest):
    front_tile(pl.program_id(0), extents, vectors, x_ref, *[weights.at[u] for u in range(4)], *rest)


def feed_kernel(
    extents, vectors, mid_ref, edge_ref, up_ref, packed,
    out_out, back_out, acts, sums_out,
    lift, carry, wg, w1, w2, load,
):
    step = pl.program_id(0)
    tile = pl.num_programs(0) - 1 - step
    rows, width = mid_ref.shape
    hidden = lift.shape[1]
    offsets = offsets_of(extents)

    @pl.when(step == 0)
    def _():
        copies = [(packed.at[4], wg), (packed.at[5:9], w1)]
        copies += [(packed.at[9 + j], w2.at[:, :, :, :, j]) for j in range(4)]
        copies = [pltpu.make_async_copy(a, b, load.at[i]) for i, (a, b) in enumerate(copies)]
        for copy in copies:
            copy.start()
        for copy in copies:
            copy.wait()
        carry[...] = jnp.zeros_like(carry)
        sums_out[...] = jnp.zeros_like(sums_out)

    gain, bias = vec(vectors, GAIN_TWO), vec(vectors, BIAS_TWO)
    mid = mid_ref[...]
    hat, scale = normed(mid)
    norm = hat * gain + bias
    edge_hat, _ = normed(edge_ref[...])
    edge = (edge_hat * gain + bias)[EDGE - 1 : EDGE]
    places = tile * rows + rows_of((rows, 1))
    keep = (places != start_of(places, offsets)).astype(F32)
    before = shift_down(norm, edge, keep)
    mix_k, mix_g = vec(vectors, FEED_MIX), vec(vectors, GATING_MIX)
    feed_key = (norm * mix_k + before * (1.0 - mix_k)).astype(LOW)
    feed_gate = (norm * mix_g + before * (1.0 - mix_g)).astype(LOW)
    acts[0] = feed_key
    acts[5] = feed_gate
    lowered = None
    group = []
    for j in range(hidden // width):
        chunk = slice(j * width, (j + 1) * width)
        lifted = jnp.maximum(dot(feed_key, matrix(w1.at[j])), 0.0)
        lift[:, chunk] = lifted.astype(LOW)
        squared = (lifted * lifted).astype(LOW)
        acts[1 + j] = squared
        group.append(squared)
        if len(group) == GROUP:
            part = dot(jnp.concatenate(group, axis=1), matrix(w2.at[j + 1 - GROUP : j + 1]))
            lowered = part if lowered is None else lowered + part
            group = []
    sig = jax.nn.sigmoid(dot(feed_gate, matrix(wg)))
    feed_out = sig * lowered
    result = mid + feed_out
    out_out[...] = result.astype(LOW)
    upstream = up_ref[...].astype(F32)
    back_lowered = (upstream * sig).astype(LOW)
    back_gate = (upstream * lowered * sig * (1.0 - sig)).astype(LOW)
    acts[10] = back_lowered
    acts[11] = back_gate
    group = []
    for j in range(hidden // width):
        chunk = slice(j * width, (j + 1) * width)
        back_lifted = (2.0 * lift[:, chunk].astype(F32) * dot_nt(back_lowered, matrix(w2.at[j]))).astype(LOW)
        acts[6 + j] = back_lifted
        group.append(back_lifted)
    back_key = dot_nt(
        jnp.concatenate(group, axis=1),
        jnp.concatenate([matrix(w1.at[j]) for j in range(hidden // width)], axis=1),
    )
    back_gating = dot_nt(back_gate, matrix(wg))
    late = norm - before
    back_before = keep * (back_key * (1.0 - mix_k) + back_gating * (1.0 - mix_g))
    back_norm = back_key * mix_k + back_gating * mix_g + shift_up(back_before, carry[0:1, :])
    carry[0:1, :] = back_before[0:1]
    back_mid = upstream + norm_grad(back_norm, hat, scale, gain)
    back_out[...] = back_mid
    acts[12] = back_mid.astype(LOW)
    for row, piece in enumerate(
        (back_key * late, back_gating * late, back_norm * hat, back_norm, result * result, feed_out * feed_out)
    ):
        sums_out[8 * row : 8 * row + 8, :] += fold(piece)


def back_tile(
    tile, begins, extents, vectors, x_ref, edge_ref, k_ref, v_ref, s_ref, y_ref, d_ref, state_ref, mid_ref, weights,
    stream_out, acts, sums_out,
    grow, shrink, carry, state, between=(),
):
    rows, width = x_ref.shape
    half = BLOCK // 2
    offsets = offsets_of(extents)
    rate = jnp.exp(vec(vectors, FADING))

    @pl.when(begins)
    def _():
        local = rows_of((BLOCK + EDGE, 1)).astype(F32)
        shrink[...] = jnp.exp((half - local[:BLOCK]) * rate)
        grow[...] = jnp.exp((local + (1 - EDGE - half)) * rate)
        carry[...] = jnp.zeros_like(carry)
        state[...] = jnp.zeros_like(state)
        sums_out[...] = jnp.zeros_like(sums_out)

    between = iter(between)
    back_mid = mid_ref[...]
    back_attended = back_mid.astype(LOW)
    back_blend = dot_nt(back_attended, matrix(weights.at[3]))
    sig = s_ref[...]
    wkv = y_ref[...]
    acts[5] = (back_blend * wkv * sig * (1.0 - sig)).astype(LOW)
    back_top = back_blend * sig * d_ref[...]
    fade_half = jnp.exp(-half * rate)
    reward = vec(vectors, REWARD)
    for block in reversed(range(rows // BLOCK)):
        next(between, int)()
        here = slice(block * BLOCK, (block + 1) * BLOCK)
        key, value = k_ref[here, :], v_ref[here, :]
        first = tile * rows + block * BLOCK
        source = first - EDGE + rows_of((BLOCK + EDGE, 1))
        column = rows_of((1, 2 * BLOCK), 1)
        after = first + jnp.where(column >= BLOCK, column - BLOCK, column)
        paired = ((source < after) & (source >= start_of(after, offsets))).astype(LOW)
        bt = back_top[here]
        weighted = shrink[...] * bt
        sums = dot(paired, split(weighted, -weighted * wkv[here]))
        following = start_of(first + BLOCK + jnp.zeros((1, 1), jnp.int32), offsets)
        tail = (source >= following).astype(F32)
        top = grow[...] * (sums[:, :width] + tail * (fade_half * state[0:1, :]))
        bottom = grow[...] * (sums[:, width:] + tail * (fade_half * state[1:2, :]))
        next(between, int)()
        crossing = state_ref[block, :, :] * state[...]
        sums_out[32:40, :] += jnp.where(rows_of((8, 1)) < 2, crossing * (-1.0 * BLOCK), 0.0)
        state[0:1, :] = top[EDGE - 1 : EDGE]
        state[1:2, :] = bottom[EDGE - 1 : EDGE]
        weight = jnp.exp(key)
        own = jnp.exp(reward + key) * bt
        passed = weight * (value * top[EDGE:] + bottom[EDGE:])
        bonus = own * (value - wkv[here])
        back_key = passed + bonus
        acts[3, here, :] = back_key.astype(LOW)
        acts[4, here, :] = (weight * top[EDGE:] + own).astype(LOW)
        local = rows_of((BLOCK, 1)).astype(F32)
        sums_out[24:32, :] += fold(bonus)
        sums_out[32:40, :] += fold(local * back_key + passed)

    gain, bias = vec(vectors, GAIN_ONE), vec(vectors, BIAS_ONE)
    hat, scale = normed(x_ref[...].astype(F32))
    norm = hat * gain + bias
    edge_hat, _ = normed(edge_ref[...].astype(F32))
    edge = (edge_hat * gain + bias)[edge_ref.shape[0] - 1 : edge_ref.shape[0]]
    places = tile * rows + rows_of((rows, 1))
    keep = (places != start_of(places, offsets)).astype(F32)
    before = shift_down(norm, edge, keep)
    late = norm - before
    back_norm, back_before = None, None
    for number, mix_row in enumerate((KEY_MIX, VALUE_MIX, GATE_MIX)):
        next(between, int)()
        mix = vec(vectors, mix_row)
        acts[number] = (norm * mix + before * (1.0 - mix)).astype(LOW)
        back_mixed = dot_nt(acts[3 + number], matrix(weights.at[number]))
        sums_out[8 * number : 8 * number + 8, :] += fold(back_mixed * late)
        one, two = back_mixed * mix, back_mixed * (1.0 - mix)
        back_norm = one if back_norm is None else back_norm + one
        back_before = two if back_before is None else back_before + two
    back_before = back_before * keep
    back_norm = back_norm + shift_up(back_before, carry[0:1, :])
    carry[0:1, :] = back_before[0:1]
    sums_out[40:48, :] += fold(back_norm * hat)
    sums_out[48:56, :] += fold(back_norm)
    stream_out[...] = (back_mid + norm_grad(back_norm, hat, scale, gain)).astype(LOW)


def back_kernel(*refs):
    step = pl.program_id(0)
    back_tile(pl.num_programs(0) - 1 - step, step == 0, *refs)


MESH = pl.DeviceIdType.MESH
GRID = (4, 2, 2, 2)
SMALL_ROWS = 16
HOPS = 13
LATE = 11


def place():
    wide, narrow = lax.axis_index("wide"), lax.axis_index("narrow")
    return wide // 2, wide % 2, narrow // 2, narrow % 2


def device(z, y, x, c):
    return (z * 2 + y, x * 2 + c)


def greet():
    z, y, x, c = place()
    others = [(z, y, x, 1 - c), (z, y, 1 - x, c), (z, 1 - y, x, c)]
    others += [(lax.rem(z + k, GRID[0]), y, x, c) for k in range(1, GRID[0])]
    barrier = pltpu.get_barrier_semaphore()
    for other in others:
        pl.semaphore_signal(barrier, inc=1, device_id=device(*other), device_id_type=MESH)
    pl.semaphore_wait(barrier, len(others))


class Gather:
    def __init__(self, own, held, send, receive):
        self.own, self.held, self.send, self.receive = own, held, send, receive
        self.z, self.y, self.x, self.c = place()

    def copy(self, number, source, target, to):
        return pltpu.make_async_remote_copy(
            src_ref=source,
            dst_ref=target,
            send_sem=self.send.at[number],
            recv_sem=self.receive.at[number],
            device_id=device(*to),
            device_id_type=MESH,
        )

    def along(self, k, mine):
        z = self.z if mine else lax.rem(self.z + GRID[0] - k, GRID[0])
        view = self.held.at[z, self.y, self.x, self.c]
        return self.copy(k - 1, self.own, view, (lax.rem(self.z + k, GRID[0]), self.y, self.x, self.c))

    def hop(self, number, mine):
        z, y, x, c = self.z, self.y, self.x, self.c
        if number < 3:
            return self.along(number + 1, mine)
        partner = (z + 1 - 2 * lax.rem(z, 2), y, x, c)
        everything = slice(None)
        one = lax.rem(z, 2)
        two = one + 2
        core = (z, y, x, 1 - c)
        sent = (
            ((everything, y, x, c), (z, y, 1 - x, c)),
            ((everything, y, x, c), (z, 1 - y, x, c)),
            ((one, y, 1 - x, c), (z, 1 - y, x, c)),
            ((two, 1 - y, x, c), (z, y, 1 - x, c)),
            ((everything, y, x, c), core),
            ((everything, y, 1 - x, c), core),
            ((everything, 1 - y, x, c), core),
            ((everything, 1 - y, 1 - x, c), core),
            ((one, 1 - y, 1 - x, c), partner),
            ((two, 1 - y, 1 - x, c), partner),
        )
        landing = (
            (everything, y, 1 - x, c),
            (everything, 1 - y, x, c),
            (one, 1 - y, 1 - x, c),
            (two, 1 - y, 1 - x, c),
            (everything, y, x, 1 - c),
            (everything, y, 1 - x, 1 - c),
            (everything, 1 - y, x, 1 - c),
            (everything, 1 - y, 1 - x, 1 - c),
            (1 - one, 1 - y, 1 - x, c),
            (3 - one, 1 - y, 1 - x, c),
        )
        source, to = sent[number - 3]
        view = self.held.at[source if mine else landing[number - 3]]
        return self.copy(number, view, view, to)

    def start(self, *numbers):
        for number in numbers:
            self.hop(number, True).start()

    def arrived(self, *numbers):
        for number in numbers:
            self.hop(number, False).wait_recv()

    def sent(self):
        for number in range(HOPS):
            self.hop(number, True).wait_send()


def gather_kernel(
    tiles, extents, wk, wv, wr, wo, wg, w1, w2, x_ref, *refs
):
    lines, refs = refs[: len(SMALL)], refs[len(SMALL) :]
    gather_steps(tiles, lines, extents, wk, wv, wr, wo, wg, w1, w2, x_ref, *refs)


def gather_steps(
    tiles, lines, extents, wk, wv, wr, wo, wg, w1, w2, x_ref,
    held, vectors, k_out, v_out, s_out, y_out, d_out, blend_out, mid_out, state_out, square_out,
    small, small_held, own, weights, grow, shrink, last, state, own_sem, load_sem, send, receive, small_send, small_receive,
):
    tick = pl.program_id(0)
    z, y, x, c = place()
    units = held.shape[0]
    width = x_ref.shape[1]
    first_tile = 8

    def unit(u):
        return Gather(own.at[u], held.at[u], send.at[lax.rem(u, 9)], receive.at[u])

    def small_unit():
        return Gather(small, small_held, small_send, small_receive)

    def keep(u):
        return pltpu.make_async_copy(own.at[u], held.at[u, z, y, x, c], own_sem.at[u])

    def load(u):
        return pltpu.make_async_copy(held.at[u], weights.at[u], load_sem.at[u])

    @pl.when(tick == 0)
    def _():
        small[...] = jnp.zeros_like(small)
        for row, line in enumerate(lines):
            small[row, : line.shape[0]] = line[...].astype(F32)
        for u, ref in enumerate((wk, wv, wr, wo, wg)):
            own[u] = ref[...]
        for j in range(4):
            own[5 + j] = w1[:, j * width : (j + 1) * width]
            own[9 + j] = w2[j]
        small_held[z, y, x, c] = small[...]
        for u in range(units):
            keep(u).start()
        greet()
        small_unit().start(0, 1, 2)
        unit(0).start(0, 1, 2)
        unit(1).start(0, 1, 2)

    @pl.when(tick < units)
    def _():
        keep(tick).wait()
        unit(tick).arrived(0, 1, 2)
        unit(tick).start(3, 4, 7)

    @pl.when(tick + 2 < units)
    def _():
        unit(tick + 2).start(0, 1, 2)

    @pl.when(tick == 0)
    def _():
        small_unit().arrived(0, 1, 2)
        small_unit().start(3, 4, 7)

    @pl.when(jnp.logical_and(tick >= 1, tick < units + 1))
    def _():
        unit(tick - 1).arrived(3, 4)
        unit(tick - 1).start(5, 6, 8, 9)

    @pl.when(tick == 1)
    def _():
        small_unit().arrived(3, 4)
        small_unit().start(5, 6, 8, 9)

    def diagonal(u):
        unit(u).arrived(5, 6)
        unit(u).start(11, 12)

    def partners(u):
        unit(u).arrived(11, 12)
        unit(u).start(10)

    def complete(u):
        unit(u).arrived(7, 8, 9, 10)
        unit(u).sent()

    def within(u, first, end):
        return jnp.logical_and(u >= first, u < end)

    pl.when(jnp.logical_or(within(tick - 2, 0, 4), within(tick - 2, LATE, units)))(lambda: diagonal(tick - 2))
    pl.when(within(tick - 3, 4, LATE))(lambda: diagonal(tick - 3))

    @pl.when(tick == 2)
    def _():
        small_unit().arrived(5, 6)
        small_unit().start(11, 12)

    pl.when(jnp.logical_or(within(tick - 3, 0, 4), within(tick - 3, LATE, units)))(lambda: partners(tick - 3))
    pl.when(within(tick - 5, 4, LATE))(lambda: partners(tick - 5))

    @pl.when(tick == 3)
    def _():
        small_unit().arrived(11, 12)
        small_unit().start(10)

    pl.when(jnp.logical_or(within(tick - 4, 0, 4), within(tick - 4, LATE, units)))(lambda: complete(tick - 4))
    pl.when(within(tick - 6, 4, LATE))(lambda: complete(tick - 6))

    @pl.when(jnp.logical_and(tick >= 4, tick < 8))
    def _():
        load(tick - 4).start()

    @pl.when(tick == first_tile)
    def _():
        for u in range(4):
            load(u).wait()

    @pl.when(tick == 4)
    def _():
        small_unit().arrived(7, 8, 9, 10)
        small_unit().sent()
        share = width // (GRID[0] * 8)
        total = jnp.zeros((SMALL_ROWS, width), F32)
        empty = jnp.zeros((SMALL_ROWS, width - 128), F32)
        for number in range(GRID[0] * 8):
            block = small_held[number // 8, number // 4 % 2, number // 2 % 2, number % 2]
            total += pltpu.roll(jnp.concatenate([block, empty], axis=1), number * share, 1)
        vectors[...] = total

    @pl.when(jnp.logical_and(tick >= first_tile, tick < first_tile + tiles))
    def _():
        front_tile(
            tick - first_tile, extents, vectors, x_ref, *[weights.at[u] for u in range(4)],
            k_out, v_out, s_out, y_out, d_out, blend_out, mid_out, state_out, square_out,
            grow, shrink, last, state,
        )


class Reduce:
    def __init__(self, out, mine, pairs, sides_x, sides_y, blocks_x, blocks_y, kept_sum, going, coming,
                 turned_in, send, receive, turned_receive):
        self.out = out
        self.mine, self.pairs, self.sides_x, self.sides_y = mine, pairs, sides_x, sides_y
        self.blocks_x, self.blocks_y, self.kept_sum, self.going, self.coming = blocks_x, blocks_y, kept_sum, going, coming
        self.send, self.receive, self.turned_in, self.turned_receive = send, receive, turned_in, turned_receive
        z, y, x, c = place()
        self.z, self.y, self.x, self.c = z, y, x, c
        self.core, self.over_x, self.over_y = (z, y, x, 1 - c), (z, y, 1 - x, c), (z, 1 - y, x, c)
        part = GRID[0] // 2
        self.low, self.high = pl.ds(0, part), pl.ds(part, part)

    def slot(self, u):
        return lax.rem(u, SLOTS)

    def remote(self, u, number, source, target, to, receive=None):
        return pltpu.make_async_remote_copy(
            src_ref=source,
            dst_ref=target,
            send_sem=self.send.at[self.slot(u), number],
            recv_sem=self.receive.at[u, number] if receive is None else receive,
            device_id=device(*to),
            device_id_type=MESH,
        )

    def pair(self, u):
        return self.remote(u, 0, self.mine.at[self.slot(u), 1 - self.c], self.pairs.at[self.slot(u)], self.core)

    def sides(self, u):
        held = self.mine.at[self.slot(u), self.c]
        y, x = 1 - self.y, 1 - self.x
        return (
            self.remote(u, 1, held.at[self.low, y, x], self.sides_x.at[u], self.over_x),
            self.remote(u, 2, held.at[self.high, y, x], self.sides_y.at[u], self.over_y),
        )

    def blocks(self, u):
        held = self.mine.at[self.slot(u), self.c]
        return (
            self.remote(u, 3, held.at[:, self.y, 1 - self.x], self.blocks_x.at[u], self.over_x),
            self.remote(u, 4, held.at[:, 1 - self.y, self.x], self.blocks_y.at[u], self.over_y),
        )

    def ends(self, u):
        found = []
        for k in range(1, GRID[0]):
            to = lax.rem(self.z + k, GRID[0])
            going = self.going.at[self.slot(u), to]
            found.append(self.remote(u, 4 + k, going, self.coming.at[u, k - 1], (to, self.y, self.x, self.c)))
        return found

    def turned_end(self, u, k):
        to = u - TURNED[0]
        return self.remote(
            u, 5, self.going.at[self.slot(u)], self.turned_in.at[k - 1], (to, self.y, self.x, self.c),
            self.turned_receive.at[k - 1],
        )

    def is_turned(self, u):
        return jnp.logical_and(u >= TURNED[0], u < TURNED[1])

    def pieces(self, u, left, right):
        slot, depth = self.slot(u), self.out.shape[-2]
        z, y, x, c = GRID
        turned = jnp.logical_and(u >= TURNED[0], u < TURNED[1]).astype(jnp.int32)

        def piece(part, columns):
            many = left.shape[-1] // PIECES[0]
            wide = right.shape[-1] // PIECES[1]
            lanes = slice(columns * wide, (columns + 1) * wide)
            grad = dot_tn(left[:, part * many : (part + 1) * many], right[:, lanes]).astype(LOW)
            blocks = grad.reshape(many // depth, depth, grad.shape[1])
            for number in range(many // depth):
                b = part * (many // depth) + number
                even = (b % c, b // (x * y * c), b // (x * c) % y, b // c % x)
                other = (b // z % c, b % z, b // (z * c * x), b // (z * c) % x)
                where = [i + turned * (j - i) for i, j in zip(even, other)]
                self.mine[slot, where[0], where[1], where[2], where[3], :, lanes] = blocks[number]

        return [functools.partial(piece, i, j) for i in range(PIECES[0]) for j in range(PIECES[1])]

    def stage(self, tick, lag, work):
        pl.when(jnp.logical_and(tick >= lag, tick < lag + UNITS))(functools.partial(work, tick - lag))

    def add_pair(self, u):
        slot, c = self.slot(u), self.c
        self.pair(u).wait()
        self.mine[slot, c] = (self.mine[slot, c].astype(F32) + self.pairs[slot].astype(F32)).astype(LOW)
        for copy in self.sides(u):
            copy.start()

    def add_sides(self, u):
        for copy in self.sides(u):
            copy.wait()
        held = self.mine.at[self.slot(u), self.c]
        low, high, y, x = self.low, self.high, self.y, self.x
        held[low, 1 - y, x] = (held[low, 1 - y, x].astype(F32) + self.sides_x[u].astype(F32)).astype(LOW)
        held[high, y, 1 - x] = (held[high, y, 1 - x].astype(F32) + self.sides_y[u].astype(F32)).astype(LOW)
        for copy in self.blocks(u):
            copy.start()

    def add_blocks(self, u):
        slot = self.slot(u)
        for copy in self.blocks(u):
            copy.wait()
        total = self.mine[slot, self.c, :, self.y, self.x].astype(F32)
        total = total + self.blocks_x[u].astype(F32) + self.blocks_y[u].astype(F32)
        self.kept_sum[slot] = total
        self.going[slot] = total.astype(LOW)

        def even():
            for copy in self.ends(u):
                copy.start()

        pl.when(jnp.logical_not(self.is_turned(u)))(even)
        for k in range(1, GRID[0]):
            away = lax.rem(self.z + 2 * GRID[0] - jnp.minimum(u, 2 * GRID[0]), GRID[0]) == k
            pl.when(jnp.logical_and(self.is_turned(u), away))(lambda k=k: self.turned_end(u, k).start())

    def add_ends(self, u):
        slot = self.slot(u)

        def even():
            for copy in self.ends(u):
                copy.wait()
            total = self.kept_sum[slot, self.z]
            for k in range(GRID[0] - 1):
                total += self.coming[u, k].astype(F32)
            self.out[u] = total

        def turned_here():
            total = self.kept_sum[slot]
            for k in range(1, GRID[0]):
                self.turned_end(u, k).wait_recv()
                total += self.turned_in[k - 1].astype(F32)
            self.out[TURNED[0] : TURNED[1]] = total

        pl.when(jnp.logical_not(self.is_turned(u)))(even)
        ahead = lax.rem(self.z + 2 * GRID[0] - jnp.minimum(u, 2 * GRID[0]), GRID[0])
        pl.when(jnp.logical_and(self.is_turned(u), ahead == 0))(turned_here)
        for k in range(1, GRID[0]):
            pl.when(jnp.logical_and(self.is_turned(u), ahead == k))(lambda k=k: self.turned_end(u, k).wait_send())


def reduce_kernel(
    extents, vectors, x_ref, edge_ref, k_ref, v_ref, s_ref, y_ref, d_ref, state_ref, mid_ref, packed,
    sums_two, square, acts, blend,
    stream_out, mixed, out, small_out,
    grow, shrink, carry, state, weights, weight_sem, staged, sums_one, lefts, rights, sums, small_in,
    stage_sem, left_sem, right_sem, small_send, small_receive, *refs,
):
    tick = pl.program_id(0)
    z, y, x, c = place()
    rows = x_ref.shape[0]
    tiles = mixed.shape[1] // rows
    job = Reduce(out, *refs)
    partners = (
        (z, y, x, 1 - c),
        (z, y, 1 - x, c),
        (z, 1 - y, x, c),
        (z + 1 - 2 * lax.rem(z, 2), y, x, c),
        (lax.rem(z + 2, GRID[0]), y, x, c),
    )

    def exchange(step):
        return pltpu.make_async_remote_copy(
            src_ref=sums.at[step],
            dst_ref=small_in.at[step],
            send_sem=small_send.at[step],
            recv_sem=small_receive.at[step],
            device_id=device(*partners[step]),
            device_id_type=MESH,
        )

    def left_of(u):
        return lax.rem(jnp.maximum(u - 3, 0), 2)

    def right_of(u):
        return lax.rem(jnp.minimum(u, 4) + jnp.maximum(u - 7, 0), 2)

    def fetch_left(u, late, last=False):
        if late:
            source = mixed.at[u - FIRST_UNITS]
        else:
            source = blend if last else acts.at[jnp.maximum(u - 3, 0)]
        return pltpu.make_async_copy(source, lefts.at[left_of(u)], left_sem.at[left_of(u)])

    def fetch_right(u, late):
        if late:
            source = mixed.at[u - FIRST_UNITS + 3]
        else:
            source = acts.at[6 + jnp.minimum(u, 4) + jnp.maximum(u - 7, 0)]
        return pltpu.make_async_copy(source, rights.at[right_of(u)], right_sem.at[right_of(u)])

    def fetches(u, work):
        early, late = u < FIRST_UNITS, jnp.logical_and(u >= FIRST_UNITS, u < UNITS)
        pl.when(jnp.logical_or(u == 0, jnp.logical_and(u >= 4, u < FIRST_UNITS - 1)))(lambda: work(fetch_left(u, False)))
        pl.when(u == FIRST_UNITS - 1)(lambda: work(fetch_left(u, False, True)))
        pl.when(jnp.logical_and(early, jnp.logical_or(u <= 4, u >= 8)))(lambda: work(fetch_right(u, False)))
        pl.when(late)(lambda: work(fetch_left(u, True)))
        pl.when(late)(lambda: work(fetch_right(u, True)))

    def keep(number):
        two = lax.rem(number, 2)
        where = pl.ds(pl.multiple_of((tiles - 1 - number) * rows, rows), rows)
        return pltpu.make_async_copy(staged.at[two], mixed.at[:, where], stage_sem.at[two])

    def start(copy):
        copy.start()

    def wait(copy):
        copy.wait()

    @pl.when(tick == 0)
    def _():
        fetches(tick, start)
        pltpu.make_async_copy(packed.at[0:4], weights, weight_sem).start()
        greet()

    @pl.when(tick == FIRST_TILE)
    def _():
        pltpu.make_async_copy(packed.at[0:4], weights, weight_sem).wait()

    number = tick - FIRST_TILE
    pl.when(jnp.logical_and(number >= 2, number < tiles + 1))(lambda: keep(number - 2).wait())
    pl.when(number == tiles)(lambda: keep(number - 1).wait())
    fetches(tick + 1, start)
    fetches(tick, wait)

    inputs = (extents, vectors, x_ref, edge_ref, k_ref, v_ref, s_ref, y_ref, d_ref, state_ref, mid_ref, weights)

    def pieces():
        return job.pieces(tick, lefts.at[left_of(tick)], rights.at[right_of(tick)])

    busy = jnp.logical_and(number >= 0, number < tiles)

    @pl.when(busy)
    def _():
        back_tile(
            tiles - 1 - number, number == 0, *inputs, stream_out, staged.at[lax.rem(number, 2)], sums_one,
            grow, shrink, carry, state, between=pieces(),
        )
        keep(number).start()
        job.pair(tick).start()

    @pl.when(jnp.logical_and(jnp.logical_not(busy), tick < UNITS))
    def _():
        for piece in pieces():
            piece()
        job.pair(tick).start()

    for lag, work in zip(LAGS, (job.add_pair, job.add_sides, job.add_blocks, job.add_ends)):
        job.stage(tick, lag, work)

    @pl.when(number == tiles - 1)
    def _():
        sums[0] = small_grads(vectors, sums_one, sums_two, square)
        exchange(0).start()

    for step in range(1, 6):

        @pl.when(number == tiles - 1 + step)
        def _():
            exchange(step - 1).wait()
            total = sums[step - 1] + small_in[step - 1]
            if step == 5:
                small_out[...] = total
            else:
                sums[step] = total
                exchange(step).start()


def whole(shape):
    return pl.BlockSpec(shape, lambda i: (0,) * len(shape), pipeline_mode=pl.Buffered(1))


def kept(shape):
    return pl.BlockSpec(shape, lambda i: (0,) * len(shape))


def smem():
    return pl.BlockSpec(memory_space=pltpu.SMEM)


ROWS = 256
UNITS = 13
SLOTS = 6
LAGS = (1, 2, 3, 6)
PIECES = (2, 1)
FIRST_UNITS = 10
FIRST_TILE = 1
TURNED = (4, 8)
FEED_ACTS = 13
GROUP = 4


def four(packed):
    return pl.BlockSpec((4, *packed.shape[1:]), lambda i: (0,) * len(packed.shape), pipeline_mode=pl.Buffered(1))


def front_shapes(tokens, width):
    wide = jax.ShapeDtypeStruct((tokens, width), F32)
    low = jax.ShapeDtypeStruct((tokens, width), LOW)
    states = jax.ShapeDtypeStruct((tokens // BLOCK, 8, width), F32)
    return [wide] * 5 + [low, wide, states, jax.ShapeDtypeStruct((8, width), F32)]


def front_specs(width, index):
    tile = pl.BlockSpec((ROWS, width), lambda i: (index(i), 0))
    states = pl.BlockSpec((ROWS // BLOCK, 8, width), lambda i: (index(i), 0, 0))
    return [tile] * 7 + [states, kept((8, width))]


def front_scratch(width):
    return [
        pltpu.VMEM((BLOCK, width), F32),
        pltpu.VMEM((BLOCK + EDGE, width), F32),
        pltpu.VMEM((8, width), F32),
        pltpu.VMEM((8, width), F32),
    ]


def front(extents, vectors, x, packed):
    tokens, width = x.shape
    return pl.pallas_call(
        front_kernel,
        name="front",
        grid=(tokens // ROWS,),
        in_specs=[smem(), whole(vectors.shape), pl.BlockSpec((ROWS, width), lambda i: (i, 0)), four(packed)],
        out_specs=front_specs(width, lambda i: i),
        out_shape=front_shapes(tokens, width),
        scratch_shapes=front_scratch(width),
        compiler_params=pltpu.CompilerParams(vmem_limit_bytes=56 * MIB),
    )(extents, vectors, x, packed)


def gather_front(extents, lines, shards, x):
    tokens, width = x.shape
    tiles = tokens // ROWS
    depth = shards[0].shape[0]
    anywhere = pl.BlockSpec(memory_space=pl.ANY)

    def index(i):
        return jnp.clip(i - 8, 0, tiles - 1)

    dma = pltpu.SemaphoreType.DMA
    return pl.pallas_call(
        functools.partial(gather_kernel, tiles),
        name="gather_front",
        grid=(max(UNITS + 4, LATE + 6, tiles + 8),),
        in_specs=[smem()]
        + [whole(part.shape) for part in shards]
        + [pl.BlockSpec((ROWS, width), lambda i: (index(i), 0))]
        + [whole(line.shape) for line in lines],
        out_specs=[anywhere, kept((SMALL_ROWS, width))] + front_specs(width, index),
        out_shape=[
            jax.ShapeDtypeStruct((UNITS, *GRID, depth, width), LOW),
            jax.ShapeDtypeStruct((SMALL_ROWS, width), F32),
        ]
        + front_shapes(tokens, width),
        scratch_shapes=[
            pltpu.VMEM((SMALL_ROWS, 128), F32),
            pltpu.VMEM((*GRID, SMALL_ROWS, 128), F32),
            pltpu.VMEM((UNITS, depth, width), LOW),
            pltpu.VMEM((4, *GRID, depth, width), LOW),
        ]
        + front_scratch(width)
        + [dma((UNITS,)), dma((4,)), dma((9, HOPS)), dma((UNITS, HOPS)), dma((HOPS,)), dma((HOPS,))],
        compiler_params=pltpu.CompilerParams(vmem_limit_bytes=56 * MIB, collective_id=0, has_side_effects=True),
    )(extents, *shards, x, *lines)


def feed(extents, vectors, mid, upstream, packed):
    tokens, width = mid.shape
    hidden = 4 * width
    rows, tiles = ROWS, tokens // ROWS
    tile = pl.BlockSpec((rows, width), lambda i: (tiles - 1 - i, 0))
    edge = pl.BlockSpec((EDGE, width), lambda i: (jnp.maximum((tiles - 1 - i) * (rows // EDGE) - 1, 0), 0))
    block = packed.shape[1:]
    return pl.pallas_call(
        feed_kernel,
        name="feed",
        grid=(tiles,),
        in_specs=[smem(), whole(vectors.shape), tile, edge, tile, pl.BlockSpec(memory_space=pl.ANY)],
        out_specs=[
            tile,
            tile,
            pl.BlockSpec((FEED_ACTS, rows, width), lambda i: (0, tiles - 1 - i, 0)),
            kept((48, width)),
        ],
        out_shape=[
            jax.ShapeDtypeStruct((tokens, width), LOW),
            jax.ShapeDtypeStruct((tokens, width), F32),
            jax.ShapeDtypeStruct((FEED_ACTS, tokens, width), LOW),
            jax.ShapeDtypeStruct((48, width), F32),
        ],
        scratch_shapes=[
            pltpu.VMEM((rows, hidden), LOW),
            pltpu.VMEM((8, width), F32),
            pltpu.VMEM(block, LOW),
            pltpu.VMEM((4, *block), LOW),
            pltpu.VMEM((*block[:4], 4, *block[4:]), LOW),
            pltpu.SemaphoreType.DMA((6,)),
        ],
        compiler_params=pltpu.CompilerParams(vmem_limit_bytes=60 * MIB),
    )(extents, vectors, mid, mid, upstream, packed)


def back_specs(tokens, width, packed, index):
    blocks = ROWS // BLOCK
    tile = pl.BlockSpec((ROWS, width), lambda i: (index(i), 0))
    edge = pl.BlockSpec((16, width), lambda i: (jnp.maximum(index(i) * (ROWS // 16) - 1, 0), 0))
    states = pl.BlockSpec((blocks, 8, width), lambda i: (index(i), 0, 0))
    inputs = [smem(), whole((SMALL_ROWS, width)), tile, edge] + [tile] * 5 + [states, tile, four(packed)]
    outputs = [tile, pl.BlockSpec((6, ROWS, width), lambda i: (0, index(i), 0)), kept((56, width))]
    shapes = [
        jax.ShapeDtypeStruct((tokens, width), LOW),
        jax.ShapeDtypeStruct((6, tokens, width), LOW),
        jax.ShapeDtypeStruct((56, width), F32),
    ]
    scratch = [
        pltpu.VMEM((BLOCK + EDGE, width), F32),
        pltpu.VMEM((BLOCK, width), F32),
        pltpu.VMEM((8, width), F32),
        pltpu.VMEM((8, width), F32),
    ]
    return inputs, outputs, shapes, scratch


def back(extents, vectors, x, saved, states, back_mid, packed):
    tokens, width = x.shape
    tiles = tokens // ROWS
    inputs, outputs, shapes, scratch = back_specs(tokens, width, packed, lambda i: tiles - 1 - i)
    return pl.pallas_call(
        back_kernel,
        name="back",
        grid=(tiles,),
        in_specs=inputs,
        out_specs=outputs,
        out_shape=shapes,
        scratch_shapes=scratch,
        compiler_params=pltpu.CompilerParams(vmem_limit_bytes=56 * MIB),
    )(extents, vectors, x, x, *saved, states, back_mid, packed)


def reduce(extents, vectors, x, saved, states, back_mid, packed, acts, blend, sums_two, square):
    tokens, width = x.shape
    tiles, depth = tokens // ROWS, packed.shape[-2]
    inputs, outputs, shapes, scratch = back_specs(
        tokens, width, packed, lambda i: tiles - 1 - jnp.clip(i - FIRST_TILE, 0, tiles - 1)
    )
    stream, mixed, sums_one = shapes
    anywhere = pl.BlockSpec(memory_space=pl.ANY)
    z, y, x_size, c = GRID
    dma = pltpu.SemaphoreType.DMA
    small = (SMALL_ROWS, width)
    return pl.pallas_call(
        reduce_kernel,
        name="reduce",
        grid=(UNITS + LAGS[3],),
        in_specs=inputs[:-1] + [anywhere, whole(sums_two.shape), whole(square.shape), anywhere, anywhere],
        out_specs=[outputs[0], anywhere, kept((UNITS, depth, width)), kept(small)],
        out_shape=[
            stream,
            mixed,
            jax.ShapeDtypeStruct((UNITS, depth, width), F32),
            jax.ShapeDtypeStruct(small, F32),
        ],
        scratch_shapes=scratch
        + [
            pltpu.VMEM((4, *packed.shape[1:]), LOW),
            dma,
            pltpu.VMEM((2, 6, ROWS, width), LOW),
            pltpu.VMEM(sums_one.shape, F32),
            pltpu.VMEM((2, tokens, width), LOW),
            pltpu.VMEM((2, tokens, width), LOW),
            pltpu.VMEM((5, *small), F32),
            pltpu.VMEM((5, *small), F32),
            dma((2,)),
            dma((2,)),
            dma((2,)),
            dma((5,)),
            dma((5,)),
            pltpu.VMEM((SLOTS, c, z, y, x_size, depth, width), LOW),
            pltpu.VMEM((SLOTS, z, y, x_size, depth, width), LOW),
            pltpu.VMEM((UNITS, z // 2, depth, width), LOW),
            pltpu.VMEM((UNITS, z // 2, depth, width), LOW),
            pltpu.VMEM((UNITS, z, depth, width), LOW),
            pltpu.VMEM((UNITS, z, depth, width), LOW),
            pltpu.VMEM((SLOTS, z, depth, width), F32),
            pltpu.VMEM((SLOTS, z, depth, width), LOW),
            pltpu.VMEM((UNITS, z - 1, depth, width), LOW),
            pltpu.VMEM((z - 1, z, depth, width), LOW),
            dma((SLOTS, 8)),
            dma((UNITS, 8)),
            dma((z - 1,)),
        ],
        compiler_params=pltpu.CompilerParams(vmem_limit_bytes=63 * MIB, collective_id=1, has_side_effects=True),
    )(extents, vectors, x, x, *saved, states, back_mid, packed, sums_two, square, acts, blend)


def finish_kernel(entries, share, stream_ref, total, small, stream_out, *outs):
    *squares, w1, w2, rms = outs[:8]
    lines = outs[8:]
    stream_out[...] = stream_ref[...]

    @pl.when(pl.program_id(0) == 0)
    def _():
        width = small.shape[1]
        for out, u in zip(squares, (10, 11, 12, 9, 8)):
            out[...] = total[u]
        for j in range(4):
            w1[:, j * width : (j + 1) * width] = total[j]
            w2[j] = total[4 + j]
        sums = small[...]
        rms[...] = jnp.sqrt(sums[len(SMALL), :3] / entries)
        mine = lax.axis_index("wide") * lax.axis_size("narrow") + lax.axis_index("narrow")
        turned = pltpu.roll(sums, lax.rem(width - mine * share, width), 1)
        for row, out in enumerate(lines):
            out[...] = turned[row, :share]


def finish_up(stream, total, small, entries):
    tokens, width = stream.shape
    depth = total.shape[1]
    parts = 1
    tile = pl.BlockSpec((tokens // parts, width), lambda i: (i, 0))
    shapes = [(depth, width)] * 5 + [(depth, 4 * width), (4, depth, width), (3,)] + [(depth,)] * len(SMALL)
    return pl.pallas_call(
        functools.partial(finish_kernel, entries, depth),
        name="finish_up",
        grid=(parts,),
        in_specs=[tile, whole(total.shape), whole(small.shape)],
        out_specs=[tile] + [kept(shape) for shape in shapes],
        out_shape=[jax.ShapeDtypeStruct(stream.shape, LOW)] + [jax.ShapeDtypeStruct(shape, F32) for shape in shapes],
        compiler_params=pltpu.CompilerParams(vmem_limit_bytes=60 * MIB),
    )(stream, total, small)


def small_grads(vectors, sums_one, sums_two, square):
    width = vectors.shape[1]
    one = [jnp.sum(sums_one[8 * i : 8 * i + 8, :], axis=0, keepdims=True) for i in range(7)]
    two = [jnp.sum(sums_two[8 * i : 8 * i + 8, :], axis=0, keepdims=True) for i in range(6)]
    decay = one[4] * jnp.exp(vec(vectors, FADING))
    lane = rows_of((1, width), 1)
    squares = jnp.zeros((1, width), F32)
    for place_of, total in enumerate((two[4], jnp.sum(square[...], axis=0, keepdims=True), two[5])):
        squares = jnp.where(lane == place_of, jnp.sum(total, axis=1, keepdims=True), squares)
    rows = [one[0], one[1], one[2], decay, one[3], two[0], two[1], one[5], one[6], two[2], two[3], squares]
    return jnp.concatenate(rows + [jnp.zeros((SMALL_ROWS - len(rows), width), F32)], axis=0)


def pack(weights):
    *square, w1, w2 = weights
    depth, width = square[0].shape[-2:]
    parts = list(square)
    parts += [w1[..., j * width : (j + 1) * width] for j in range(4)]
    parts += [w2[..., j * depth : (j + 1) * depth, :] for j in range(4)]
    return jnp.stack(parts)


SMALL = (0, 1, 2, 3, 4, 9, 10, 14, 15, 16, 17)
LARGE = (5, 6, 7, 8, 13, 11, 12)


def finish(outcome, stream, large, small, squares, entries):
    shards = [None] * 18
    for row, i in enumerate(SMALL):
        shards[i] = small[row]
    for grad, i in zip(large, LARGE):
        shards[i] = grad
    return (outcome, stream, *shards, jnp.sqrt(squares / entries))


def body_any(residual_input, extents, *rest):
    parameters, upstream = rest[:18], rest[18]
    devices = lax.axis_size(AXES)
    held = jnp.stack([parameters[i] for i in SMALL])
    width = held.shape[1] * devices
    vectors = lax.all_gather(held, AXES, axis=1, tiled=True).astype(F32)
    vectors = jnp.pad(vectors, ((0, SMALL_ROWS - len(SMALL)), (0, 0)))
    blocks = 1
    for size in GRID:
        blocks *= size
    weights = [lax.all_gather(parameters[i], AXES, axis=0, tiled=True) for i in LARGE]
    packed = pack([w.reshape(blocks, -1, w.shape[1]) for w in weights])
    packed = packed.reshape(UNITS, *GRID, *packed.shape[2:])
    *saved, blend, mid, states, square = front(extents, vectors, residual_input, packed)
    outcome, back_mid, acts, sums_two = feed(extents, vectors, mid, upstream, packed)
    stream, mixed, sums_one = back(extents, vectors, residual_input, saved, states, back_mid, packed)
    small = small_grads(vectors, sums_one, sums_two, square)
    grads = [dot_tn(mixed[i], mixed[3 + i]) for i in range(3)] + [dot_tn(blend, acts[12]), dot_tn(acts[5], acts[11])]
    grads.append(jnp.concatenate([dot_tn(acts[0], acts[6 + j]) for j in range(4)], axis=1))
    grads.append(jnp.concatenate([dot_tn(acts[1 + j], acts[10]) for j in range(4)], axis=0))
    squares = lax.psum(small[len(SMALL), :3], AXES)
    small = lax.psum_scatter(small[: len(SMALL)], AXES, scatter_dimension=1, tiled=True)
    large = [lax.psum_scatter(grad, AXES, scatter_dimension=0, tiled=True) for grad in grads]
    return finish(outcome, stream, large, small, squares, residual_input.shape[0] * width * devices)


def body(residual_input, extents, *rest):
    parameters, upstream = rest[:18], rest[18]
    devices = lax.axis_size(AXES)
    width = residual_input.shape[1]
    share = width // devices
    shards = [parameters[i] for i in LARGE]
    shards[6] = shards[6].reshape(4, share, width)
    packed, vectors, *saved, blend, mid, states, square = gather_front(
        extents, [parameters[i] for i in SMALL], shards, residual_input
    )
    outcome, back_mid, acts, sums_two = feed(extents, vectors, mid, upstream, packed)
    stream, _, total, small = reduce(
        extents, vectors, residual_input, saved, states, back_mid, packed, acts, blend, sums_two, square
    )
    stream, *rest = finish_up(stream, total, small, residual_input.shape[0] * width * devices)
    large, rms, lines = rest[:7], rest[7], rest[8:]
    large[6] = large[6].reshape(4 * share, width)
    shards = [None] * 18
    for line, i in zip(lines, SMALL):
        shards[i] = line
    for grad, i in zip(large, LARGE):
        shards[i] = grad
    return (outcome, stream, *shards, rms)


def solution(mesh):
    rows, vector = P(AXES, None), P(AXES)
    kinds = [vector] * 5 + [rows] * 4 + [vector] * 2 + [rows] * 3 + [vector] * 4
    sizes = (mesh.shape["wide"], mesh.shape["narrow"])
    return jax.shard_map(
        body if sizes == (GRID[0] * GRID[1], GRID[2] * GRID[3]) else body_any,
        mesh=mesh,
        in_specs=(rows, rows, *kinds, rows),
        out_specs=(rows, rows, *kinds, P()),
        check_vma=False,
    )
```
